32 devices in a mesh: wide: 8 (over y, x, core), narrow: 4 (over z).
Axes of the slice: x: 2, y: 2, z: 4, core: 2. Of those that a mesh axis runs over, the one named last changes fastest.
Arguments:
- tile_flow_speed: float32 [512, 3, 4096], P(('wide', 'narrow')), may hold values from -3 to 3
- tile_stress_mean: float32 [512, 4096], P(('wide', 'narrow')), may hold values from -3 to 3
- tile_heat_state: float32 [512, 4096], P(('wide', 'narrow')), may hold values from 0 to 1
- tile_drag_coefficient: float32 [512, 4096], P(('wide', 'narrow')), may hold values from 0.5 to 2
- marker_attributes: float32 [8, 262144], P(None, ('wide', 'narrow')), may hold values from -6 to 6
- marker_holding_tile: int32 [262144], P(('wide', 'narrow')), may hold values from 0 to 511, as said below
- marker_voxel_number: int32 [262144], P(('wide', 'narrow')), may hold values from 0 to 4095
- prior_slot_of_tile: int32 [512], P(('wide', 'narrow')), may hold values from 0 to 511, as said below
Outputs:
- velocity: float32 [3, 128, 128, 128], P(None, 'wide', 'narrow')
- pressure: float32 [128, 128, 128], P('wide', 'narrow')
- heat_on_fresh_grid: float32 [128, 128, 128], P('wide', 'narrow')
- bin_mean_attributes: float32 [8, 32, 32, 32], P(None, 'wide', 'narrow')
The draws below stay inside these ranges and needn't reach their ends.
Inputs may be any that keep to these rules, and one draw needn't show every extreme that they name: prior_slot_of_tile is a permutation: new owner q // 16 holds at place q % 16 the block that old owner prior_slot_of_tile[q] // 16 held at place prior_slot_of_tile[q] % 16. Every old owner sends to every new owner either none or exactly 1 of its blocks. `marker_holding_tile`: the tracer at position t is stored on old owner t // 8192 and lies in one of that owner's blocks. The tracers of one old owner whose blocks go to one new owner number at most 640, and every old owner has exactly 640 for one of its new owners.
All inputs are finite; a program needn't handle non-finite values.
Results may differ from the reference program's by a relative error of at most 0.00013.
Values sent between devices are 32-bit elements; how exact they have to be, the bound alone decides.
A program may use at most 256 MiB of HBM per device.

```python
import math
import jax
import jax.numpy as jnp

BS = 16
LX = 1
LY = 2
LZ = 8
TR_DEV = 8192
NPROP = 8
SWEEPS = 3
BLOCKS_DEV = 16
SUBGRID_COUNT = 512
SUBGRID_SITES = 4096
CAP = 1
GROUPS = 16
TCAP = 640
NT = 262144
NX = 128
NY = 128
NZ = 128
NXB = 32
NYB = 32
NZB = 32
N_WIDE = 8
N_NARROW = 4
DEVICES = 32


def draw_prior_slot_of_tile(key, part):
    base = jax.random.fold_in(key, 101)
    key_spread, key_shuffle, key_offset, key_places = jax.random.split(base, 4)
    spread = jax.random.permutation(key_spread, DEVICES)
    shuffle = jax.random.permutation(key_shuffle, DEVICES)
    offsets = jax.random.permutation(key_offset, DEVICES)
    device_ids = jnp.arange(DEVICES, dtype=jnp.int32)
    block_ids = jnp.arange(BLOCKS_DEV, dtype=jnp.int32)
    group_offset = offsets[block_ids // CAP]
    spread_inv = jnp.zeros((DEVICES,), jnp.int32).at[spread].set(device_ids)
    shuffle_inv = jnp.zeros((DEVICES,), jnp.int32).at[shuffle].set(device_ids)
    source = shuffle_inv[(spread_inv[device_ids][:, None] - group_offset[None, :]) % DEVICES]
    places = jax.vmap(lambda one_key: jax.random.permutation(one_key, BLOCKS_DEV))(jax.random.split(key_places, DEVICES))
    target = device_ids[:, None] * BLOCKS_DEV + places
    old_index = source * BLOCKS_DEV + block_ids[None, :]
    result = jnp.zeros((DEVICES * BLOCKS_DEV,), jnp.int32).at[target.reshape(-1)].set(old_index.reshape(-1))
    return result.astype(jnp.int32)


def draw_marker_holding_tile(key, part):
    base = jax.random.fold_in(key, 202)

    def one_source(source_key, source):
        key_full, key_caps, key_score, key_order, key_block = jax.random.split(source_key, 5)
        full_group = jax.random.randint(key_full, (), 0, GROUPS)
        group_ids = jnp.arange(GROUPS, dtype=jnp.int32)
        group_caps = jax.random.randint(key_caps, (GROUPS,), 4 * TCAP // 5, TCAP + 1)
        group_caps = jnp.where(group_ids == full_group, TCAP, group_caps)
        slot_total = GROUPS * TCAP
        slot_ids = jnp.arange(slot_total, dtype=jnp.int32)
        slot_group = slot_ids // TCAP
        slot_place = slot_ids % TCAP
        raw_score = jax.random.permutation(key_score, slot_total)
        score = jnp.where(slot_group == full_group, raw_score - slot_total, jnp.where(slot_place < group_caps[slot_group], raw_score, raw_score + slot_total))
        chosen = jnp.argsort(score, stable=True)[:TR_DEV]
        groups = (chosen // TCAP)[jax.random.permutation(key_order, TR_DEV)]
        local_block = groups * CAP + jax.random.randint(key_block, (TR_DEV,), 0, CAP)
        return source * BLOCKS_DEV + local_block
    keys = jax.random.split(base, DEVICES)
    result = jax.vmap(one_source)(keys, jnp.arange(DEVICES, dtype=jnp.int32))
    return result.reshape(-1).astype(jnp.int32)


def place_ends(array, own_key, smallest, high):
    dims = array.shape
    spot = [jax.random.randint(jax.random.fold_in(own_key, axis), (), 0, dims[axis]) for axis in range(len(dims))]
    array = array.at[tuple(spot)].set(smallest)
    longest = dims.index(max(dims))
    spot[longest] = (spot[longest] + 1) % dims[longest]
    return array.at[tuple(spot)].set(high)


def block_levels(key, extent, shards, smallest, high):
    level, own = 1.0, jax.random.fold_in(key, 6)
    for position, blocks in shards:
        heights = jnp.exp(jax.random.uniform(jax.random.fold_in(own, position), (blocks,), jnp.float32, smallest / len(shards), high / len(shards)))
        level = level * jnp.repeat(heights, extent[position] // blocks).reshape([-1 if axis == position else 1 for axis in range(len(extent))])
    return level


def gaussian(stream_key, dims, scale, limit, pieces=(), kind=jnp.bfloat16):
    values = scale * jax.random.normal(stream_key, dims, jnp.float32)
    if pieces:
        values = values * block_levels(stream_key, dims, pieces, -0.22, 0.18)
    return jnp.clip(values, -limit, limit).astype(kind)


def setup_inputs(seed: int = 0) -> dict:
    streams_of = jax.random.split(jax.random.key(seed), 9)
    return {
        "tile_flow_speed": gaussian(streams_of[0], (SUBGRID_COUNT, 3, SUBGRID_SITES), 0.5, 3.0, ((0, 32),), jnp.float32),
        "tile_stress_mean": gaussian(streams_of[1], (SUBGRID_COUNT, SUBGRID_SITES), 0.5, 3.0, ((0, 32),), jnp.float32),
        "tile_heat_state": jnp.clip(1.0 * jax.random.uniform(streams_of[2], (SUBGRID_COUNT, SUBGRID_SITES), jnp.float32) ** block_levels(streams_of[2], (SUBGRID_COUNT, SUBGRID_SITES), ((0, 32),), -0.2, 0.2), 0.0, 1.0),
        "tile_drag_coefficient": jnp.clip(jnp.exp(math.log(2.0) - 1.3862944 * jax.random.uniform(streams_of[3], (SUBGRID_COUNT, SUBGRID_SITES), jnp.float32) ** block_levels(streams_of[3], (SUBGRID_COUNT, SUBGRID_SITES), ((0, 32),), -0.2, 0.2)), 0.5, 2.0),
        "marker_attributes": gaussian(streams_of[4], (NPROP, NT), 1.0, 6.0, ((1, 32),), jnp.float32),
        "marker_holding_tile": draw_marker_holding_tile(jax.random.fold_in(streams_of[8], 71), 0),
        "marker_voxel_number": place_ends(jax.random.randint(streams_of[6], (NT,), 0, SUBGRID_SITES), jax.random.fold_in(streams_of[6], 1), 0, SUBGRID_SITES - 1).astype(jnp.int32),
        "prior_slot_of_tile": draw_prior_slot_of_tile(jax.random.fold_in(streams_of[8], 71), 0),
    }


MIX_WEIGHTS = (0.3, -0.25, 0.2, -0.15, 0.35, -0.3, 0.25, -0.2)
RELAX_WEIGHT = 0.7
PRESSURE_WEIGHT = 0.3
HEAT_FACTOR = 2.0
DENSITY_FACTOR = 4.0
DIRECTIONS = ((1, 0, 0), (-1, 0, 0), (0, 1, 0), (0, -1, 0), (0, 0, 1), (0, 0, -1))


def offset_view(field, shift):
    return field[1 + shift[0]:field.shape[0] - 1 + shift[0],
                 1 + shift[1]:field.shape[1] - 1 + shift[1],
                 1 + shift[2]:field.shape[2] - 1 + shift[2]]


def relax_sweep(state_pad, eta_pad, density_driving_term, hole):
    eta_centre = offset_view(eta_pad, (0, 0, 0))
    face_eta = [0.5 * (eta_centre + offset_view(eta_pad, shift)) for shift in DIRECTIONS]
    diagonal = face_eta[0]
    for index_m in range(1, 6):
        diagonal = diagonal + face_eta[index_m]
    diagonal = diagonal + hole
    press_pad = state_pad[3]
    updated = []
    divergence = None
    for component in range(3):
        speed_pad = state_pad[component]
        speed_centre = offset_view(speed_pad, (0, 0, 0))
        laplace = face_eta[0] * (offset_view(speed_pad, DIRECTIONS[0]) - speed_centre)
        for index_m in range(1, 6):
            laplace = laplace + face_eta[index_m] * (offset_view(speed_pad, DIRECTIONS[index_m]) - speed_centre)
        forward = DIRECTIONS[2 * component]
        backward = DIRECTIONS[2 * component + 1]
        gradient = 0.5 * (offset_view(press_pad, forward) - offset_view(press_pad, backward))
        residual = laplace - gradient
        if component == 2:
            residual = residual + density_driving_term
        updated.append(speed_centre + RELAX_WEIGHT * residual / diagonal)
        flux_term = 0.5 * (offset_view(speed_pad, forward) - offset_view(speed_pad, backward))
        divergence = flux_term if divergence is None else divergence + flux_term
    updated.append(offset_view(press_pad, (0, 0, 0)) - PRESSURE_WEIGHT * eta_centre * divergence)
    return jnp.stack(updated)


def spread_bins(field, edge):
    return jnp.repeat(jnp.repeat(jnp.repeat(field, edge, axis=0), edge, axis=1), edge, axis=2)


def reference(tile_flow_speed, tile_stress_mean, tile_heat_state, tile_drag_coefficient, marker_attributes, marker_holding_tile, marker_voxel_number, prior_slot_of_tile):
    def grid_arrangement(field):
        moved = field[prior_slot_of_tile]
        depth = field.shape[1]
        laid = moved.reshape(N_WIDE, N_NARROW, LX, LY, LZ, depth, BS, BS, BS)
        laid = laid.transpose(5, 0, 2, 6, 1, 3, 7, 4, 8)
        return laid.reshape(depth, NX, NY, NZ)

    velocity_start = grid_arrangement(tile_flow_speed)
    pressure_start = grid_arrangement(tile_stress_mean[:, None])[0]
    heat_on_fresh_grid = grid_arrangement(tile_heat_state[:, None])[0]
    reference_drag_level = grid_arrangement(tile_drag_coefficient[:, None])[0]

    inverse = jnp.zeros((SUBGRID_COUNT,), jnp.int32).at[prior_slot_of_tile].set(jnp.arange(SUBGRID_COUNT, dtype=jnp.int32))
    new_index = inverse[marker_holding_tile]
    owner = new_index // BLOCKS_DEV
    place = new_index % BLOCKS_DEV
    outer = owner // N_NARROW
    inner = owner % N_NARROW
    bin_edge = BS // 4
    layer = marker_voxel_number // (BS * BS)
    row_cell = (marker_voxel_number // BS) % BS
    column = marker_voxel_number % BS
    bin_x = (outer * LX + place // (LY * LZ)) * 4 + layer // bin_edge
    bin_y = (inner * LY + (place // LZ) % LY) * 4 + row_cell // bin_edge
    bin_z = (place % LZ) * 4 + column // bin_edge
    segment = ((bin_x * NYB + bin_y) * NZB + bin_z).astype(jnp.int32)
    bin_total = NXB * NYB * NZB
    prop_sums = jax.ops.segment_sum(marker_attributes.T, segment, bin_total)
    live_counts = jax.ops.segment_sum(jnp.ones((NT,), jnp.float32), segment, bin_total)
    bin_mean_attributes = prop_sums / jnp.maximum(live_counts, 1.0)[:, None]
    bin_mean_attributes = bin_mean_attributes.T.reshape(NPROP, NXB, NYB, NZB)

    mixture = MIX_WEIGHTS[0] * bin_mean_attributes[0]
    for index_p in range(1, NPROP):
        mixture = mixture + MIX_WEIGHTS[index_p] * bin_mean_attributes[index_p]
    voxel_blend_share = spread_bins(mixture, bin_edge)
    drag_coefficient_grid = reference_drag_level * jnp.exp(HEAT_FACTOR * (0.5 - heat_on_fresh_grid) + voxel_blend_share)
    density_driving_term = DENSITY_FACTOR * heat_on_fresh_grid

    solved_quantities = jnp.concatenate([velocity_start, pressure_start[None]], axis=0)
    eta_pad = jnp.pad(drag_coefficient_grid, 1)
    for sweep_step in range(SWEEPS):
        solved_quantities = relax_sweep(jnp.pad(solved_quantities, ((0, 0), (1, 1), (1, 1), (1, 1))), eta_pad, density_driving_term, 0.0)
    return solved_quantities[:3], solved_quantities[3], heat_on_fresh_grid, bin_mean_attributes
```

```python
import functools

import jax
import jax.numpy as jnp
from jax import lax
from jax.experimental import pallas as pl
from jax.experimental.pallas import tpu as pltpu
from jax.sharding import PartitionSpec as P

BS = 16
LX = 1
LY = 2
LZ = 8
SWEEPS = 3
BINS = 64
FIELDS = 6
AHEAD = 3

MIX_WEIGHTS = (0.3, -0.25, 0.2, -0.15, 0.35, -0.3, 0.25, -0.2)
RELAX_WEIGHT = 0.7
PRESSURE_WEIGHT = 0.3
HEAT_FACTOR = 2.0
DENSITY_FACTOR = 4.0
MESH = pl.DeviceIdType.MESH


def swap_groups(x):
    row = lax.broadcasted_iota(jnp.int32, x.shape, 1)
    group = lax.broadcasted_iota(jnp.int32, x.shape, 2) // BS
    for bit in (1, 2, 4):
        row_set = (row & bit) != 0
        group_set = (group & bit) != 0
        from_above = pltpu.roll(pltpu.roll(x, 8 - bit, 1), BS * bit, 2)
        from_below = pltpu.roll(pltpu.roll(x, bit, 1), 8 * BS - BS * bit, 2)
        x = jnp.where(
            row_set == group_set, x, jnp.where(group_set, from_above, from_below)
        )
    return x


def bin_sums(base, holder_ref, voxel_ref, attr_ref, blocks, chunk):
    props, tracers = attr_ref.shape
    total_bins = blocks * BINS
    bin_ids = lax.broadcasted_iota(jnp.int32, (total_bins, chunk), 0)

    def step(turn, sums):
        at = pl.ds(pl.multiple_of(turn * chunk, chunk), chunk)
        voxel = voxel_ref[:, at]
        key = (
            (holder_ref[:, at] - base) * BINS
            + (voxel >> 10) * 16
            + ((voxel >> 6) & 3) * 4
            + ((voxel >> 2) & 3)
        )
        table = jnp.where(bin_ids == key, 1.0, 0.0).astype(jnp.bfloat16)
        values = attr_ref[:, at]
        high = values.astype(jnp.bfloat16)
        rest = values - high.astype(jnp.float32)
        middle = rest.astype(jnp.bfloat16)
        low = (rest - middle.astype(jnp.float32)).astype(jnp.bfloat16)
        ones = jnp.ones((props, chunk), jnp.bfloat16)
        rows = jnp.concatenate([high, middle, low, ones], axis=0)
        return sums + lax.dot_general(
            rows, table, (((1,), (1,)), ((), ())), preferred_element_type=jnp.float32
        )

    sums = lax.fori_loop(
        0, tracers // chunk, step, jnp.zeros((4 * props, total_bins), jnp.float32)
    )
    total = sums[:props] + sums[props : 2 * props] + sums[2 * props : 3 * props]
    return total / jnp.maximum(sums[3 * props :], 1.0)


def relax_slab(x, eta_pad, eta_edges, pad, edges, heat_ref):
    ny, nz = heat_ref.shape[1:]
    row = lax.broadcasted_iota(jnp.int32, (ny, nz), 0)
    column = lax.broadcasted_iota(jnp.int32, (ny, nz), 1)

    def around(here, lower, upper, low, high):
        return (
            here,
            upper,
            lower,
            jnp.where(row == ny - 1, high, pltpu.roll(here, ny - 1, 0)),
            jnp.where(row == 0, low, pltpu.roll(here, 1, 0)),
            jnp.where(column == nz - 1, 0.0, pltpu.roll(here, nz - 1, 1)),
            jnp.where(column == 0, 0.0, pltpu.roll(here, 1, 1)),
        )

    def field(k):
        return around(
            pad[k, x + 1], pad[k, x], pad[k, x + 2],
            edges[0, k, pl.ds(x, 1), :], edges[1, k, pl.ds(x, 1), :],
        )

    eta = around(
        eta_pad[x + 1], eta_pad[x], eta_pad[x + 2],
        eta_edges[0, pl.ds(x, 1), :], eta_edges[1, pl.ds(x, 1), :],
    )
    face = [0.5 * (eta[0] + eta[m]) for m in range(1, 7)]
    diagonal = face[0]
    for m in range(1, 6):
        diagonal = diagonal + face[m]
    scale = RELAX_WEIGHT / diagonal
    press = field(3)
    divergence = None
    moved = []
    for component in range(3):
        speed = field(component)
        residual = face[0] * (speed[1] - speed[0])
        for m in range(1, 6):
            residual = residual + face[m] * (speed[m + 1] - speed[0])
        up, down = 2 * component + 1, 2 * component + 2
        residual = residual - 0.5 * (press[up] - press[down])
        if component == 2:
            residual = residual + DENSITY_FACTOR * heat_ref[x]
        moved.append(speed[0] + residual * scale)
        flux = 0.5 * (speed[up] - speed[down])
        divergence = flux if divergence is None else divergence + flux
    moved.append(press[0] - PRESSURE_WEIGHT * eta[0] * divergence)
    return moved


def migrate_kernel(
    row_ref, slot_ref, flow_ref, stress_ref, warm_ref, drag_ref, attr_ref, holder_ref, voxel_ref,
    pad_ref, edge_ref, eta_ref, eta_edge_ref, heat_ref, mean_ref,
    table, wanted, wanted_smem, raw, lined, mine, stage_0, stage_1, stage_2, stage_3, stage_4, stage_5,
    land_0, land_1, land_2, land_3, land_4, land_5,
    attr, holder, voxel, mean_mine, mean_stage, mean_land, mean_held, held, drag_grid,
    pad_0, pad_1, edge_0, edge_1, edge_out, eta_out,
    raw_sems, table_sems, data_send, data_recv, mean_sems,
    eta_send, eta_recv, halo_send, halo_recv, small_sem,
    *, wide_count, narrow_count,
):
    count = wide_count * narrow_count
    wide, narrow = lax.axis_index("wide"), lax.axis_index("narrow")
    me = wide * narrow_count + narrow
    blocks = raw.shape[1]
    nx, ny, nz = heat_ref.shape
    stages = (stage_0, stage_1, stage_2, stage_3, stage_4, stage_5)
    lands = (land_0, land_1, land_2, land_3, land_4, land_5)
    pads = (pad_0, pad_1, pad_ref)
    edges = (edge_0, edge_1, edge_ref)

    sources = (
        warm_ref, drag_ref, flow_ref.at[0], flow_ref.at[1], flow_ref.at[2], stress_ref,
    )
    loads = [
        pltpu.make_async_copy(source, raw.at[f], raw_sems.at[f]) for f, source in enumerate(sources)
    ]
    loads.append(pltpu.make_async_copy(attr_ref, attr, raw_sems.at[FIELDS]))
    loads.append(pltpu.make_async_copy(holder_ref, holder, raw_sems.at[FIELDS + 1]))
    loads.append(pltpu.make_async_copy(voxel_ref, voxel, raw_sems.at[FIELDS + 2]))
    for load in loads:
        load.start()

    for pad in pads:
        for x in (0, nx + 1):
            pad[:, x] = jnp.zeros((4, ny, nz), jnp.float32)
    for x in (0, nx + 1):
        eta_ref[x] = jnp.zeros((ny, nz), jnp.float32)
    for edge in edges:
        edge[...] = jnp.zeros(edge.shape, jnp.float32)
    eta_edge_ref[...] = jnp.zeros(eta_edge_ref.shape, jnp.float32)

    def others(act):
        near = [lax.rem(narrow + b, narrow_count) for b in range(narrow_count)]
        for b in range(1, narrow_count):
            act(wide, near[b])

        def row(a, carry):
            far = lax.rem(wide + a, wide_count)
            for b in range(narrow_count):
                act(far, near[b])
            return carry

        lax.fori_loop(1, wide_count, row, 0)

    barrier = pltpu.get_barrier_semaphore()
    others(
        lambda w, n: pl.semaphore_signal(
            barrier, inc=1, device_id=(w, n), device_id_type=MESH
        )
    )
    table[me] = row_ref[...]
    pl.semaphore_wait(barrier, count - 1)

    def send_row(w, n):
        pltpu.make_async_remote_copy(
            src_ref=row_ref,
            dst_ref=table.at[me],
            send_sem=table_sems.at[0],
            recv_sem=table_sems.at[1],
            device_id=(w, n),
            device_id_type=MESH,
        ).start()

    others(send_row)

    def whole(ref, send_sem, recv_sem):
        part = ref.at[pl.ds(0, count - 1)]
        return pltpu.make_async_remote_copy(
            src_ref=part,
            dst_ref=part,
            send_sem=send_sem,
            recv_sem=recv_sem,
            device_id=(wide, narrow),
            device_id_type=MESH,
        )

    rows = BS * BS * BS // 128
    for f in range(FIELDS):
        loads[f].wait()
        for g in range(blocks // 8):
            for j in range(rows):
                lined[pl.ds(g * 8 * rows + j, 8, stride=rows), :] = raw[
                    f, g * 8 : g * 8 + 8, j * 128 : j * 128 + 128
                ]
        mine[f] = lined[...].reshape(blocks, rows, 128)

    whole(table, table_sems.at[0], table_sems.at[1]).wait_recv()
    local_old = table[...] - me * blocks
    is_mine = (local_old >= 0) & (local_old < blocks)
    chosen = jnp.sum(jnp.where(is_mine, local_old, 0), axis=2, keepdims=True)
    wanted[...] = jnp.broadcast_to(chosen, wanted.shape)
    to_scalar = pltpu.make_async_copy(wanted, wanted_smem, small_sem)
    to_scalar.start()
    to_scalar.wait()

    def block_rows(f, d):
        return mine[f, wanted_smem[d, 0, 0]]

    def send_field(f):
        def send(w, n):
            d = w * narrow_count + n
            stages[f][d] = block_rows(f, d)
            pltpu.make_async_remote_copy(
                src_ref=stages[f].at[d],
                dst_ref=lands[f].at[me],
                send_sem=data_send.at[f],
                recv_sem=data_recv.at[f],
                device_id=(w, n),
                device_id_type=MESH,
            ).start()

        others(send)
        lands[f][me] = block_rows(f, me)

    for f in range(AHEAD):
        send_field(f)

    for load in loads[FIELDS:]:
        load.wait()
    tracers = attr.shape[1]
    chunk = 1024 if tracers % 1024 == 0 else tracers
    means = bin_sums(me * blocks, holder, voxel, attr, blocks, chunk)
    left = lax.broadcasted_iota(jnp.int32, (8, 128), 1) < BINS
    for q in range(blocks // 2):
        pair = means[:, q * 128 : q * 128 + 128]
        across = pltpu.roll(pair, BINS, 1)
        below = pltpu.roll(pair, 4, 0)
        both = pltpu.roll(across, 4, 0)
        mean_mine[2 * q] = jnp.where(left, pair, both)[:4]
        mean_mine[2 * q + 1] = jnp.where(left, across, below)[:4]

    def send_mean(w, n):
        d = w * narrow_count + n
        mean_stage[d] = mean_mine[wanted_smem[d, 0, 0]]
        pltpu.make_async_remote_copy(
            src_ref=mean_stage.at[d],
            dst_ref=mean_land.at[me],
            send_sem=mean_sems.at[0],
            recv_sem=mean_sems.at[1],
            device_id=(w, n),
            device_id_type=MESH,
        ).start()

    others(send_mean)
    mean_land[me] = mean_mine[wanted_smem[me, 0, 0]]

    def source_of(y, z):
        return lax.div(slot_ref[y * LZ + z], blocks)

    def grid_part(f, y):
        for z in range(LZ):
            held[pl.ds(z, rows, stride=LZ), :] = lands[f][source_of(y, z)]
        return swap_groups(held[...].reshape(rows, LZ, 128)).reshape(BS, BS, 128)

    exists = (wide > 0, wide < wide_count - 1, narrow > 0, narrow < narrow_count - 1)
    partner = ((wide - 1, narrow), (wide + 1, narrow), (wide, narrow - 1), (wide, narrow + 1))

    def eta_copy(side, arriving=False):
        if side < 2:
            source = eta_ref.at[1 if side == 0 else nx]
            target = eta_ref.at[nx + 1 if side == 0 else 0]
            mine_at = eta_ref.at[0 if side == 0 else nx + 1]
        else:
            source = eta_out.at[side - 2]
            target = eta_edge_ref.at[3 - side]
            mine_at = eta_edge_ref.at[side - 2]
        return pltpu.make_async_remote_copy(
            src_ref=mine_at if arriving else source,
            dst_ref=mine_at if arriving else target,
            send_sem=eta_send.at[side],
            recv_sem=eta_recv.at[side if arriving else side ^ 1],
            device_id=partner[side],
            device_id_type=MESH,
        )

    def halo_copy(turn, side, arriving=False):
        pad = pads[turn]
        if side < 2:
            source = pad.at[:, 1 if side == 0 else nx]
            target = pad.at[:, nx + 1 if side == 0 else 0]
            mine_at = pad.at[:, 0 if side == 0 else nx + 1]
        else:
            source = edge_out.at[turn, side - 2]
            target = edges[turn].at[3 - side]
            mine_at = edges[turn].at[side - 2]
        return pltpu.make_async_remote_copy(
            src_ref=mine_at if arriving else source,
            dst_ref=mine_at if arriving else target,
            send_sem=halo_send.at[turn, side],
            recv_sem=halo_recv.at[turn, side if arriving else side ^ 1],
            device_id=partner[side],
            device_id_type=MESH,
        )

    def each_side(act, sides=range(4)):
        for side in sides:

            @pl.when(exists[side])
            def _(side=side):
                act(side)

    def viscosity():
        whole(mean_land, mean_sems.at[0], mean_sems.at[1]).wait_recv()
        expand = (
            lax.broadcasted_iota(jnp.int32, (LZ, 32), 0)
            == lax.broadcasted_iota(jnp.int32, (LZ, 32), 1) // 4
        ).astype(jnp.float32)
        same = (
            lax.broadcasted_iota(jnp.int32, (128, 32), 0) % 4
            == lax.broadcasted_iota(jnp.int32, (128, 32), 1) % 4
        )
        gather = (
            lax.broadcasted_iota(jnp.int32, (32, 128), 0)
            == lax.broadcasted_iota(jnp.int32, (32, 128), 1) // 4
        ).astype(jnp.float32)
        for y in range(LY):
            for z in range(LZ):
                mean_held[pl.ds(z, 4, stride=LZ), :] = mean_land[source_of(y, z)]
            for p in range(4):
                tall = jnp.dot(
                    mean_held[p * LZ : p * LZ + LZ].T, expand,
                    precision=lax.Precision.HIGHEST, preferred_element_type=jnp.float32,
                )
                cells = jnp.dot(
                    gather, jnp.where(same, tall, 0.0),
                    precision=lax.Precision.HIGHEST, preferred_element_type=jnp.float32,
                )
                for half in range(2):
                    for layer in range(4):
                        at = half * 16 + layer * 4
                        mean_ref[half * 4 + p, layer, y * 4 : y * 4 + 4, :] = cells[at : at + 4]
        for layer in range(4):
            mixture = MIX_WEIGHTS[0] * mean_ref[0, layer]
            for p in range(1, len(MIX_WEIGHTS)):
                mixture = mixture + MIX_WEIGHTS[p] * mean_ref[p, layer]
            wide_mix = jnp.dot(
                mixture, gather,
                precision=lax.Precision.HIGHEST, preferred_element_type=jnp.float32,
            )
            spread = jnp.concatenate(
                [jnp.broadcast_to(wide_mix[j : j + 1], (4, 128)) for j in range(LY * 4)], axis=0
            )
            for x in range(layer * 4, layer * 4 + 4):
                eta_ref[x + 1] = drag_grid[x] * jnp.exp(
                    HEAT_FACTOR * (0.5 - heat_ref[x]) + spread
                )
        for x in range(nx):
            eta_out[0, x : x + 1] = eta_ref[x + 1, 0:1]
            eta_out[1, x : x + 1] = eta_ref[x + 1, ny - 1 : ny]
        each_side(lambda side: eta_copy(side).start())

    for f in range(FIELDS):
        whole(lands[f], data_send.at[f], data_recv.at[f]).wait_recv()
        if f + AHEAD < FIELDS:
            send_field(f + AHEAD)
        for y in range(LY):
            at = slice(y * BS, (y + 1) * BS)
            part = grid_part(f, y)
            if f == 0:
                heat_ref[:, at, :] = part
            elif f == 1:
                drag_grid[:, at, :] = part
            else:
                pad_0[f - 2, 1 : nx + 1, at, :] = part
        if f == 1:
            viscosity()

    for turn in range(SWEEPS):
        pad = pads[turn]
        each_side(lambda side: halo_copy(turn, side).start(), range(2))
        for k in range(4):
            edge_out[turn, 0, k] = pad[k, 1 : nx + 1, 0, :]
            edge_out[turn, 1, k] = pad[k, 1 : nx + 1, ny - 1, :]
        each_side(lambda side: halo_copy(turn, side).start(), range(2, 4))
        if turn == 0:
            each_side(lambda side: eta_copy(side, True).wait_recv())
        each_side(lambda side: halo_copy(turn, side, True).wait_recv())
        if turn < SWEEPS - 1:

            def slab(x, carry, turn=turn):
                moved = relax_slab(x, eta_ref, eta_edge_ref, pads[turn], edges[turn], heat_ref)
                for k in range(4):
                    pads[turn + 1][k, x + 1] = moved[k]
                return carry

            lax.fori_loop(0, nx, slab, 0)

    whole(table, table_sems.at[0], table_sems.at[1]).wait_send()
    whole(mean_land, mean_sems.at[0], mean_sems.at[1]).wait_send()
    for f in range(FIELDS):
        whole(lands[f], data_send.at[f], data_recv.at[f]).wait_send()
    each_side(lambda side: eta_copy(side).wait_send())
    for turn in range(SWEEPS):
        each_side(lambda side: halo_copy(turn, side).wait_send())


def migrate(row, slots, flow, stress, heat, drag, attributes, holder, voxel):
    wide_count, narrow_count = lax.axis_size("wide"), lax.axis_size("narrow")
    count = wide_count * narrow_count
    blocks = slots.shape[0]
    tracers = attributes.shape[1]
    nx, ny, nz = LX * BS, LY * BS, LZ * BS
    rows = BS * BS * BS // 128
    vmem = pl.BlockSpec(memory_space=pltpu.VMEM)
    smem = pl.BlockSpec(memory_space=pltpu.SMEM)
    hbm = pl.BlockSpec(memory_space=pltpu.HBM)
    f32 = jnp.float32
    per_field = [pltpu.VMEM((count, rows, 128), f32)] * FIELDS
    dma = pltpu.SemaphoreType.DMA
    return pl.pallas_call(
        functools.partial(migrate_kernel, wide_count=wide_count, narrow_count=narrow_count),
        out_shape=(
            jax.ShapeDtypeStruct((4, nx + 2, ny, nz), f32),
            jax.ShapeDtypeStruct((2, 4, nx, nz), f32),
            jax.ShapeDtypeStruct((nx + 2, ny, nz), f32),
            jax.ShapeDtypeStruct((2, nx, nz), f32),
            jax.ShapeDtypeStruct((nx, ny, nz), f32),
            jax.ShapeDtypeStruct((8, LX * 4, LY * 4, LZ * 4), f32),
        ),
        in_specs=[vmem, smem] + [hbm] * 7,
        out_specs=(vmem,) * 6,
        scratch_shapes=[
            pltpu.VMEM((count, 1, 128), jnp.int32),
            pltpu.VMEM((count, 1, 128), jnp.int32),
            pltpu.SMEM((count, 1, 128), jnp.int32),
            pltpu.VMEM((FIELDS, blocks, rows * 128), f32),
            pltpu.VMEM((blocks * rows, 128), f32),
            pltpu.VMEM((FIELDS, blocks, rows, 128), f32),
            *per_field,
            *per_field,
            pltpu.VMEM((8, tracers), f32),
            pltpu.VMEM((1, tracers), jnp.int32),
            pltpu.VMEM((1, tracers), jnp.int32),
            pltpu.VMEM((blocks, 4, 128), f32),
            pltpu.VMEM((count, 4, 128), f32),
            pltpu.VMEM((count, 4, 128), f32),
            pltpu.VMEM((4 * LZ, 128), f32),
            pltpu.VMEM((rows * LZ, 128), f32),
            pltpu.VMEM((nx, ny, nz), f32),
            pltpu.VMEM((4, nx + 2, ny, nz), f32),
            pltpu.VMEM((4, nx + 2, ny, nz), f32),
            pltpu.VMEM((2, 4, nx, nz), f32),
            pltpu.VMEM((2, 4, nx, nz), f32),
            pltpu.VMEM((SWEEPS, 2, 4, nx, nz), f32),
            pltpu.VMEM((2, nx, nz), f32),
            dma((FIELDS + 3,)),
            dma((2,)),
            dma((FIELDS,)),
            dma((FIELDS,)),
            dma((2,)),
            dma((4,)),
            dma((4,)),
            dma((SWEEPS, 4)),
            dma((SWEEPS, 4)),
            dma(()),
        ],
        compiler_params=pltpu.CompilerParams(
            collective_id=1,
            has_side_effects=True,
            vmem_limit_bytes=(24 if count <= 32 else 52) * 1024 * 1024,
        ),
    )(row, slots, flow, stress, heat, drag, attributes, holder, voxel)


def last_kernel(
    pad_ref, edge_ref, eta_ref, eta_edge_ref, heat_ref, mean_ref,
    velocity_ref, pressure_ref, heat_out_ref, mean_out_ref, fresh, sems, *, parts,
):
    nx = heat_ref.shape[0]
    thick = nx // parts
    copies = [
        pltpu.make_async_copy(heat_ref, heat_out_ref, sems.at[2 * parts]),
        pltpu.make_async_copy(mean_ref, mean_out_ref, sems.at[2 * parts + 1]),
    ]
    for copy in copies:
        copy.start()
    for part in range(parts):

        def slab(x, carry):
            moved = relax_slab(x, eta_ref, eta_edge_ref, pad_ref, edge_ref, heat_ref)
            for k in range(4):
                fresh[k, x] = moved[k]
            return carry

        lax.fori_loop(part * thick, (part + 1) * thick, slab, 0)
        at = pl.ds(part * thick, thick)
        copies.append(
            pltpu.make_async_copy(
                fresh.at[pl.ds(0, 3), at], velocity_ref.at[:, at], sems.at[2 * part]
            )
        )
        copies.append(
            pltpu.make_async_copy(fresh.at[3, at], pressure_ref.at[at], sems.at[2 * part + 1])
        )
        for copy in copies[-2:]:
            copy.start()
    for copy in copies:
        copy.wait()


def last_sweep(pad, edge, eta, eta_edge, heat, means):
    nx, ny, nz = heat.shape
    parts = 4
    vmem = pl.BlockSpec(memory_space=pltpu.VMEM)
    hbm = pl.BlockSpec(memory_space=pltpu.HBM)
    return pl.pallas_call(
        functools.partial(last_kernel, parts=parts),
        out_shape=(
            jax.ShapeDtypeStruct((3, nx, ny, nz), jnp.float32),
            jax.ShapeDtypeStruct((nx, ny, nz), jnp.float32),
            jax.ShapeDtypeStruct(heat.shape, jnp.float32),
            jax.ShapeDtypeStruct(means.shape, jnp.float32),
        ),
        in_specs=[vmem] * 6,
        out_specs=(hbm,) * 4,
        scratch_shapes=[
            pltpu.VMEM((4, nx, ny, nz), jnp.float32),
            pltpu.SemaphoreType.DMA((2 * parts + 2,)),
        ],
        compiler_params=pltpu.CompilerParams(vmem_limit_bytes=16 * 1024 * 1024),
    )(pad, edge, eta, eta_edge, heat, means)


def per_device(
    tile_flow_speed,
    tile_stress_mean,
    tile_heat_state,
    tile_drag_coefficient,
    marker_attributes,
    marker_holding_tile,
    marker_voxel_number,
    prior_slot_of_tile,
):
    blocks = prior_slot_of_tile.shape[0]
    tracers = marker_attributes.shape[1]
    row = jnp.pad(prior_slot_of_tile, (0, 128 - blocks), constant_values=-1).reshape(1, 128)
    pad, edge, eta, eta_edge, heat, means = migrate(
        row,
        prior_slot_of_tile,
        tile_flow_speed.transpose(1, 0, 2),
        tile_stress_mean,
        tile_heat_state,
        tile_drag_coefficient,
        marker_attributes,
        marker_holding_tile.reshape(1, tracers),
        marker_voxel_number.reshape(1, tracers),
    )
    return last_sweep(pad, edge, eta, eta_edge, heat, means)


def solution(mesh):
    in_specs = (
        P(("wide", "narrow"), None, None),
        P(("wide", "narrow"), None),
        P(("wide", "narrow"), None),
        P(("wide", "narrow"), None),
        P(None, ("wide", "narrow")),
        P(("wide", "narrow")),
        P(("wide", "narrow")),
        P(("wide", "narrow")),
    )
    out_specs = (
        P(None, "wide", "narrow", None),
        P("wide", "narrow", None),
        P("wide", "narrow", None),
        P(None, "wide", "narrow", None),
    )
    return jax.shard_map(
        per_device, mesh=mesh, in_specs=in_specs, out_specs=out_specs, check_vma=False
    )
```

```python
import functools

import jax
import jax.numpy as jnp
from jax import lax
from jax.experimental import pallas as pl
from jax.experimental.pallas import tpu as pltpu
from jax.sharding import PartitionSpec as P

BS = 16
LX = 1
LY = 2
LZ = 8
SWEEPS = 3
BINS = 64
FIELDS = 6
AHEAD = 3

MIX_WEIGHTS = (0.3, -0.25, 0.2, -0.15, 0.35, -0.3, 0.25, -0.2)
RELAX_WEIGHT = 0.7
PRESSURE_WEIGHT = 0.3
HEAT_FACTOR = 2.0
DENSITY_FACTOR = 4.0
MESH = pl.DeviceIdType.MESH


def swap_groups(x):
    row = lax.broadcasted_iota(jnp.int32, x.shape, 1)
    group = lax.broadcasted_iota(jnp.int32, x.shape, 2) // BS
    for bit in (1, 2, 4):
        row_set = (row & bit) != 0
        group_set = (group & bit) != 0
        from_above = pltpu.roll(pltpu.roll(x, 8 - bit, 1), BS * bit, 2)
        from_below = pltpu.roll(pltpu.roll(x, bit, 1), 8 * BS - BS * bit, 2)
        x = jnp.where(
            row_set == group_set, x, jnp.where(group_set, from_above, from_below)
        )
    return x


def bin_sums(base, holder_ref, voxel_ref, attr_ref, blocks, chunk):
    props, tracers = attr_ref.shape
    total_bins = blocks * BINS
    bin_ids = lax.broadcasted_iota(jnp.int32, (total_bins, chunk), 0)

    def step(turn, sums):
        at = pl.ds(pl.multiple_of(turn * chunk, chunk), chunk)
        voxel = voxel_ref[:, at]
        key = (
            (holder_ref[:, at] - base) * BINS
            + (voxel >> 10) * 16
            + ((voxel >> 6) & 3) * 4
            + ((voxel >> 2) & 3)
        )
        table = jnp.where(bin_ids == key, 1.0, 0.0).astype(jnp.bfloat16)
        values = attr_ref[:, at]
        high = values.astype(jnp.bfloat16)
        rest = values - high.astype(jnp.float32)
        middle = rest.astype(jnp.bfloat16)
        low = (rest - middle.astype(jnp.float32)).astype(jnp.bfloat16)
        ones = jnp.ones((props, chunk), jnp.bfloat16)
        rows = jnp.concatenate([high, middle, low, ones], axis=0)
        return sums + lax.dot_general(
            rows, table, (((1,), (1,)), ((), ())), preferred_element_type=jnp.float32
        )

    sums = lax.fori_loop(
        0, tracers // chunk, step, jnp.zeros((4 * props, total_bins), jnp.float32)
    )
    total = sums[:props] + sums[props : 2 * props] + sums[2 * props : 3 * props]
    return total / jnp.maximum(sums[3 * props :], 1.0)


def relax_slab(x, eta_pad, eta_edges, pad, edges, heat_ref):
    ny, nz = heat_ref.shape[1:]
    row = lax.broadcasted_iota(jnp.int32, (ny, nz), 0)
    column = lax.broadcasted_iota(jnp.int32, (ny, nz), 1)

    def around(here, lower, upper, low, high):
        return (
            here,
            upper,
            lower,
            jnp.where(row == ny - 1, high, pltpu.roll(here, ny - 1, 0)),
            jnp.where(row == 0, low, pltpu.roll(here, 1, 0)),
            jnp.where(column == nz - 1, 0.0, pltpu.roll(here, nz - 1, 1)),
            jnp.where(column == 0, 0.0, pltpu.roll(here, 1, 1)),
        )

    def field(k):
        return around(
            pad[k, x + 1], pad[k, x], pad[k, x + 2],
            edges[0, k, pl.ds(x, 1), :], edges[1, k, pl.ds(x, 1), :],
        )

    eta = around(
        eta_pad[x + 1], eta_pad[x], eta_pad[x + 2],
        eta_edges[0, pl.ds(x, 1), :], eta_edges[1, pl.ds(x, 1), :],
    )
    face = [0.5 * (eta[0] + eta[m]) for m in range(1, 7)]
    diagonal = face[0]
    for m in range(1, 6):
        diagonal = diagonal + face[m]
    scale = RELAX_WEIGHT / diagonal
    press = field(3)
    divergence = None
    moved = []
    for component in range(3):
        speed = field(component)
        residual = face[0] * (speed[1] - speed[0])
        for m in range(1, 6):
            residual = residual + face[m] * (speed[m + 1] - speed[0])
        up, down = 2 * component + 1, 2 * component + 2
        residual = residual - 0.5 * (press[up] - press[down])
        if component == 2:
            residual = residual + DENSITY_FACTOR * heat_ref[x]
        moved.append(speed[0] + residual * scale)
        flux = 0.5 * (speed[up] - speed[down])
        divergence = flux if divergence is None else divergence + flux
    moved.append(press[0] - PRESSURE_WEIGHT * eta[0] * divergence)
    return moved


def migrate_kernel(
    places_ref, flow_ref, stress_ref, warm_ref, drag_ref, attr_ref, holder_ref, voxel_ref,
    pad_ref, edge_ref, eta_ref, eta_edge_ref, heat_ref, mean_ref,
    slot_ref, row_ref, table, wanted, wanted_smem, raw, lined, mine, stage_0, stage_1, stage_2, stage_3, stage_4, stage_5,
    land_0, land_1, land_2, land_3, land_4, land_5,
    attr, holder, voxel, mean_mine, mean_stage, mean_land, mean_held, held, drag_grid,
    pad_0, pad_1, edge_0, edge_1, edge_out, eta_out,
    raw_sems, table_sems, data_send, data_recv, mean_sems,
    eta_send, eta_recv, halo_send, halo_recv, small_sem,
    *, wide_count, narrow_count,
):
    count = wide_count * narrow_count
    wide, narrow = lax.axis_index("wide"), lax.axis_index("narrow")
    me = wide * narrow_count + narrow
    blocks = raw.shape[1]
    nx, ny, nz = heat_ref.shape
    stages = (stage_0, stage_1, stage_2, stage_3, stage_4, stage_5)
    lands = (land_0, land_1, land_2, land_3, land_4, land_5)
    pads = (pad_0, pad_1, pad_ref)
    edges = (edge_0, edge_1, edge_ref)

    to_slots = pltpu.make_async_copy(places_ref, slot_ref, small_sem)
    to_slots.start()
    sources = (
        warm_ref, drag_ref, flow_ref.at[0], flow_ref.at[1], flow_ref.at[2], stress_ref,
    )
    loads = [
        pltpu.make_async_copy(source, raw.at[f], raw_sems.at[f]) for f, source in enumerate(sources)
    ]
    loads.append(pltpu.make_async_copy(attr_ref, attr, raw_sems.at[FIELDS]))
    loads.append(pltpu.make_async_copy(holder_ref, holder, raw_sems.at[FIELDS + 1]))
    loads.append(pltpu.make_async_copy(voxel_ref, voxel, raw_sems.at[FIELDS + 2]))
    for load in loads:
        load.start()

    for pad in pads:
        for x in (0, nx + 1):
            pad[:, x] = jnp.zeros((4, ny, nz), jnp.float32)
    for x in (0, nx + 1):
        eta_ref[x] = jnp.zeros((ny, nz), jnp.float32)
    for edge in edges:
        edge[...] = jnp.zeros(edge.shape, jnp.float32)
    eta_edge_ref[...] = jnp.zeros(eta_edge_ref.shape, jnp.float32)

    def others(act):
        near = [lax.rem(narrow + b, narrow_count) for b in range(narrow_count)]
        for b in range(1, narrow_count):
            act(wide, near[b])

        def row(a, carry):
            far = lax.rem(wide + a, wide_count)
            for b in range(narrow_count):
                act(far, near[b])
            return carry

        lax.fori_loop(1, wide_count, row, 0)

    barrier = pltpu.get_barrier_semaphore()
    others(
        lambda w, n: pl.semaphore_signal(
            barrier, inc=1, device_id=(w, n), device_id_type=MESH
        )
    )
    to_slots.wait()
    lane = lax.broadcasted_iota(jnp.int32, (1, 128), 1)
    places = jnp.full((1, 128), -1, jnp.int32)
    for r in range(blocks):
        places = jnp.where(lane == r, slot_ref[r], places)
    row_ref[...] = places
    table[me] = places
    pl.semaphore_wait(barrier, count - 1)

    def send_row(w, n):
        pltpu.make_async_remote_copy(
            src_ref=row_ref,
            dst_ref=table.at[me],
            send_sem=table_sems.at[0],
            recv_sem=table_sems.at[1],
            device_id=(w, n),
            device_id_type=MESH,
        ).start()

    others(send_row)

    def whole(ref, send_sem, recv_sem):
        part = ref.at[pl.ds(0, count - 1)]
        return pltpu.make_async_remote_copy(
            src_ref=part,
            dst_ref=part,
            send_sem=send_sem,
            recv_sem=recv_sem,
            device_id=(wide, narrow),
            device_id_type=MESH,
        )

    rows = BS * BS * BS // 128
    for f in range(FIELDS):
        loads[f].wait()
        for g in range(blocks // 8):
            for j in range(rows):
                lined[pl.ds(g * 8 * rows + j, 8, stride=rows), :] = raw[
                    f, g * 8 : g * 8 + 8, j * 128 : j * 128 + 128
                ]
        mine[f] = lined[...].reshape(blocks, rows, 128)

    whole(table, table_sems.at[0], table_sems.at[1]).wait_recv()
    local_old = table[...] - me * blocks
    is_mine = (local_old >= 0) & (local_old < blocks)
    chosen = jnp.sum(jnp.where(is_mine, local_old, 0), axis=2, keepdims=True)
    wanted[...] = jnp.broadcast_to(chosen, wanted.shape)
    to_scalar = pltpu.make_async_copy(wanted, wanted_smem, small_sem)
    to_scalar.start()
    to_scalar.wait()

    def block_rows(f, d):
        return mine[f, wanted_smem[d, 0, 0]]

    def send_field(f):
        def send(w, n):
            d = w * narrow_count + n
            stages[f][d] = block_rows(f, d)
            pltpu.make_async_remote_copy(
                src_ref=stages[f].at[d],
                dst_ref=lands[f].at[me],
                send_sem=data_send.at[f],
                recv_sem=data_recv.at[f],
                device_id=(w, n),
                device_id_type=MESH,
            ).start()

        others(send)
        lands[f][me] = block_rows(f, me)

    for f in range(AHEAD):
        send_field(f)

    for load in loads[FIELDS:]:
        load.wait()
    tracers = attr.shape[1]
    chunk = 1024 if tracers % 1024 == 0 else tracers
    means = bin_sums(me * blocks, holder, voxel, attr, blocks, chunk)
    left = lax.broadcasted_iota(jnp.int32, (8, 128), 1) < BINS
    for q in range(blocks // 2):
        pair = means[:, q * 128 : q * 128 + 128]
        across = pltpu.roll(pair, BINS, 1)
        below = pltpu.roll(pair, 4, 0)
        both = pltpu.roll(across, 4, 0)
        mean_mine[2 * q] = jnp.where(left, pair, both)[:4]
        mean_mine[2 * q + 1] = jnp.where(left, across, below)[:4]

    def send_mean(w, n):
        d = w * narrow_count + n
        mean_stage[d] = mean_mine[wanted_smem[d, 0, 0]]
        pltpu.make_async_remote_copy(
            src_ref=mean_stage.at[d],
            dst_ref=mean_land.at[me],
            send_sem=mean_sems.at[0],
            recv_sem=mean_sems.at[1],
            device_id=(w, n),
            device_id_type=MESH,
        ).start()

    others(send_mean)
    mean_land[me] = mean_mine[wanted_smem[me, 0, 0]]

    def source_of(y, z):
        return lax.div(slot_ref[y * LZ + z], blocks)

    def grid_part(f, y):
        for z in range(LZ):
            held[pl.ds(z, rows, stride=LZ), :] = lands[f][source_of(y, z)]
        return swap_groups(held[...].reshape(rows, LZ, 128)).reshape(BS, BS, 128)

    exists = (wide > 0, wide < wide_count - 1, narrow > 0, narrow < narrow_count - 1)
    partner = ((wide - 1, narrow), (wide + 1, narrow), (wide, narrow - 1), (wide, narrow + 1))

    def eta_copy(side, arriving=False):
        if side < 2:
            source = eta_ref.at[1 if side == 0 else nx]
            target = eta_ref.at[nx + 1 if side == 0 else 0]
            mine_at = eta_ref.at[0 if side == 0 else nx + 1]
        else:
            source = eta_out.at[side - 2]
            target = eta_edge_ref.at[3 - side]
            mine_at = eta_edge_ref.at[side - 2]
        return pltpu.make_async_remote_copy(
            src_ref=mine_at if arriving else source,
            dst_ref=mine_at if arriving else target,
            send_sem=eta_send.at[side],
            recv_sem=eta_recv.at[side if arriving else side ^ 1],
            device_id=partner[side],
            device_id_type=MESH,
        )

    def halo_copy(turn, side, arriving=False):
        pad = pads[turn]
        if side < 2:
            source = pad.at[:, 1 if side == 0 else nx]
            target = pad.at[:, nx + 1 if side == 0 else 0]
            mine_at = pad.at[:, 0 if side == 0 else nx + 1]
        else:
            source = edge_out.at[turn, side - 2]
            target = edges[turn].at[3 - side]
            mine_at = edges[turn].at[side - 2]
        return pltpu.make_async_remote_copy(
            src_ref=mine_at if arriving else source,
            dst_ref=mine_at if arriving else target,
            send_sem=halo_send.at[turn, side],
            recv_sem=halo_recv.at[turn, side if arriving else side ^ 1],
            device_id=partner[side],
            device_id_type=MESH,
        )

    def each_side(act, sides=range(4)):
        for side in sides:

            @pl.when(exists[side])
            def _(side=side):
                act(side)

    def viscosity():
        whole(mean_land, mean_sems.at[0], mean_sems.at[1]).wait_recv()
        expand = (
            lax.broadcasted_iota(jnp.int32, (LZ, 32), 0)
            == lax.broadcasted_iota(jnp.int32, (LZ, 32), 1) // 4
        ).astype(jnp.float32)
        same = (
            lax.broadcasted_iota(jnp.int32, (128, 32), 0) % 4
            == lax.broadcasted_iota(jnp.int32, (128, 32), 1) % 4
        )
        gather = (
            lax.broadcasted_iota(jnp.int32, (32, 128), 0)
            == lax.broadcasted_iota(jnp.int32, (32, 128), 1) // 4
        ).astype(jnp.float32)
        for y in range(LY):
            for z in range(LZ):
                mean_held[pl.ds(z, 4, stride=LZ), :] = mean_land[source_of(y, z)]
            for p in range(4):
                tall = jnp.dot(
                    mean_held[p * LZ : p * LZ + LZ].T, expand,
                    precision=lax.Precision.HIGHEST, preferred_element_type=jnp.float32,
                )
                cells = jnp.dot(
                    gather, jnp.where(same, tall, 0.0),
                    precision=lax.Precision.HIGHEST, preferred_element_type=jnp.float32,
                )
                for half in range(2):
                    for layer in range(4):
                        at = half * 16 + layer * 4
                        mean_ref[half * 4 + p, layer, y * 4 : y * 4 + 4, :] = cells[at : at + 4]
        for layer in range(4):
            mixture = MIX_WEIGHTS[0] * mean_ref[0, layer]
            for p in range(1, len(MIX_WEIGHTS)):
                mixture = mixture + MIX_WEIGHTS[p] * mean_ref[p, layer]
            wide_mix = jnp.dot(
                mixture, gather,
                precision=lax.Precision.HIGHEST, preferred_element_type=jnp.float32,
            )
            spread = jnp.concatenate(
                [jnp.broadcast_to(wide_mix[j : j + 1], (4, 128)) for j in range(LY * 4)], axis=0
            )
            for x in range(layer * 4, layer * 4 + 4):
                eta_ref[x + 1] = drag_grid[x] * jnp.exp(
                    HEAT_FACTOR * (0.5 - heat_ref[x]) + spread
                )
        for x in range(nx):
            eta_out[0, x : x + 1] = eta_ref[x + 1, 0:1]
            eta_out[1, x : x + 1] = eta_ref[x + 1, ny - 1 : ny]
        each_side(lambda side: eta_copy(side).start())

    for f in range(FIELDS):
        whole(lands[f], data_send.at[f], data_recv.at[f]).wait_recv()
        if f + AHEAD < FIELDS:
            send_field(f + AHEAD)
        for y in range(LY):
            at = slice(y * BS, (y + 1) * BS)
            part = grid_part(f, y)
            if f == 0:
                heat_ref[:, at, :] = part
            elif f == 1:
                drag_grid[:, at, :] = part
            else:
                pad_0[f - 2, 1 : nx + 1, at, :] = part
        if f == 1:
            viscosity()

    for turn in range(SWEEPS):
        pad = pads[turn]
        each_side(lambda side: halo_copy(turn, side).start(), range(2))
        for k in range(4):
            edge_out[turn, 0, k] = pad[k, 1 : nx + 1, 0, :]
            edge_out[turn, 1, k] = pad[k, 1 : nx + 1, ny - 1, :]
        each_side(lambda side: halo_copy(turn, side).start(), range(2, 4))
        if turn == 0:
            each_side(lambda side: eta_copy(side, True).wait_recv())
        each_side(lambda side: halo_copy(turn, side, True).wait_recv())
        if turn < SWEEPS - 1:

            def slab(x, carry, turn=turn):
                moved = relax_slab(x, eta_ref, eta_edge_ref, pads[turn], edges[turn], heat_ref)
                for k in range(4):
                    pads[turn + 1][k, x + 1] = moved[k]
                return carry

            lax.fori_loop(0, nx, slab, 0)

    whole(table, table_sems.at[0], table_sems.at[1]).wait_send()
    whole(mean_land, mean_sems.at[0], mean_sems.at[1]).wait_send()
    for f in range(FIELDS):
        whole(lands[f], data_send.at[f], data_recv.at[f]).wait_send()
    each_side(lambda side: eta_copy(side).wait_send())
    for turn in range(SWEEPS):
        each_side(lambda side: halo_copy(turn, side).wait_send())


def migrate(slots, flow, stress, heat, drag, attributes, holder, voxel):
    wide_count, narrow_count = lax.axis_size("wide"), lax.axis_size("narrow")
    count = wide_count * narrow_count
    blocks = slots.shape[0]
    tracers = attributes.shape[1]
    nx, ny, nz = LX * BS, LY * BS, LZ * BS
    rows = BS * BS * BS // 128
    vmem = pl.BlockSpec(memory_space=pltpu.VMEM)
    hbm = pl.BlockSpec(memory_space=pltpu.HBM)
    f32 = jnp.float32
    per_field = [pltpu.VMEM((count, rows, 128), f32)] * FIELDS
    dma = pltpu.SemaphoreType.DMA
    pinned = [
        pltpu.with_memory_space_constraint(array, pltpu.HBM)
        for array in (slots, flow, stress, heat, drag, attributes, holder, voxel)
    ]
    return pl.pallas_call(
        functools.partial(migrate_kernel, wide_count=wide_count, narrow_count=narrow_count),
        out_shape=(
            jax.ShapeDtypeStruct((4, nx + 2, ny, nz), f32),
            jax.ShapeDtypeStruct((2, 4, nx, nz), f32),
            jax.ShapeDtypeStruct((nx + 2, ny, nz), f32),
            jax.ShapeDtypeStruct((2, nx, nz), f32),
            jax.ShapeDtypeStruct((nx, ny, nz), f32),
            jax.ShapeDtypeStruct((8, LX * 4, LY * 4, LZ * 4), f32),
        ),
        in_specs=[hbm] * 8,
        out_specs=(vmem,) * 6,
        scratch_shapes=[
            pltpu.SMEM((blocks,), jnp.int32),
            pltpu.VMEM((1, 128), jnp.int32),
            pltpu.VMEM((count, 1, 128), jnp.int32),
            pltpu.VMEM((count, 1, 128), jnp.int32),
            pltpu.SMEM((count, 1, 128), jnp.int32),
            pltpu.VMEM((FIELDS, blocks, rows * 128), f32),
            pltpu.VMEM((blocks * rows, 128), f32),
            pltpu.VMEM((FIELDS, blocks, rows, 128), f32),
            *per_field,
            *per_field,
            pltpu.VMEM((8, tracers), f32),
            pltpu.VMEM((1, tracers), jnp.int32),
            pltpu.VMEM((1, tracers), jnp.int32),
            pltpu.VMEM((blocks, 4, 128), f32),
            pltpu.VMEM((count, 4, 128), f32),
            pltpu.VMEM((count, 4, 128), f32),
            pltpu.VMEM((4 * LZ, 128), f32),
            pltpu.VMEM((rows * LZ, 128), f32),
            pltpu.VMEM((nx, ny, nz), f32),
            pltpu.VMEM((4, nx + 2, ny, nz), f32),
            pltpu.VMEM((4, nx + 2, ny, nz), f32),
            pltpu.VMEM((2, 4, nx, nz), f32),
            pltpu.VMEM((2, 4, nx, nz), f32),
            pltpu.VMEM((SWEEPS, 2, 4, nx, nz), f32),
            pltpu.VMEM((2, nx, nz), f32),
            dma((FIELDS + 3,)),
            dma((2,)),
            dma((FIELDS,)),
            dma((FIELDS,)),
            dma((2,)),
            dma((4,)),
            dma((4,)),
            dma((SWEEPS, 4)),
            dma((SWEEPS, 4)),
            dma(()),
        ],
        compiler_params=pltpu.CompilerParams(
            collective_id=1,
            has_side_effects=True,
            vmem_limit_bytes=(24 if count <= 32 else 52) * 1024 * 1024,
        ),
    )(*pinned)


def last_kernel(
    pad_ref, edge_ref, eta_ref, eta_edge_ref, heat_ref, mean_ref,
    velocity_ref, pressure_ref, heat_out_ref, mean_out_ref, fresh, sems, *, parts,
):
    nx = heat_ref.shape[0]
    thick = nx // parts
    copies = [
        pltpu.make_async_copy(heat_ref, heat_out_ref, sems.at[2 * parts]),
        pltpu.make_async_copy(mean_ref, mean_out_ref, sems.at[2 * parts + 1]),
    ]
    for copy in copies:
        copy.start()
    for part in range(parts):

        def slab(x, carry):
            moved = relax_slab(x, eta_ref, eta_edge_ref, pad_ref, edge_ref, heat_ref)
            for k in range(4):
                fresh[k, x] = moved[k]
            return carry

        lax.fori_loop(part * thick, (part + 1) * thick, slab, 0)
        at = pl.ds(part * thick, thick)
        copies.append(
            pltpu.make_async_copy(
                fresh.at[pl.ds(0, 3), at], velocity_ref.at[:, at], sems.at[2 * part]
            )
        )
        copies.append(
            pltpu.make_async_copy(fresh.at[3, at], pressure_ref.at[at], sems.at[2 * part + 1])
        )
        for copy in copies[-2:]:
            copy.start()
    for copy in copies:
        copy.wait()


def last_sweep(pad, edge, eta, eta_edge, heat, means):
    nx, ny, nz = heat.shape
    parts = 4
    vmem = pl.BlockSpec(memory_space=pltpu.VMEM)
    hbm = pl.BlockSpec(memory_space=pltpu.HBM)
    return pl.pallas_call(
        functools.partial(last_kernel, parts=parts),
        out_shape=(
            jax.ShapeDtypeStruct((3, nx, ny, nz), jnp.float32),
            jax.ShapeDtypeStruct((nx, ny, nz), jnp.float32),
            jax.ShapeDtypeStruct(heat.shape, jnp.float32),
            jax.ShapeDtypeStruct(means.shape, jnp.float32),
        ),
        in_specs=[vmem] * 6,
        out_specs=(hbm,) * 4,
        scratch_shapes=[
            pltpu.VMEM((4, nx, ny, nz), jnp.float32),
            pltpu.SemaphoreType.DMA((2 * parts + 2,)),
        ],
        compiler_params=pltpu.CompilerParams(vmem_limit_bytes=16 * 1024 * 1024),
    )(pad, edge, eta, eta_edge, heat, means)


def per_device(
    tile_flow_speed,
    tile_stress_mean,
    tile_heat_state,
    tile_drag_coefficient,
    marker_attributes,
    marker_holding_tile,
    marker_voxel_number,
    prior_slot_of_tile,
):
    tracers = marker_attributes.shape[1]
    pad, edge, eta, eta_edge, heat, means = migrate(
        prior_slot_of_tile,
        tile_flow_speed.transpose(1, 0, 2),
        tile_stress_mean,
        tile_heat_state,
        tile_drag_coefficient,
        marker_attributes,
        marker_holding_tile.reshape(1, tracers),
        marker_voxel_number.reshape(1, tracers),
    )
    return last_sweep(pad, edge, eta, eta_edge, heat, means)


def solution(mesh):
    in_specs = (
        P(("wide", "narrow"), None, None),
        P(("wide", "narrow"), None),
        P(("wide", "narrow"), None),
        P(("wide", "narrow"), None),
        P(None, ("wide", "narrow")),
        P(("wide", "narrow")),
        P(("wide", "narrow")),
        P(("wide", "narrow")),
    )
    out_specs = (
        P(None, "wide", "narrow", None),
        P("wide", "narrow", None),
        P("wide", "narrow", None),
        P(None, "wide", "narrow", None),
    )
    return jax.shard_map(
        per_device, mesh=mesh, in_specs=in_specs, out_specs=out_specs, check_vma=False
    )
```

```python
import functools

import jax
import jax.numpy as jnp
from jax import lax
from jax.experimental import pallas as pl
from jax.experimental.pallas import tpu as pltpu
from jax.sharding import PartitionSpec as P

BS = 16
LX = 1
LY = 2
LZ = 8
SWEEPS = 3
BINS = 64
FIELDS = 6
AHEAD = 3
PITCH = 40
FIRST = 8

MIX_WEIGHTS = (0.3, -0.25, 0.2, -0.15, 0.35, -0.3, 0.25, -0.2)
RELAX_WEIGHT = 0.7
PRESSURE_WEIGHT = 0.3
HEAT_FACTOR = 2.0
DENSITY_FACTOR = 4.0
MESH = pl.DeviceIdType.MESH


def swap_groups(x):
    row = lax.broadcasted_iota(jnp.int32, x.shape, 1)
    group = lax.broadcasted_iota(jnp.int32, x.shape, 2) // BS
    for bit in (1, 2, 4):
        row_set = (row & bit) != 0
        group_set = (group & bit) != 0
        from_above = pltpu.roll(pltpu.roll(x, 8 - bit, 1), BS * bit, 2)
        from_below = pltpu.roll(pltpu.roll(x, bit, 1), 8 * BS - BS * bit, 2)
        x = jnp.where(
            row_set == group_set, x, jnp.where(group_set, from_above, from_below)
        )
    return x


def bin_sums(base, holder_ref, voxel_ref, attr_ref, blocks, chunk):
    props, tracers = attr_ref.shape
    total_bins = blocks * BINS
    bin_ids = lax.broadcasted_iota(jnp.int32, (total_bins, chunk), 0)

    def step(turn, sums):
        at = pl.ds(pl.multiple_of(turn * chunk, chunk), chunk)
        voxel = voxel_ref[:, at]
        key = (
            (holder_ref[:, at] - base) * BINS
            + (voxel >> 10) * 16
            + ((voxel >> 6) & 3) * 4
            + ((voxel >> 2) & 3)
        )
        table = jnp.where(bin_ids == key, 1.0, 0.0).astype(jnp.bfloat16)
        values = attr_ref[:, at]
        high = values.astype(jnp.bfloat16)
        rest = values - high.astype(jnp.float32)
        middle = rest.astype(jnp.bfloat16)
        low = (rest - middle.astype(jnp.float32)).astype(jnp.bfloat16)
        ones = jnp.ones((props, chunk), jnp.bfloat16)
        rows = jnp.concatenate([high, middle, low, ones], axis=0)
        return sums + lax.dot_general(
            rows, table, (((1,), (1,)), ((), ())), preferred_element_type=jnp.float32
        )

    sums = lax.fori_loop(
        0, tracers // chunk, step, jnp.zeros((4 * props, total_bins), jnp.float32)
    )
    total = sums[:props] + sums[props : 2 * props] + sums[2 * props : 3 * props]
    return total / jnp.maximum(sums[3 * props :], 1.0)


def at_ends(shape):
    column = lax.broadcasted_iota(jnp.int32, shape, 1)
    return column == 0, column == shape[1] - 1


def z_pair(here):
    low_end, high_end = at_ends(here.shape)
    nz = here.shape[1]
    return (
        jnp.where(high_end, 0.0, pltpu.roll(here, nz - 1, 1)),
        jnp.where(low_end, 0.0, pltpu.roll(here, 1, 1)),
    )


def factors(x, eta_ref, heat_ref, side_ref, rest_ref):
    ny = heat_ref.shape[1]
    base = pl.multiple_of((x + 1) * PITCH + FIRST, 8)
    here = eta_ref[pl.ds(base, ny), :]
    around = [
        eta_ref[pl.ds(base + off, ny), :] for off in (PITCH, -PITCH, 1, -1)
    ] + list(z_pair(here))
    face = [0.5 * (here + other) for other in around]
    diagonal = face[0]
    for m in range(1, 6):
        diagonal = diagonal + face[m]
    scale = RELAX_WEIGHT / diagonal
    low_end, high_end = at_ends(here.shape)
    for m in range(6):
        value = face[m] * scale
        if m == 4:
            value = jnp.where(high_end, 0.0, value)
        elif m == 5:
            value = jnp.where(low_end, 0.0, value)
        side_ref[m, x] = value
    rest_ref[0, x] = 0.5 * scale
    rest_ref[1, x] = (0.5 * PRESSURE_WEIGHT) * here
    rest_ref[2, x] = scale * (DENSITY_FACTOR * heat_ref[x])


def relax(x, first, rows, pad, side_ref, rest_ref):
    base = (x + 1) * PITCH + FIRST + first
    nz = pad.shape[2]
    own = pl.ds(first, rows)

    def value(k, off=0):
        return pad[k, pl.ds(base + off, rows), :]

    side = [side_ref[m, x, own, :] for m in range(6)]
    half_scale, squeeze, lift = (rest_ref[m, x, own, :] for m in range(3))
    press = value(3)
    press_up_z, press_down_z = z_pair(press)
    drops = (
        value(3, PITCH) - value(3, -PITCH),
        value(3, 1) - value(3, -1),
        press_up_z - press_down_z,
    )
    moved = []
    divergence = None
    for k in range(3):
        here = value(k)
        if k == 2:
            up_z, down_z = z_pair(here)
        else:
            up_z, down_z = pltpu.roll(here, nz - 1, 1), pltpu.roll(here, 1, 1)
        near = (
            value(k, PITCH), value(k, -PITCH), value(k, 1), value(k, -1), up_z, down_z,
        )
        fresh = (1.0 - RELAX_WEIGHT) * here - half_scale * drops[k]
        for m in range(6):
            fresh = fresh + side[m] * near[m]
        if k == 2:
            fresh = fresh + lift
        moved.append(fresh)
        flux = near[2 * k] - near[2 * k + 1]
        divergence = flux if divergence is None else divergence + flux
    moved.append(press - squeeze * divergence)
    return moved


def migrate_kernel(
    places_ref, flow_ref, stress_ref, warm_ref, drag_ref, attr_ref, holder_ref, voxel_ref,
    pad_ref, inner_ref, side_ref, rest_ref, heat_ref, mean_ref,
    slot_ref, row_ref, table, table_smem, raw, lined, mine, stage_0, stage_1, stage_2, stage_3, stage_4, stage_5,
    land_0, land_1, land_2, land_3, land_4, land_5,
    attr, holder, voxel, mean_mine, mean_stage, mean_land, mean_held, held, drag_grid,
    pad_0, pad_1, eta, edge_in, edge_out, eta_in, eta_out,
    raw_sems, table_sems, data_send, data_recv, mean_sems,
    eta_send, eta_recv, halo_send, halo_recv, small_sem,
    *, wide_count, narrow_count,
):
    count = wide_count * narrow_count
    wide, narrow = lax.axis_index("wide"), lax.axis_index("narrow")
    me = wide * narrow_count + narrow
    blocks = raw.shape[1]
    nx, ny, nz = heat_ref.shape
    stages = (stage_0, stage_1, stage_2, stage_3, stage_4, stage_5)
    lands = (land_0, land_1, land_2, land_3, land_4, land_5)
    pads = (pad_0, pad_1, pad_ref)

    to_slots = pltpu.make_async_copy(places_ref, slot_ref, small_sem)
    to_slots.start()
    sources = (
        warm_ref, drag_ref, flow_ref.at[0], flow_ref.at[1], flow_ref.at[2], stress_ref,
    )
    loads = [
        pltpu.make_async_copy(source, raw.at[f], raw_sems.at[f]) for f, source in enumerate(sources)
    ]
    loads.append(pltpu.make_async_copy(attr_ref, attr, raw_sems.at[FIELDS]))
    loads.append(pltpu.make_async_copy(holder_ref, holder, raw_sems.at[FIELDS + 1]))
    loads.append(pltpu.make_async_copy(voxel_ref, voxel, raw_sems.at[FIELDS + 2]))
    for load in loads:
        load.start()

    def others(act):
        near = [lax.rem(narrow + b, narrow_count) for b in range(narrow_count)]
        for b in range(1, narrow_count):
            act(wide, near[b])

        def row(a, carry):
            far = lax.rem(wide + a, wide_count)
            for b in range(narrow_count):
                act(far, near[b])
            return carry

        lax.fori_loop(1, wide_count, row, 0)

    barrier = pltpu.get_barrier_semaphore()
    others(
        lambda w, n: pl.semaphore_signal(
            barrier, inc=1, device_id=(w, n), device_id_type=MESH
        )
    )
    to_slots.wait()
    lane = lax.broadcasted_iota(jnp.int32, (1, 128), 1)
    places = jnp.zeros((1, 128), jnp.int32)
    my_own = jnp.int32(0)
    for r in range(blocks):
        owner = lax.div(slot_ref[r], blocks)
        local = slot_ref[r] - owner * blocks
        places = jnp.where(lane == owner, local, places)
        my_own = jnp.where(owner == me, local, my_own)
    row_ref[...] = places
    table[me] = places
    pl.semaphore_wait(barrier, count - 1)

    def send_row(w, n):
        pltpu.make_async_remote_copy(
            src_ref=row_ref,
            dst_ref=table.at[me],
            send_sem=table_sems.at[0],
            recv_sem=table_sems.at[1],
            device_id=(w, n),
            device_id_type=MESH,
        ).start()

    others(send_row)

    for pad in pads:
        pad[...] = jnp.zeros(pad.shape, jnp.float32)
    eta[...] = jnp.zeros(eta.shape, jnp.float32)
    edge_in[...] = jnp.zeros(edge_in.shape, jnp.float32)
    eta_in[...] = jnp.zeros(eta_in.shape, jnp.float32)

    def whole(ref, send_sem, recv_sem):
        part = ref.at[pl.ds(0, count - 1)]
        return pltpu.make_async_remote_copy(
            src_ref=part,
            dst_ref=part,
            send_sem=send_sem,
            recv_sem=recv_sem,
            device_id=(wide, narrow),
            device_id_type=MESH,
        )

    rows = BS * BS * BS // 128
    for f in range(FIELDS):
        loads[f].wait()
        for g in range(blocks // 8):
            for j in range(rows):
                lined[pl.ds(g * 8 * rows + j, 8, stride=rows), :] = raw[
                    f, g * 8 : g * 8 + 8, j * 128 : j * 128 + 128
                ]
        mine[f] = lined[...].reshape(blocks, rows, 128)

    whole(table, table_sems.at[0], table_sems.at[1]).wait_recv()
    to_scalar = pltpu.make_async_copy(table, table_smem, small_sem)
    to_scalar.start()
    to_scalar.wait()

    def wanted(d):
        return table_smem[d, 0, me]

    def send_field(f):
        def send(w, n):
            d = w * narrow_count + n
            stages[f][d] = mine[f, wanted(d)]
            pltpu.make_async_remote_copy(
                src_ref=stages[f].at[d],
                dst_ref=lands[f].at[me],
                send_sem=data_send.at[f],
                recv_sem=data_recv.at[f],
                device_id=(w, n),
                device_id_type=MESH,
            ).start()

        others(send)
        lands[f][me] = mine[f, my_own]

    for f in range(AHEAD):
        send_field(f)

    for load in loads[FIELDS:]:
        load.wait()
    tracers = attr.shape[1]
    chunk = 1024 if tracers % 1024 == 0 else tracers
    means = bin_sums(me * blocks, holder, voxel, attr, blocks, chunk)
    left = lax.broadcasted_iota(jnp.int32, (8, 128), 1) < BINS
    for q in range(blocks // 2):
        pair = means[:, q * 128 : q * 128 + 128]
        across = pltpu.roll(pair, BINS, 1)
        below = pltpu.roll(pair, 4, 0)
        both = pltpu.roll(across, 4, 0)
        mean_mine[2 * q] = jnp.where(left, pair, both)[:4]
        mean_mine[2 * q + 1] = jnp.where(left, across, below)[:4]

    def send_mean(w, n):
        d = w * narrow_count + n
        mean_stage[d] = mean_mine[wanted(d)]
        pltpu.make_async_remote_copy(
            src_ref=mean_stage.at[d],
            dst_ref=mean_land.at[me],
            send_sem=mean_sems.at[0],
            recv_sem=mean_sems.at[1],
            device_id=(w, n),
            device_id_type=MESH,
        ).start()

    others(send_mean)
    mean_land[me] = mean_mine[my_own]

    def source_of(y, z):
        return lax.div(slot_ref[y * LZ + z], blocks)

    def grid_part(f, y):
        for z in range(LZ):
            held[pl.ds(z, rows, stride=LZ), :] = lands[f][source_of(y, z)]
        return swap_groups(held[...].reshape(rows, LZ, 128)).reshape(BS, BS, 128)

    exists = (wide > 0, wide < wide_count - 1, narrow > 0, narrow < narrow_count - 1)
    partner = ((wide - 1, narrow), (wide + 1, narrow), (wide, narrow - 1), (wide, narrow + 1))

    def slab_rows(x):
        return pl.ds(x * PITCH + FIRST, ny)

    def edge_rows(side):
        return pl.ds(PITCH + FIRST + (0 if side == 2 else ny - 1), nx, stride=PITCH)

    def beside_rows(side):
        return pl.ds(PITCH + FIRST + (-1 if side == 2 else ny), nx, stride=PITCH)

    def eta_copy(side, arriving=False):
        if side < 2:
            source = eta.at[slab_rows(1 if side == 0 else nx)]
            target = eta.at[slab_rows(nx + 1 if side == 0 else 0)]
            mine_at = eta.at[slab_rows(0 if side == 0 else nx + 1)]
        else:
            source = eta_out.at[side - 2]
            target = eta_in.at[3 - side]
            mine_at = eta_in.at[side - 2]
        return pltpu.make_async_remote_copy(
            src_ref=mine_at if arriving else source,
            dst_ref=mine_at if arriving else target,
            send_sem=eta_send.at[side],
            recv_sem=eta_recv.at[side if arriving else side ^ 1],
            device_id=partner[side],
            device_id_type=MESH,
        )

    groups = ((0, 0, 1), (0, 1, 1), (0, 2, 1), (0, 3, 1), (1, 0, 4), (2, 0, 4))

    def halo_copy(group, side, arriving=False):
        turn, first, fields = groups[group]
        ks = pl.ds(first, fields)
        pad = pads[turn]
        if side < 2:
            source = pad.at[ks, slab_rows(1 if side == 0 else nx)]
            target = pad.at[ks, slab_rows(nx + 1 if side == 0 else 0)]
            mine_at = pad.at[ks, slab_rows(0 if side == 0 else nx + 1)]
        else:
            source = edge_out.at[turn, side - 2, ks]
            target = edge_in.at[turn, 3 - side, ks]
            mine_at = edge_in.at[turn, side - 2, ks]
        return pltpu.make_async_remote_copy(
            src_ref=mine_at if arriving else source,
            dst_ref=mine_at if arriving else target,
            send_sem=halo_send.at[group, side],
            recv_sem=halo_recv.at[group, side if arriving else side ^ 1],
            device_id=partner[side],
            device_id_type=MESH,
        )

    def each_side(act, sides=range(4)):
        for side in sides:

            @pl.when(exists[side])
            def _(side=side):
                act(side)

    def send_halo(group):
        turn, first, fields = groups[group]
        each_side(lambda side: halo_copy(group, side).start(), range(2))
        for k in range(first, first + fields):
            for side in (2, 3):
                edge_out[turn, side - 2, k] = pads[turn][k, edge_rows(side), :]
        each_side(lambda side: halo_copy(group, side).start(), range(2, 4))

    def take_halo(group):
        turn, first, fields = groups[group]
        each_side(lambda side: halo_copy(group, side, True).wait_recv())
        for k in range(first, first + fields):
            for side in (2, 3):
                pads[turn][k, beside_rows(side), :] = edge_in[turn, side - 2, k]

    def viscosity():
        whole(mean_land, mean_sems.at[0], mean_sems.at[1]).wait_recv()
        expand = (
            lax.broadcasted_iota(jnp.int32, (LZ, 32), 0)
            == lax.broadcasted_iota(jnp.int32, (LZ, 32), 1) // 4
        ).astype(jnp.float32)
        same = (
            lax.broadcasted_iota(jnp.int32, (128, 32), 0) % 4
            == lax.broadcasted_iota(jnp.int32, (128, 32), 1) % 4
        )
        gather = (
            lax.broadcasted_iota(jnp.int32, (32, 128), 0)
            == lax.broadcasted_iota(jnp.int32, (32, 128), 1) // 4
        ).astype(jnp.float32)
        for y in range(LY):
            for z in range(LZ):
                mean_held[pl.ds(z, 4, stride=LZ), :] = mean_land[source_of(y, z)]
            for p in range(4):
                tall = jnp.dot(
                    mean_held[p * LZ : p * LZ + LZ].T, expand,
                    precision=lax.Precision.HIGHEST, preferred_element_type=jnp.float32,
                )
                cells = jnp.dot(
                    gather, jnp.where(same, tall, 0.0),
                    precision=lax.Precision.HIGHEST, preferred_element_type=jnp.float32,
                )
                for half in range(2):
                    for layer in range(4):
                        at = half * 16 + layer * 4
                        mean_ref[half * 4 + p, layer, y * 4 : y * 4 + 4, :] = cells[at : at + 4]
        for layer in range(4):
            mixture = MIX_WEIGHTS[0] * mean_ref[0, layer]
            for p in range(1, len(MIX_WEIGHTS)):
                mixture = mixture + MIX_WEIGHTS[p] * mean_ref[p, layer]
            wide_mix = jnp.dot(
                mixture, gather,
                precision=lax.Precision.HIGHEST, preferred_element_type=jnp.float32,
            )
            spread = jnp.concatenate(
                [jnp.broadcast_to(wide_mix[j : j + 1], (4, 128)) for j in range(LY * 4)], axis=0
            )
            for x in range(layer * 4, layer * 4 + 4):
                eta[slab_rows(x + 1), :] = drag_grid[x] * jnp.exp(
                    HEAT_FACTOR * (0.5 - heat_ref[x]) + spread
                )
        for side in (2, 3):
            eta_out[side - 2] = eta[edge_rows(side), :]
        each_side(lambda side: eta_copy(side).start())

    def take_eta():
        each_side(lambda side: eta_copy(side, True).wait_recv())
        for side in (2, 3):
            eta[beside_rows(side), :] = eta_in[side - 2]

        def slab(x, carry):
            factors(x, eta, heat_ref, side_ref, rest_ref)
            return carry

        lax.fori_loop(0, nx, slab, 0)

    for f in range(FIELDS):
        whole(lands[f], data_send.at[f], data_recv.at[f]).wait_recv()
        if f + AHEAD < FIELDS:
            send_field(f + AHEAD)
        for y in range(LY):
            at = slice(y * BS, (y + 1) * BS)
            part = grid_part(f, y)
            if f == 0:
                heat_ref[:, at, :] = part
            elif f == 1:
                drag_grid[:, at, :] = part
            else:
                for x in range(nx):
                    pad_0[f - 2, pl.ds((x + 1) * PITCH + FIRST + y * BS, BS), :] = part[x]
        if f == 1:
            viscosity()
        elif f > 1:
            send_halo(f - 2)
        if f == 3:
            take_eta()

    def sweep(turn, first_x, end_x, first, rows):
        def slab(x, carry):
            moved = relax(x, first, rows, pads[turn], side_ref, rest_ref)
            for k in range(4):
                if turn == SWEEPS - 1:
                    inner_ref[k, x - 1] = moved[k]
                else:
                    pads[turn + 1][k, pl.ds((x + 1) * PITCH + FIRST + first, rows), :] = moved[k]
            return carry

        lax.fori_loop(first_x, end_x, slab, 0)

    for turn in range(SWEEPS):
        if turn > 0:
            send_halo(3 + turn)
        sweep(turn, 1, nx - 1, 8, ny - 16)
        for group in range(4) if turn == 0 else (3 + turn,):
            take_halo(group)
        if turn < SWEEPS - 1:
            sweep(turn, 0, 1, 0, ny)
            sweep(turn, nx - 1, nx, 0, ny)
            sweep(turn, 1, nx - 1, 0, 8)
            sweep(turn, 1, nx - 1, ny - 8, 8)

    whole(table, table_sems.at[0], table_sems.at[1]).wait_send()
    whole(mean_land, mean_sems.at[0], mean_sems.at[1]).wait_send()
    for f in range(FIELDS):
        whole(lands[f], data_send.at[f], data_recv.at[f]).wait_send()
    each_side(lambda side: eta_copy(side).wait_send())
    for group in range(len(groups)):
        each_side(lambda side: halo_copy(group, side).wait_send())


def migrate(slots, flow, stress, heat, drag, attributes, holder, voxel):
    wide_count, narrow_count = lax.axis_size("wide"), lax.axis_size("narrow")
    count = wide_count * narrow_count
    blocks = slots.shape[0]
    tracers = attributes.shape[1]
    nx, ny, nz = LX * BS, LY * BS, LZ * BS
    rows = BS * BS * BS // 128
    pad_rows = (nx + 2) * PITCH + 8
    vmem = pl.BlockSpec(memory_space=pltpu.VMEM)
    hbm = pl.BlockSpec(memory_space=pltpu.HBM)
    f32 = jnp.float32
    per_field = [pltpu.VMEM((count, rows, 128), f32)] * FIELDS
    dma = pltpu.SemaphoreType.DMA
    pinned = [
        pltpu.with_memory_space_constraint(array, pltpu.HBM)
        for array in (slots, flow, stress, heat, drag, attributes, holder, voxel)
    ]
    return pl.pallas_call(
        functools.partial(migrate_kernel, wide_count=wide_count, narrow_count=narrow_count),
        out_shape=(
            jax.ShapeDtypeStruct((4, pad_rows, nz), f32),
            jax.ShapeDtypeStruct((4, nx - 2, ny - 16, nz), f32),
            jax.ShapeDtypeStruct((6, nx, ny, nz), f32),
            jax.ShapeDtypeStruct((3, nx, ny, nz), f32),
            jax.ShapeDtypeStruct((nx, ny, nz), f32),
            jax.ShapeDtypeStruct((8, LX * 4, LY * 4, LZ * 4), f32),
        ),
        in_specs=[hbm] * 8,
        out_specs=(vmem,) * 6,
        scratch_shapes=[
            pltpu.SMEM((blocks,), jnp.int32),
            pltpu.VMEM((1, 128), jnp.int32),
            pltpu.VMEM((count, 1, 128), jnp.int32),
            pltpu.SMEM((count, 1, 128), jnp.int32),
            pltpu.VMEM((FIELDS, blocks, rows * 128), f32),
            pltpu.VMEM((blocks * rows, 128), f32),
            pltpu.VMEM((FIELDS, blocks, rows, 128), f32),
            *per_field,
            *per_field,
            pltpu.VMEM((8, tracers), f32),
            pltpu.VMEM((1, tracers), jnp.int32),
            pltpu.VMEM((1, tracers), jnp.int32),
            pltpu.VMEM((blocks, 4, 128), f32),
            pltpu.VMEM((count, 4, 128), f32),
            pltpu.VMEM((count, 4, 128), f32),
            pltpu.VMEM((4 * LZ, 128), f32),
            pltpu.VMEM((rows * LZ, 128), f32),
            pltpu.VMEM((nx, ny, nz), f32),
            pltpu.VMEM((4, pad_rows, nz), f32),
            pltpu.VMEM((4, pad_rows, nz), f32),
            pltpu.VMEM((pad_rows, nz), f32),
            pltpu.VMEM((SWEEPS, 2, 4, nx, nz), f32),
            pltpu.VMEM((SWEEPS, 2, 4, nx, nz), f32),
            pltpu.VMEM((2, nx, nz), f32),
            pltpu.VMEM((2, nx, nz), f32),
            dma((FIELDS + 3,)),
            dma((2,)),
            dma((FIELDS,)),
            dma((FIELDS,)),
            dma((2,)),
            dma((4,)),
            dma((4,)),
            dma((SWEEPS + 3, 4)),
            dma((SWEEPS + 3, 4)),
            dma(()),
        ],
        compiler_params=pltpu.CompilerParams(
            collective_id=1,
            has_side_effects=True,
            vmem_limit_bytes=(24 if count <= 32 else 52) * 1024 * 1024,
        ),
    )(*pinned)


def last_kernel(
    pad_ref, inner_ref, side_ref, rest_ref, heat_ref, mean_ref,
    velocity_ref, pressure_ref, heat_out_ref, mean_out_ref, fresh, sems,
):
    nx, ny, nz = heat_ref.shape
    copies = []

    def send(source, target):
        copies.append(pltpu.make_async_copy(source, target, sems.at[len(copies)]))
        copies[-1].start()

    def send_fresh(xs, ys):
        send(fresh.at[pl.ds(0, 3), xs, ys], velocity_ref.at[:, xs, ys])
        send(fresh.at[3, xs, ys], pressure_ref.at[xs, ys])

    send(heat_ref, heat_out_ref)
    send(mean_ref, mean_out_ref)
    middle, centre = pl.ds(1, nx - 2), pl.ds(8, ny - 16)
    send(inner_ref.at[pl.ds(0, 3)], velocity_ref.at[:, middle, centre])
    send(inner_ref.at[3], pressure_ref.at[middle, centre])

    def sweep(first_x, end_x, first, rows):
        def slab(x, carry):
            moved = relax(x, first, rows, pad_ref, side_ref, rest_ref)
            for k in range(4):
                fresh[k, x, pl.ds(first, rows), :] = moved[k]
            return carry

        lax.fori_loop(first_x, end_x, slab, 0)

    for first in (0, ny - 8):
        sweep(1, nx - 1, first, 8)
        send_fresh(middle, pl.ds(first, 8))
    for x in (0, nx - 1):
        sweep(x, x + 1, 0, ny)
        send_fresh(pl.ds(x, 1), pl.ds(0, ny))
    for copy in copies:
        copy.wait()


def last_sweep(pad, inner, side, rest, heat, means):
    nx, ny, nz = heat.shape
    vmem = pl.BlockSpec(memory_space=pltpu.VMEM)
    hbm = pl.BlockSpec(memory_space=pltpu.HBM)
    return pl.pallas_call(
        last_kernel,
        out_shape=(
            jax.ShapeDtypeStruct((3, nx, ny, nz), jnp.float32),
            jax.ShapeDtypeStruct((nx, ny, nz), jnp.float32),
            jax.ShapeDtypeStruct(heat.shape, jnp.float32),
            jax.ShapeDtypeStruct(means.shape, jnp.float32),
        ),
        in_specs=[vmem] * 6,
        out_specs=(hbm,) * 4,
        scratch_shapes=[
            pltpu.VMEM((4, nx, ny, nz), jnp.float32),
            pltpu.SemaphoreType.DMA((12,)),
        ],
        compiler_params=pltpu.CompilerParams(vmem_limit_bytes=16 * 1024 * 1024),
    )(pad, inner, side, rest, heat, means)


def per_device(
    tile_flow_speed,
    tile_stress_mean,
    tile_heat_state,
    tile_drag_coefficient,
    marker_attributes,
    marker_holding_tile,
    marker_voxel_number,
    prior_slot_of_tile,
):
    tracers = marker_attributes.shape[1]
    results = migrate(
        prior_slot_of_tile,
        tile_flow_speed.transpose(1, 0, 2),
        tile_stress_mean,
        tile_heat_state,
        tile_drag_coefficient,
        marker_attributes,
        marker_holding_tile.reshape(1, tracers),
        marker_voxel_number.reshape(1, tracers),
    )
    return last_sweep(*results)


def solution(mesh):
    in_specs = (
        P(("wide", "narrow"), None, None),
        P(("wide", "narrow"), None),
        P(("wide", "narrow"), None),
        P(("wide", "narrow"), None),
        P(None, ("wide", "narrow")),
        P(("wide", "narrow")),
        P(("wide", "narrow")),
        P(("wide", "narrow")),
    )
    out_specs = (
        P(None, "wide", "narrow", None),
        P("wide", "narrow", None),
        P("wide", "narrow", None),
        P(None, "wide", "narrow", None),
    )
    return jax.shard_map(
        per_device, mesh=mesh, in_specs=in_specs, out_specs=out_specs, check_vma=False
    )
```

```python
import functools

import jax
import jax.numpy as jnp
from jax import lax
from jax.experimental import pallas as pl
from jax.experimental.pallas import tpu as pltpu
from jax.sharding import PartitionSpec as P

BS = 16
LX = 1
LY = 2
LZ = 8
SWEEPS = 3
BINS = 64
FIELDS = 6
AHEAD = 3
PITCH = 40
FIRST = 8
INNER = 14
OUTER = 14

MIX_WEIGHTS = (0.3, -0.25, 0.2, -0.15, 0.35, -0.3, 0.25, -0.2)
RELAX_WEIGHT = 0.7
PRESSURE_WEIGHT = 0.3
HEAT_FACTOR = 2.0
DENSITY_FACTOR = 4.0
MESH = pl.DeviceIdType.MESH


def swap_groups(x):
    row = lax.broadcasted_iota(jnp.int32, x.shape, 1)
    group = lax.broadcasted_iota(jnp.int32, x.shape, 2) // BS
    for bit in (1, 2, 4):
        row_set = (row & bit) != 0
        group_set = (group & bit) != 0
        from_above = pltpu.roll(pltpu.roll(x, 8 - bit, 1), BS * bit, 2)
        from_below = pltpu.roll(pltpu.roll(x, bit, 1), 8 * BS - BS * bit, 2)
        x = jnp.where(
            row_set == group_set, x, jnp.where(group_set, from_above, from_below)
        )
    return x


def bin_sums(base, holder_ref, voxel_ref, attr_ref, blocks, chunk):
    props, tracers = attr_ref.shape
    total_bins = blocks * BINS
    bin_ids = lax.broadcasted_iota(jnp.int32, (total_bins, chunk), 0)

    def step(turn, sums):
        at = pl.ds(pl.multiple_of(turn * chunk, chunk), chunk)
        voxel = voxel_ref[:, at]
        key = (
            (holder_ref[:, at] - base) * BINS
            + (voxel >> 10) * 16
            + ((voxel >> 6) & 3) * 4
            + ((voxel >> 2) & 3)
        )
        table = jnp.where(bin_ids == key, 1.0, 0.0).astype(jnp.bfloat16)
        values = attr_ref[:, at]
        high = values.astype(jnp.bfloat16)
        rest = values - high.astype(jnp.float32)
        middle = rest.astype(jnp.bfloat16)
        low = (rest - middle.astype(jnp.float32)).astype(jnp.bfloat16)
        ones = jnp.ones((props, chunk), jnp.bfloat16)
        rows = jnp.concatenate([high, middle, low, ones], axis=0)
        return sums + lax.dot_general(
            rows, table, (((1,), (1,)), ((), ())), preferred_element_type=jnp.float32
        )

    sums = lax.fori_loop(
        0, tracers // chunk, step, jnp.zeros((4 * props, total_bins), jnp.float32)
    )
    total = sums[:props] + sums[props : 2 * props] + sums[2 * props : 3 * props]
    return total / jnp.maximum(sums[3 * props :], 1.0)


def at_ends(shape):
    column = lax.broadcasted_iota(jnp.int32, shape, 1)
    return column == 0, column == shape[1] - 1


def z_pair(here):
    low_end, high_end = at_ends(here.shape)
    nz = here.shape[1]
    return (
        jnp.where(high_end, 0.0, pltpu.roll(here, nz - 1, 1)),
        jnp.where(low_end, 0.0, pltpu.roll(here, 1, 1)),
    )


def factors(x, eta_ref, heat_ref, side_ref, rest_ref):
    ny = heat_ref.shape[1]
    base = pl.multiple_of((x + 1) * PITCH + FIRST, 8)
    here = eta_ref[pl.ds(base, ny), :]
    around = [
        eta_ref[pl.ds(base + off, ny), :] for off in (PITCH, -PITCH, 1, -1)
    ] + list(z_pair(here))
    face = [0.5 * (here + other) for other in around]
    diagonal = face[0]
    for m in range(1, 6):
        diagonal = diagonal + face[m]
    scale = RELAX_WEIGHT / diagonal
    low_end, high_end = at_ends(here.shape)
    for m in range(6):
        value = face[m] * scale
        if m == 4:
            value = jnp.where(high_end, 0.0, value)
        elif m == 5:
            value = jnp.where(low_end, 0.0, value)
        side_ref[m, x] = value
    rest_ref[0, x] = 0.5 * scale
    rest_ref[1, x] = (0.5 * PRESSURE_WEIGHT) * here
    rest_ref[2, x] = scale * (DENSITY_FACTOR * heat_ref[x])


def relax(x, first, rows, pad, side_ref, rest_ref):
    base = (x + 1) * PITCH + FIRST + first
    nz = pad.shape[2]
    own = pl.ds(first, rows)

    def value(k, off=0):
        return pad[k, pl.ds(base + off, rows), :]

    side = [side_ref[m, x, own, :] for m in range(6)]
    half_scale, squeeze, lift = (rest_ref[m, x, own, :] for m in range(3))
    press = value(3)
    press_up_z, press_down_z = z_pair(press)
    drops = (
        value(3, PITCH) - value(3, -PITCH),
        value(3, 1) - value(3, -1),
        press_up_z - press_down_z,
    )
    moved = []
    divergence = None
    for k in range(3):
        here = value(k)
        if k == 2:
            up_z, down_z = z_pair(here)
        else:
            up_z, down_z = pltpu.roll(here, nz - 1, 1), pltpu.roll(here, 1, 1)
        near = (
            value(k, PITCH), value(k, -PITCH), value(k, 1), value(k, -1), up_z, down_z,
        )
        fresh = (1.0 - RELAX_WEIGHT) * here - half_scale * drops[k]
        for m in range(6):
            fresh = fresh + side[m] * near[m]
        if k == 2:
            fresh = fresh + lift
        moved.append(fresh)
        flux = near[2 * k] - near[2 * k + 1]
        divergence = flux if divergence is None else divergence + flux
    moved.append(press - squeeze * divergence)
    return moved


def migrate_kernel(
    places_ref, flow_ref, stress_ref, warm_ref, drag_ref, attr_ref, holder_ref, voxel_ref,
    pad_ref, inner_ref, side_ref, rest_ref, heat_ref, mean_ref,
    slot_ref, row_ref, table, table_smem, raw, lined, mine, stage_0, stage_1, stage_2, stage_3, stage_4, stage_5,
    land_0, land_1, land_2, land_3, land_4, land_5,
    attr, holder, voxel, mean_mine, mean_stage, mean_land, mean_held, held, drag_grid,
    pad_0, pad_1, eta, edge_in, edge_out, eta_in, eta_out,
    raw_sems, table_sems, data_send, data_recv, mean_sems,
    eta_send, eta_recv, halo_send, halo_recv, small_sem,
    *, wide_count, narrow_count,
):
    count = wide_count * narrow_count
    wide, narrow = lax.axis_index("wide"), lax.axis_index("narrow")
    me = wide * narrow_count + narrow
    blocks = raw.shape[1]
    nx, ny, nz = heat_ref.shape
    stages = (stage_0, stage_1, stage_2, stage_3, stage_4, stage_5)
    lands = (land_0, land_1, land_2, land_3, land_4, land_5)
    pads = (pad_0, pad_1, pad_ref)

    to_slots = pltpu.make_async_copy(places_ref, slot_ref, small_sem)
    to_slots.start()
    sources = (
        warm_ref, drag_ref, flow_ref.at[0], flow_ref.at[1], flow_ref.at[2], stress_ref,
    )
    loads = [
        pltpu.make_async_copy(source, raw.at[f], raw_sems.at[f]) for f, source in enumerate(sources)
    ]
    loads.append(pltpu.make_async_copy(attr_ref, attr, raw_sems.at[FIELDS]))
    loads.append(pltpu.make_async_copy(holder_ref, holder, raw_sems.at[FIELDS + 1]))
    loads.append(pltpu.make_async_copy(voxel_ref, voxel, raw_sems.at[FIELDS + 2]))
    for load in loads:
        load.start()

    def others(act):
        near = [lax.rem(narrow + b, narrow_count) for b in range(narrow_count)]
        for b in range(1, narrow_count):
            act(wide, near[b])

        def row(a, carry):
            far = lax.rem(wide + a, wide_count)
            for b in range(narrow_count):
                act(far, near[b])
            return carry

        lax.fori_loop(1, wide_count, row, 0)

    barrier = pltpu.get_barrier_semaphore()
    others(
        lambda w, n: pl.semaphore_signal(
            barrier, inc=1, device_id=(w, n), device_id_type=MESH
        )
    )
    to_slots.wait()
    lane = lax.broadcasted_iota(jnp.int32, (1, 128), 1)
    places = jnp.zeros((1, 128), jnp.int32)
    my_own = jnp.int32(0)
    for r in range(blocks):
        owner = lax.div(slot_ref[r], blocks)
        local = slot_ref[r] - owner * blocks
        places = jnp.where(lane == owner, local, places)
        my_own = jnp.where(owner == me, local, my_own)
    row_ref[...] = places
    table[me] = places
    pl.semaphore_wait(barrier, count - 1)

    def send_row(w, n):
        pltpu.make_async_remote_copy(
            src_ref=row_ref,
            dst_ref=table.at[me],
            send_sem=table_sems.at[0],
            recv_sem=table_sems.at[1],
            device_id=(w, n),
            device_id_type=MESH,
        ).start()

    others(send_row)

    for pad in pads:
        pad[...] = jnp.zeros(pad.shape, jnp.float32)
    eta[...] = jnp.zeros(eta.shape, jnp.float32)
    edge_in[...] = jnp.zeros(edge_in.shape, jnp.float32)
    eta_in[...] = jnp.zeros(eta_in.shape, jnp.float32)

    def whole(ref, send_sem, recv_sem):
        part = ref.at[pl.ds(0, count - 1)]
        return pltpu.make_async_remote_copy(
            src_ref=part,
            dst_ref=part,
            send_sem=send_sem,
            recv_sem=recv_sem,
            device_id=(wide, narrow),
            device_id_type=MESH,
        )

    rows = BS * BS * BS // 128
    for f in range(FIELDS):
        loads[f].wait()
        for g in range(blocks // 8):
            for j in range(rows):
                lined[pl.ds(g * 8 * rows + j, 8, stride=rows), :] = raw[
                    f, g * 8 : g * 8 + 8, j * 128 : j * 128 + 128
                ]
        mine[f] = lined[...].reshape(blocks, rows, 128)

    whole(table, table_sems.at[0], table_sems.at[1]).wait_recv()
    to_scalar = pltpu.make_async_copy(table, table_smem, small_sem)
    to_scalar.start()
    to_scalar.wait()

    def wanted(d):
        return table_smem[d, 0, me]

    def send_field(f):
        def send(w, n):
            d = w * narrow_count + n
            stages[f][d] = mine[f, wanted(d)]
            pltpu.make_async_remote_copy(
                src_ref=stages[f].at[d],
                dst_ref=lands[f].at[me],
                send_sem=data_send.at[f],
                recv_sem=data_recv.at[f],
                device_id=(w, n),
                device_id_type=MESH,
            ).start()

        others(send)
        lands[f][me] = mine[f, my_own]

    for f in range(AHEAD):
        send_field(f)

    for load in loads[FIELDS:]:
        load.wait()
    tracers = attr.shape[1]
    chunk = 1024 if tracers % 1024 == 0 else tracers
    means = bin_sums(me * blocks, holder, voxel, attr, blocks, chunk)
    left = lax.broadcasted_iota(jnp.int32, (8, 128), 1) < BINS
    for q in range(blocks // 2):
        pair = means[:, q * 128 : q * 128 + 128]
        across = pltpu.roll(pair, BINS, 1)
        below = pltpu.roll(pair, 4, 0)
        both = pltpu.roll(across, 4, 0)
        mean_mine[2 * q] = jnp.where(left, pair, both)[:4]
        mean_mine[2 * q + 1] = jnp.where(left, across, below)[:4]

    def send_mean(w, n):
        d = w * narrow_count + n
        mean_stage[d] = mean_mine[wanted(d)]
        pltpu.make_async_remote_copy(
            src_ref=mean_stage.at[d],
            dst_ref=mean_land.at[me],
            send_sem=mean_sems.at[0],
            recv_sem=mean_sems.at[1],
            device_id=(w, n),
            device_id_type=MESH,
        ).start()

    others(send_mean)
    mean_land[me] = mean_mine[my_own]

    def source_of(y, z):
        return lax.div(slot_ref[y * LZ + z], blocks)

    def grid_part(f, y):
        for z in range(LZ):
            held[pl.ds(z, rows, stride=LZ), :] = lands[f][source_of(y, z)]
        return swap_groups(held[...].reshape(rows, LZ, 128)).reshape(BS, BS, 128)

    exists = (wide > 0, wide < wide_count - 1, narrow > 0, narrow < narrow_count - 1)
    partner = ((wide - 1, narrow), (wide + 1, narrow), (wide, narrow - 1), (wide, narrow + 1))

    def slab_rows(x):
        return pl.ds(x * PITCH + FIRST, ny)

    def edge_rows(side):
        return pl.ds(PITCH + FIRST + (0 if side == 2 else ny - 1), nx, stride=PITCH)

    def beside_rows(side):
        return pl.ds(PITCH + FIRST + (-1 if side == 2 else ny), nx, stride=PITCH)

    def eta_copy(side, arriving=False):
        if side < 2:
            source = eta.at[slab_rows(1 if side == 0 else nx)]
            target = eta.at[slab_rows(nx + 1 if side == 0 else 0)]
            mine_at = eta.at[slab_rows(0 if side == 0 else nx + 1)]
        else:
            source = eta_out.at[side - 2]
            target = eta_in.at[3 - side]
            mine_at = eta_in.at[side - 2]
        return pltpu.make_async_remote_copy(
            src_ref=mine_at if arriving else source,
            dst_ref=mine_at if arriving else target,
            send_sem=eta_send.at[side],
            recv_sem=eta_recv.at[side if arriving else side ^ 1],
            device_id=partner[side],
            device_id_type=MESH,
        )

    groups = ((0, 0, 1), (0, 1, 1), (0, 2, 1), (0, 3, 1), (1, 0, 4), (2, 0, 4))

    def halo_copy(group, side, arriving=False):
        turn, first, fields = groups[group]
        ks = pl.ds(first, fields)
        pad = pads[turn]
        if side < 2:
            source = pad.at[ks, slab_rows(1 if side == 0 else nx)]
            target = pad.at[ks, slab_rows(nx + 1 if side == 0 else 0)]
            mine_at = pad.at[ks, slab_rows(0 if side == 0 else nx + 1)]
        else:
            source = edge_out.at[turn, side - 2, ks]
            target = edge_in.at[turn, 3 - side, ks]
            mine_at = edge_in.at[turn, side - 2, ks]
        return pltpu.make_async_remote_copy(
            src_ref=mine_at if arriving else source,
            dst_ref=mine_at if arriving else target,
            send_sem=halo_send.at[group, side],
            recv_sem=halo_recv.at[group, side if arriving else side ^ 1],
            device_id=partner[side],
            device_id_type=MESH,
        )

    def each_side(act, sides=range(4)):
        for side in sides:

            @pl.when(exists[side])
            def _(side=side):
                act(side)

    def send_halo(group):
        turn, first, fields = groups[group]
        each_side(lambda side: halo_copy(group, side).start(), range(2))
        for k in range(first, first + fields):
            for side in (2, 3):
                edge_out[turn, side - 2, k] = pads[turn][k, edge_rows(side), :]
        each_side(lambda side: halo_copy(group, side).start(), range(2, 4))

    def take_halo(group):
        turn, first, fields = groups[group]
        each_side(lambda side: halo_copy(group, side, True).wait_recv())
        for k in range(first, first + fields):
            for side in (2, 3):
                pads[turn][k, beside_rows(side), :] = edge_in[turn, side - 2, k]

    def viscosity():
        whole(mean_land, mean_sems.at[0], mean_sems.at[1]).wait_recv()
        expand = (
            lax.broadcasted_iota(jnp.int32, (LZ, 32), 0)
            == lax.broadcasted_iota(jnp.int32, (LZ, 32), 1) // 4
        ).astype(jnp.float32)
        same = (
            lax.broadcasted_iota(jnp.int32, (128, 32), 0) % 4
            == lax.broadcasted_iota(jnp.int32, (128, 32), 1) % 4
        )
        gather = (
            lax.broadcasted_iota(jnp.int32, (32, 128), 0)
            == lax.broadcasted_iota(jnp.int32, (32, 128), 1) // 4
        ).astype(jnp.float32)
        for y in range(LY):
            for z in range(LZ):
                mean_held[pl.ds(z, 4, stride=LZ), :] = mean_land[source_of(y, z)]
            for p in range(4):
                tall = jnp.dot(
                    mean_held[p * LZ : p * LZ + LZ].T, expand,
                    precision=lax.Precision.HIGHEST, preferred_element_type=jnp.float32,
                )
                cells = jnp.dot(
                    gather, jnp.where(same, tall, 0.0),
                    precision=lax.Precision.HIGHEST, preferred_element_type=jnp.float32,
                )
                for half in range(2):
                    for layer in range(4):
                        at = half * 16 + layer * 4
                        mean_ref[half * 4 + p, layer, y * 4 : y * 4 + 4, :] = cells[at : at + 4]
        for layer in range(4):
            mixture = MIX_WEIGHTS[0] * mean_ref[0, layer]
            for p in range(1, len(MIX_WEIGHTS)):
                mixture = mixture + MIX_WEIGHTS[p] * mean_ref[p, layer]
            wide_mix = jnp.dot(
                mixture, gather,
                precision=lax.Precision.HIGHEST, preferred_element_type=jnp.float32,
            )
            spread = jnp.concatenate(
                [jnp.broadcast_to(wide_mix[j : j + 1], (4, 128)) for j in range(LY * 4)], axis=0
            )
            for x in range(layer * 4, layer * 4 + 4):
                eta[slab_rows(x + 1), :] = drag_grid[x] * jnp.exp(
                    HEAT_FACTOR * (0.5 - heat_ref[x]) + spread
                )
        for side in (2, 3):
            eta_out[side - 2] = eta[edge_rows(side), :]
        each_side(lambda side: eta_copy(side).start())

    def take_eta():
        each_side(lambda side: eta_copy(side, True).wait_recv())
        for side in (2, 3):
            eta[beside_rows(side), :] = eta_in[side - 2]

        def slab(x, carry):
            factors(x, eta, heat_ref, side_ref, rest_ref)
            return carry

        lax.fori_loop(0, nx, slab, 0)

    for f in range(FIELDS):
        whole(lands[f], data_send.at[f], data_recv.at[f]).wait_recv()
        if f + AHEAD < FIELDS:
            send_field(f + AHEAD)
        for y in range(LY):
            at = slice(y * BS, (y + 1) * BS)
            part = grid_part(f, y)
            if f == 0:
                heat_ref[:, at, :] = part
            elif f == 1:
                drag_grid[:, at, :] = part
            else:
                for x in range(nx):
                    pad_0[f - 2, pl.ds((x + 1) * PITCH + FIRST + y * BS, BS), :] = part[x]
        if f == 1:
            viscosity()
        elif f > 1:
            send_halo(f - 2)
        if f == 3:
            take_eta()

    def sweep(turn, xs, together, first, rows):
        def slabs(step, carry):
            for i in range(together):
                x = xs[0] + (step * together + i) * xs[1]
                moved = relax(x, first, rows, pads[turn], side_ref, rest_ref)
                for k in range(4):
                    if turn == SWEEPS - 1:
                        inner_ref[k, x - 1] = moved[k]
                    else:
                        at = pl.ds((x + 1) * PITCH + FIRST + first, rows)
                        pads[turn + 1][k, at, :] = moved[k]
            return carry

        lax.fori_loop(0, xs[2] // together, slabs, 0)

    inside, ends = (1, 1, nx - 2), (0, nx - 1, 2)
    for turn in range(SWEEPS):
        if turn > 0:
            send_halo(3 + turn)
        sweep(turn, inside, INNER, 8, ny - 16)
        for group in range(4) if turn == 0 else (3 + turn,):
            take_halo(group)
        if turn < SWEEPS - 1:
            sweep(turn, ends, 2, 0, ny)
            for first in (0, ny - 8):
                sweep(turn, inside, OUTER, first, 8)

    whole(table, table_sems.at[0], table_sems.at[1]).wait_send()
    whole(mean_land, mean_sems.at[0], mean_sems.at[1]).wait_send()
    for f in range(FIELDS):
        whole(lands[f], data_send.at[f], data_recv.at[f]).wait_send()
    each_side(lambda side: eta_copy(side).wait_send())
    for group in range(len(groups)):
        each_side(lambda side: halo_copy(group, side).wait_send())


def migrate(slots, flow, stress, heat, drag, attributes, holder, voxel):
    wide_count, narrow_count = lax.axis_size("wide"), lax.axis_size("narrow")
    count = wide_count * narrow_count
    blocks = slots.shape[0]
    tracers = attributes.shape[1]
    nx, ny, nz = LX * BS, LY * BS, LZ * BS
    rows = BS * BS * BS // 128
    pad_rows = (nx + 2) * PITCH + 8
    vmem = pl.BlockSpec(memory_space=pltpu.VMEM)
    hbm = pl.BlockSpec(memory_space=pltpu.HBM)
    f32 = jnp.float32
    per_field = [pltpu.VMEM((count, rows, 128), f32)] * FIELDS
    dma = pltpu.SemaphoreType.DMA
    pinned = [
        pltpu.with_memory_space_constraint(array, pltpu.HBM)
        for array in (slots, flow, stress, heat, drag, attributes, holder, voxel)
    ]
    return pl.pallas_call(
        functools.partial(migrate_kernel, wide_count=wide_count, narrow_count=narrow_count),
        out_shape=(
            jax.ShapeDtypeStruct((4, pad_rows, nz), f32),
            jax.ShapeDtypeStruct((4, nx - 2, ny - 16, nz), f32),
            jax.ShapeDtypeStruct((6, nx, ny, nz), f32),
            jax.ShapeDtypeStruct((3, nx, ny, nz), f32),
            jax.ShapeDtypeStruct((nx, ny, nz), f32),
            jax.ShapeDtypeStruct((8, LX * 4, LY * 4, LZ * 4), f32),
        ),
        in_specs=[hbm] * 8,
        out_specs=(vmem,) * 6,
        scratch_shapes=[
            pltpu.SMEM((blocks,), jnp.int32),
            pltpu.VMEM((1, 128), jnp.int32),
            pltpu.VMEM((count, 1, 128), jnp.int32),
            pltpu.SMEM((count, 1, 128), jnp.int32),
            pltpu.VMEM((FIELDS, blocks, rows * 128), f32),
            pltpu.VMEM((blocks * rows, 128), f32),
            pltpu.VMEM((FIELDS, blocks, rows, 128), f32),
            *per_field,
            *per_field,
            pltpu.VMEM((8, tracers), f32),
            pltpu.VMEM((1, tracers), jnp.int32),
            pltpu.VMEM((1, tracers), jnp.int32),
            pltpu.VMEM((blocks, 4, 128), f32),
            pltpu.VMEM((count, 4, 128), f32),
            pltpu.VMEM((count, 4, 128), f32),
            pltpu.VMEM((4 * LZ, 128), f32),
            pltpu.VMEM((rows * LZ, 128), f32),
            pltpu.VMEM((nx, ny, nz), f32),
            pltpu.VMEM((4, pad_rows, nz), f32),
            pltpu.VMEM((4, pad_rows, nz), f32),
            pltpu.VMEM((pad_rows, nz), f32),
            pltpu.VMEM((SWEEPS, 2, 4, nx, nz), f32),
            pltpu.VMEM((SWEEPS, 2, 4, nx, nz), f32),
            pltpu.VMEM((2, nx, nz), f32),
            pltpu.VMEM((2, nx, nz), f32),
            dma((FIELDS + 3,)),
            dma((2,)),
            dma((FIELDS,)),
            dma((FIELDS,)),
            dma((2,)),
            dma((4,)),
            dma((4,)),
            dma((SWEEPS + 3, 4)),
            dma((SWEEPS + 3, 4)),
            dma(()),
        ],
        compiler_params=pltpu.CompilerParams(
            collective_id=1,
            has_side_effects=True,
            vmem_limit_bytes=(24 if count <= 32 else 52) * 1024 * 1024,
        ),
    )(*pinned)


def last_kernel(
    pad_ref, inner_ref, side_ref, rest_ref, heat_ref, mean_ref,
    velocity_ref, pressure_ref, heat_out_ref, mean_out_ref, fresh, sems,
):
    nx, ny, nz = heat_ref.shape
    copies = []

    def send(source, target):
        copies.append(pltpu.make_async_copy(source, target, sems.at[len(copies)]))
        copies[-1].start()

    def send_fresh(xs, ys):
        send(fresh.at[pl.ds(0, 3), xs, ys], velocity_ref.at[:, xs, ys])
        send(fresh.at[3, xs, ys], pressure_ref.at[xs, ys])

    send(heat_ref, heat_out_ref)
    send(mean_ref, mean_out_ref)
    middle, centre = pl.ds(1, nx - 2), pl.ds(8, ny - 16)
    send(inner_ref.at[pl.ds(0, 3)], velocity_ref.at[:, middle, centre])
    send(inner_ref.at[3], pressure_ref.at[middle, centre])

    def sweep(xs, together, first, rows):
        def slabs(step, carry):
            for i in range(together):
                x = xs[0] + (step * together + i) * xs[1]
                moved = relax(x, first, rows, pad_ref, side_ref, rest_ref)
                for k in range(4):
                    fresh[k, x, pl.ds(first, rows), :] = moved[k]
            return carry

        lax.fori_loop(0, xs[2] // together, slabs, 0)

    for first in (0, ny - 8):
        sweep((1, 1, nx - 2), OUTER, first, 8)
        send_fresh(middle, pl.ds(first, 8))
    sweep((0, nx - 1, 2), 2, 0, ny)
    for x in (0, nx - 1):
        send_fresh(pl.ds(x, 1), pl.ds(0, ny))
    for copy in copies:
        copy.wait()


def last_sweep(pad, inner, side, rest, heat, means):
    nx, ny, nz = heat.shape
    vmem = pl.BlockSpec(memory_space=pltpu.VMEM)
    hbm = pl.BlockSpec(memory_space=pltpu.HBM)
    return pl.pallas_call(
        last_kernel,
        out_shape=(
            jax.ShapeDtypeStruct((3, nx, ny, nz), jnp.float32),
            jax.ShapeDtypeStruct((nx, ny, nz), jnp.float32),
            jax.ShapeDtypeStruct(heat.shape, jnp.float32),
            jax.ShapeDtypeStruct(means.shape, jnp.float32),
        ),
        in_specs=[vmem] * 6,
        out_specs=(hbm,) * 4,
        scratch_shapes=[
            pltpu.VMEM((4, nx, ny, nz), jnp.float32),
            pltpu.SemaphoreType.DMA((12,)),
        ],
        compiler_params=pltpu.CompilerParams(vmem_limit_bytes=16 * 1024 * 1024),
    )(pad, inner, side, rest, heat, means)


def per_device(
    tile_flow_speed,
    tile_stress_mean,
    tile_heat_state,
    tile_drag_coefficient,
    marker_attributes,
    marker_holding_tile,
    marker_voxel_number,
    prior_slot_of_tile,
):
    tracers = marker_attributes.shape[1]
    results = migrate(
        prior_slot_of_tile,
        tile_flow_speed.transpose(1, 0, 2),
        tile_stress_mean,
        tile_heat_state,
        tile_drag_coefficient,
        marker_attributes,
        marker_holding_tile.reshape(1, tracers),
        marker_voxel_number.reshape(1, tracers),
    )
    return last_sweep(*results)


def solution(mesh):
    in_specs = (
        P(("wide", "narrow"), None, None),
        P(("wide", "narrow"), None),
        P(("wide", "narrow"), None),
        P(("wide", "narrow"), None),
        P(None, ("wide", "narrow")),
        P(("wide", "narrow")),
        P(("wide", "narrow")),
        P(("wide", "narrow")),
    )
    out_specs = (
        P(None, "wide", "narrow", None),
        P("wide", "narrow", None),
        P("wide", "narrow", None),
        P(None, "wide", "narrow", None),
    )
    return jax.shard_map(
        per_device, mesh=mesh, in_specs=in_specs, out_specs=out_specs, check_vma=False
    )
```

```python
import functools

import jax
import jax.numpy as jnp
from jax import lax
from jax.experimental import pallas as pl
from jax.experimental.pallas import tpu as pltpu
from jax.sharding import PartitionSpec as P

BS = 16
LX = 1
LY = 2
LZ = 8
SWEEPS = 3
BINS = 64
FIELDS = 6
AHEAD = 3
PITCH = 40
FIRST = 8
DEEP = 3
STEP = 16
TOGETHER = 5

MIX_WEIGHTS = (0.3, -0.25, 0.2, -0.15, 0.35, -0.3, 0.25, -0.2)
RELAX_WEIGHT = 0.7
PRESSURE_WEIGHT = 0.3
HEAT_FACTOR = 2.0
DENSITY_FACTOR = 4.0
MESH = pl.DeviceIdType.MESH


def swap_groups(x):
    row = lax.broadcasted_iota(jnp.int32, x.shape, 1)
    group = lax.broadcasted_iota(jnp.int32, x.shape, 2) // BS
    for bit in (1, 2, 4):
        row_set = (row & bit) != 0
        group_set = (group & bit) != 0
        from_above = pltpu.roll(pltpu.roll(x, 8 - bit, 1), BS * bit, 2)
        from_below = pltpu.roll(pltpu.roll(x, bit, 1), 8 * BS - BS * bit, 2)
        x = jnp.where(
            row_set == group_set, x, jnp.where(group_set, from_above, from_below)
        )
    return x


def bin_sums(base, holder_ref, voxel_ref, attr_ref, blocks, chunk):
    props, tracers = attr_ref.shape
    total_bins = blocks * BINS
    bin_ids = lax.broadcasted_iota(jnp.int32, (total_bins, chunk), 0)

    def step(turn, sums):
        at = pl.ds(pl.multiple_of(turn * chunk, chunk), chunk)
        voxel = voxel_ref[:, at]
        key = (
            (holder_ref[:, at] - base) * BINS
            + (voxel >> 10) * 16
            + ((voxel >> 6) & 3) * 4
            + ((voxel >> 2) & 3)
        )
        table = jnp.where(bin_ids == key, 1.0, 0.0).astype(jnp.bfloat16)
        values = attr_ref[:, at]
        high = values.astype(jnp.bfloat16)
        rest = values - high.astype(jnp.float32)
        middle = rest.astype(jnp.bfloat16)
        low = (rest - middle.astype(jnp.float32)).astype(jnp.bfloat16)
        ones = jnp.ones((props, chunk), jnp.bfloat16)
        rows = jnp.concatenate([high, middle, low, ones], axis=0)
        return sums + lax.dot_general(
            rows, table, (((1,), (1,)), ((), ())), preferred_element_type=jnp.float32
        )

    sums = lax.fori_loop(
        0, tracers // chunk, step, jnp.zeros((4 * props, total_bins), jnp.float32)
    )
    total = sums[:props] + sums[props : 2 * props] + sums[2 * props : 3 * props]
    return total / jnp.maximum(sums[3 * props :], 1.0)


def at_ends(shape):
    column = lax.broadcasted_iota(jnp.int32, shape, 1)
    return column == 0, column == shape[1] - 1


def z_pair(here):
    low_end, high_end = at_ends(here.shape)
    nz = here.shape[1]
    return (
        jnp.where(high_end, 0.0, pltpu.roll(here, nz - 1, 1)),
        jnp.where(low_end, 0.0, pltpu.roll(here, 1, 1)),
    )


def factors(base, rows, eta_ref, heat_ref, side_ref, rest_ref):
    here = eta_ref[pl.ds(base, rows), :]
    around = [
        eta_ref[pl.ds(base + off, rows), :] for off in (PITCH, -PITCH, 1, -1)
    ] + list(z_pair(here))
    face = [0.5 * (here + other) for other in around]
    diagonal = face[0]
    for m in range(1, 6):
        diagonal = diagonal + face[m]
    inside = here > 0.0
    scale = jnp.where(inside, RELAX_WEIGHT / jnp.where(inside, diagonal, 1.0), 0.0)
    low_end, high_end = at_ends(here.shape)
    own = pl.ds(base, rows)
    for m in range(6):
        value = face[m] * scale
        if m == 4:
            value = jnp.where(high_end, 0.0, value)
        elif m == 5:
            value = jnp.where(low_end, 0.0, value)
        side_ref[m, own, :] = value
    rest_ref[0, own, :] = 0.5 * scale
    rest_ref[1, own, :] = (0.5 * PRESSURE_WEIGHT) * here
    rest_ref[2, own, :] = scale * (DENSITY_FACTOR * heat_ref[own, :])


def relax(base, rows, pad, side_ref, rest_ref):
    nz = pad.shape[2]
    own = pl.ds(base, rows)

    def value(k, off=0):
        return pad[k, pl.ds(base + off, rows), :]

    side = [side_ref[m, own, :] for m in range(6)]
    half_scale, squeeze, lift = (rest_ref[m, own, :] for m in range(3))
    press = value(3)
    press_up_z, press_down_z = z_pair(press)
    drops = (
        value(3, PITCH) - value(3, -PITCH),
        value(3, 1) - value(3, -1),
        press_up_z - press_down_z,
    )
    moved = []
    divergence = None
    for k in range(3):
        here = value(k)
        if k == 2:
            up_z, down_z = z_pair(here)
        else:
            up_z, down_z = pltpu.roll(here, nz - 1, 1), pltpu.roll(here, 1, 1)
        near = (
            value(k, PITCH), value(k, -PITCH), value(k, 1), value(k, -1), up_z, down_z,
        )
        fresh = (1.0 - RELAX_WEIGHT) * here - half_scale * drops[k]
        for m in range(6):
            fresh = fresh + side[m] * near[m]
        if k == 2:
            fresh = fresh + lift
        moved.append(fresh)
        flux = near[2 * k] - near[2 * k + 1]
        divergence = flux if divergence is None else divergence + flux
    moved.append(press - squeeze * divergence)
    return moved


def migrate_kernel(
    places_ref, flow_ref, stress_ref, warm_ref, drag_ref, attr_ref, holder_ref, voxel_ref,
    pad_ref, side_ref, rest_ref, heat_ref, mean_ref,
    slot_ref, row_ref, table, table_smem, raw, lined, mine, stage_0, stage_1, stage_2, stage_3, stage_4, stage_5,
    land_0, land_1, land_2, land_3, land_4, land_5,
    attr, holder, voxel, mean_mine, mean_stage, mean_land, mean_held, held, drag_grid,
    eta, warm, edge_in, edge_out, corner_in, corner_out,
    raw_sems, table_sems, data_send, data_recv, mean_sems,
    halo_send, halo_recv, small_sem,
    *, wide_count, narrow_count,
):
    count = wide_count * narrow_count
    wide, narrow = lax.axis_index("wide"), lax.axis_index("narrow")
    me = wide * narrow_count + narrow
    blocks = raw.shape[1]
    nx, ny, nz = heat_ref.shape
    stages = (stage_0, stage_1, stage_2, stage_3, stage_4, stage_5)
    lands = (land_0, land_1, land_2, land_3, land_4, land_5)

    to_slots = pltpu.make_async_copy(places_ref, slot_ref, small_sem)
    to_slots.start()
    sources = (
        warm_ref, drag_ref, flow_ref.at[0], flow_ref.at[1], flow_ref.at[2], stress_ref,
    )
    loads = [
        pltpu.make_async_copy(source, raw.at[f], raw_sems.at[f]) for f, source in enumerate(sources)
    ]
    loads.append(pltpu.make_async_copy(attr_ref, attr, raw_sems.at[FIELDS]))
    loads.append(pltpu.make_async_copy(holder_ref, holder, raw_sems.at[FIELDS + 1]))
    loads.append(pltpu.make_async_copy(voxel_ref, voxel, raw_sems.at[FIELDS + 2]))
    for load in loads:
        load.start()

    def others(act):
        near = [lax.rem(narrow + b, narrow_count) for b in range(narrow_count)]
        for b in range(1, narrow_count):
            act(wide, near[b])

        def row(a, carry):
            far = lax.rem(wide + a, wide_count)
            for b in range(narrow_count):
                act(far, near[b])
            return carry

        lax.fori_loop(1, wide_count, row, 0)

    barrier = pltpu.get_barrier_semaphore()
    others(
        lambda w, n: pl.semaphore_signal(
            barrier, inc=1, device_id=(w, n), device_id_type=MESH
        )
    )
    to_slots.wait()
    lane = lax.broadcasted_iota(jnp.int32, (1, 128), 1)
    places = jnp.zeros((1, 128), jnp.int32)
    my_own = jnp.int32(0)
    for r in range(blocks):
        owner = lax.div(slot_ref[r], blocks)
        local = slot_ref[r] - owner * blocks
        places = jnp.where(lane == owner, local, places)
        my_own = jnp.where(owner == me, local, my_own)
    row_ref[...] = places
    table[me] = places
    pl.semaphore_wait(barrier, count - 1)

    def send_row(w, n):
        pltpu.make_async_remote_copy(
            src_ref=row_ref,
            dst_ref=table.at[me],
            send_sem=table_sems.at[0],
            recv_sem=table_sems.at[1],
            device_id=(w, n),
            device_id_type=MESH,
        ).start()

    others(send_row)

    for ref in (pad_ref, eta, warm, edge_in, corner_in, corner_out):
        ref[...] = jnp.zeros(ref.shape, jnp.float32)

    def whole(ref, send_sem, recv_sem):
        part = ref.at[pl.ds(0, count - 1)]
        return pltpu.make_async_remote_copy(
            src_ref=part,
            dst_ref=part,
            send_sem=send_sem,
            recv_sem=recv_sem,
            device_id=(wide, narrow),
            device_id_type=MESH,
        )

    rows = BS * BS * BS // 128
    for f in range(FIELDS):
        loads[f].wait()
        for g in range(blocks // 8):
            for j in range(rows):
                lined[pl.ds(g * 8 * rows + j, 8, stride=rows), :] = raw[
                    f, g * 8 : g * 8 + 8, j * 128 : j * 128 + 128
                ]
        mine[f] = lined[...].reshape(blocks, rows, 128)

    whole(table, table_sems.at[0], table_sems.at[1]).wait_recv()
    to_scalar = pltpu.make_async_copy(table, table_smem, small_sem)
    to_scalar.start()
    to_scalar.wait()

    def wanted(d):
        return table_smem[d, 0, me]

    def send_field(f):
        def send(w, n):
            d = w * narrow_count + n
            stages[f][d] = mine[f, wanted(d)]
            pltpu.make_async_remote_copy(
                src_ref=stages[f].at[d],
                dst_ref=lands[f].at[me],
                send_sem=data_send.at[f],
                recv_sem=data_recv.at[f],
                device_id=(w, n),
                device_id_type=MESH,
            ).start()

        others(send)
        lands[f][me] = mine[f, my_own]

    for f in range(AHEAD):
        send_field(f)

    for load in loads[FIELDS:]:
        load.wait()
    tracers = attr.shape[1]
    chunk = 1024 if tracers % 1024 == 0 else tracers
    means = bin_sums(me * blocks, holder, voxel, attr, blocks, chunk)
    left = lax.broadcasted_iota(jnp.int32, (8, 128), 1) < BINS
    for q in range(blocks // 2):
        pair = means[:, q * 128 : q * 128 + 128]
        across = pltpu.roll(pair, BINS, 1)
        below = pltpu.roll(pair, 4, 0)
        both = pltpu.roll(across, 4, 0)
        mean_mine[2 * q] = jnp.where(left, pair, both)[:4]
        mean_mine[2 * q + 1] = jnp.where(left, across, below)[:4]

    def send_mean(w, n):
        d = w * narrow_count + n
        mean_stage[d] = mean_mine[wanted(d)]
        pltpu.make_async_remote_copy(
            src_ref=mean_stage.at[d],
            dst_ref=mean_land.at[me],
            send_sem=mean_sems.at[0],
            recv_sem=mean_sems.at[1],
            device_id=(w, n),
            device_id_type=MESH,
        ).start()

    others(send_mean)
    mean_land[me] = mean_mine[my_own]

    def source_of(y, z):
        return lax.div(slot_ref[y * LZ + z], blocks)

    def grid_part(f, y):
        for z in range(LZ):
            held[pl.ds(z, rows, stride=LZ), :] = lands[f][source_of(y, z)]
        return swap_groups(held[...].reshape(rows, LZ, 128)).reshape(BS, BS, 128)

    ways = ((-1, 0), (1, 0), (0, -1), (0, 1), (-1, -1), (-1, 1), (1, -1), (1, 1))
    low_side = {-1: (wide > 0, narrow > 0), 1: (wide < wide_count - 1, narrow < narrow_count - 1)}

    def exists(way):
        there = [low_side[step][axis] for axis, step in enumerate(way) if step]
        return there[0] if len(there) == 1 else there[0] & there[1]

    def row_of(x, y):
        return (x + DEEP) * PITCH + FIRST + y

    def grid_rows(g, at):
        if g < 2:
            return (warm, eta)[g].at[at]
        return pad_ref.at[g - 2, at]

    def depth_of(g):
        return DEEP - 1 if g == 0 else DEEP

    def messages(g):
        found = []
        for i in range(DEEP):
            for way, slot in ((-1, i), (1, DEEP + i)):
                mine_x, theirs_x = (i, nx + i) if way < 0 else (nx - DEEP + i, i - DEEP)
                here_x = i - DEEP if way < 0 else nx + i
                rows_at = [
                    grid_rows(g, pl.ds(row_of(x, 0), ny)) for x in (mine_x, theirs_x, here_x)
                ]
                found.append(
                    ((way, 0), slot, rows_at[0], rows_at[1], (slot + DEEP) % (2 * DEEP), rows_at[2])
                )
        deep = pl.ds(0, depth_of(g))
        for side, way in enumerate((-1, 1)):
            slot = 2 * DEEP + side
            found.append(
                (
                    (0, way), slot, edge_out.at[g, side, deep], edge_in.at[g, 1 - side, deep],
                    2 * DEEP + 1 - side, edge_in.at[g, side, deep],
                )
            )
        for c, way in enumerate(ways[4:]):
            found.append(
                (
                    way, 2 * DEEP + 2 + c, corner_out.at[g, c], corner_in.at[g, 3 - c],
                    2 * DEEP + 5 - c, corner_in.at[g, c],
                )
            )
        return found

    def each_message(g, act):
        for way in ways:
            group = [m for m in messages(g) if m[0] == way]

            @pl.when(exists(way))
            def _(way=way, group=group):
                for _, slot, source, target, far_slot, here in group:
                    act(way, slot, source, target, far_slot, here)

    def start_message(g):
        def act(way, slot, source, target, far_slot, here):
            pltpu.make_async_remote_copy(
                src_ref=source, dst_ref=target,
                send_sem=halo_send.at[g, slot], recv_sem=halo_recv.at[g, far_slot],
                device_id=(wide + way[0], narrow + way[1]), device_id_type=MESH,
            ).start()

        return act

    def wait_message(g, sent):
        def act(way, slot, source, target, far_slot, here):
            copy = pltpu.make_async_remote_copy(
                src_ref=source if sent else here, dst_ref=target if sent else here,
                send_sem=halo_send.at[g, slot], recv_sem=halo_recv.at[g, slot],
                device_id=(wide + way[0], narrow + way[1]), device_id_type=MESH,
            )
            copy.wait_send() if sent else copy.wait_recv()

        return act

    def read_rows(g, at):
        return (warm, eta)[g][at, :] if g < 2 else pad_ref[g - 2, at, :]

    def write_rows(g, at, value):
        if g < 2:
            (warm, eta)[g][at, :] = value
        else:
            pad_ref[g - 2, at, :] = value

    def send_halo(g):
        depth = depth_of(g)
        for side in range(2):
            for i in range(depth):
                y = i if side == 0 else ny - depth + i
                edge_out[g, side, i] = read_rows(g, pl.ds(row_of(0, y), nx, stride=PITCH))
        for c, (dx, dy) in enumerate(ways[4:]):
            for i in range(2):
                x = i if dx < 0 else nx - 2 + i
                y = 0 if dy < 0 else ny - 2
                corner_out[g, c, 2 * i : 2 * i + 2, :] = read_rows(g, pl.ds(row_of(x, y), 2))
        each_message(g, start_message(g))

    def take_halo(g):
        depth = depth_of(g)
        each_message(g, wait_message(g, False))
        for side in range(2):
            for i in range(depth):
                y = i - depth if side == 0 else ny + i
                write_rows(g, pl.ds(row_of(0, y), nx, stride=PITCH), edge_in[g, side, i])
        for c, (dx, dy) in enumerate(ways[4:]):
            for i in range(2):
                x = i - 2 if dx < 0 else nx + i
                y = -2 if dy < 0 else ny
                write_rows(g, pl.ds(row_of(x, y), 2), corner_in[g, c, 2 * i : 2 * i + 2, :])

    def viscosity():
        whole(mean_land, mean_sems.at[0], mean_sems.at[1]).wait_recv()
        expand = (
            lax.broadcasted_iota(jnp.int32, (LZ, 32), 0)
            == lax.broadcasted_iota(jnp.int32, (LZ, 32), 1) // 4
        ).astype(jnp.float32)
        same = (
            lax.broadcasted_iota(jnp.int32, (128, 32), 0) % 4
            == lax.broadcasted_iota(jnp.int32, (128, 32), 1) % 4
        )
        gather = (
            lax.broadcasted_iota(jnp.int32, (32, 128), 0)
            == lax.broadcasted_iota(jnp.int32, (32, 128), 1) // 4
        ).astype(jnp.float32)
        for y in range(LY):
            for z in range(LZ):
                mean_held[pl.ds(z, 4, stride=LZ), :] = mean_land[source_of(y, z)]
            for p in range(4):
                tall = jnp.dot(
                    mean_held[p * LZ : p * LZ + LZ].T, expand,
                    precision=lax.Precision.HIGHEST, preferred_element_type=jnp.float32,
                )
                cells = jnp.dot(
                    gather, jnp.where(same, tall, 0.0),
                    precision=lax.Precision.HIGHEST, preferred_element_type=jnp.float32,
                )
                for half in range(2):
                    for layer in range(4):
                        at = half * 16 + layer * 4
                        mean_ref[half * 4 + p, layer, y * 4 : y * 4 + 4, :] = cells[at : at + 4]
        for layer in range(4):
            mixture = MIX_WEIGHTS[0] * mean_ref[0, layer]
            for p in range(1, len(MIX_WEIGHTS)):
                mixture = mixture + MIX_WEIGHTS[p] * mean_ref[p, layer]
            wide_mix = jnp.dot(
                mixture, gather,
                precision=lax.Precision.HIGHEST, preferred_element_type=jnp.float32,
            )
            spread = jnp.concatenate(
                [jnp.broadcast_to(wide_mix[j : j + 1], (4, 128)) for j in range(LY * 4)], axis=0
            )
            for x in range(layer * 4, layer * 4 + 4):
                eta[pl.ds(row_of(x, 0), ny), :] = drag_grid[x] * jnp.exp(
                    HEAT_FACTOR * (0.5 - heat_ref[x]) + spread
                )

    def all_factors():
        step_rows = STEP * TOGETHER

        def step(turn, carry):
            base = pl.multiple_of(PITCH + turn * step_rows, 8)
            factors(base, step_rows, eta, warm, side_ref, rest_ref)
            return carry

        lax.fori_loop(0, (nx + 2 * DEEP - 2) * PITCH // step_rows, step, 0)

    for f in range(FIELDS):
        whole(lands[f], data_send.at[f], data_recv.at[f]).wait_recv()
        if f + AHEAD < FIELDS:
            send_field(f + AHEAD)
        for y in range(LY):
            at = slice(y * BS, (y + 1) * BS)
            part = grid_part(f, y)
            if f == 0:
                heat_ref[:, at, :] = part
            if f == 1:
                drag_grid[:, at, :] = part
            else:
                for x in range(nx):
                    write_rows(f, pl.ds(row_of(x, y * BS), BS), part[x])
        if f == 1:
            viscosity()
        send_halo(f)
        if f == 3:
            take_halo(0)
            take_halo(1)
            all_factors()
    for f in range(2, FIELDS):
        take_halo(f)

    whole(table, table_sems.at[0], table_sems.at[1]).wait_send()
    whole(mean_land, mean_sems.at[0], mean_sems.at[1]).wait_send()
    for f in range(FIELDS):
        whole(lands[f], data_send.at[f], data_recv.at[f]).wait_send()
    for f in range(FIELDS):
        each_message(f, wait_message(f, True))


def migrate(slots, flow, stress, heat, drag, attributes, holder, voxel):
    wide_count, narrow_count = lax.axis_size("wide"), lax.axis_size("narrow")
    count = wide_count * narrow_count
    blocks = slots.shape[0]
    tracers = attributes.shape[1]
    nx, ny, nz = LX * BS, LY * BS, LZ * BS
    rows = BS * BS * BS // 128
    pad_rows = (nx + 2 * DEEP) * PITCH + 8
    vmem = pl.BlockSpec(memory_space=pltpu.VMEM)
    hbm = pl.BlockSpec(memory_space=pltpu.HBM)
    f32 = jnp.float32
    per_field = [pltpu.VMEM((count, rows, 128), f32)] * FIELDS
    dma = pltpu.SemaphoreType.DMA
    pinned = [
        pltpu.with_memory_space_constraint(array, pltpu.HBM)
        for array in (slots, flow, stress, heat, drag, attributes, holder, voxel)
    ]
    return pl.pallas_call(
        functools.partial(migrate_kernel, wide_count=wide_count, narrow_count=narrow_count),
        out_shape=(
            jax.ShapeDtypeStruct((4, pad_rows, nz), f32),
            jax.ShapeDtypeStruct((6, pad_rows, nz), f32),
            jax.ShapeDtypeStruct((3, pad_rows, nz), f32),
            jax.ShapeDtypeStruct((nx, ny, nz), f32),
            jax.ShapeDtypeStruct((8, LX * 4, LY * 4, LZ * 4), f32),
        ),
        in_specs=[hbm] * 8,
        out_specs=(vmem,) * 5,
        scratch_shapes=[
            pltpu.SMEM((blocks,), jnp.int32),
            pltpu.VMEM((1, 128), jnp.int32),
            pltpu.VMEM((count, 1, 128), jnp.int32),
            pltpu.SMEM((count, 1, 128), jnp.int32),
            pltpu.VMEM((FIELDS, blocks, rows * 128), f32),
            pltpu.VMEM((blocks * rows, 128), f32),
            pltpu.VMEM((FIELDS, blocks, rows, 128), f32),
            *per_field,
            *per_field,
            pltpu.VMEM((8, tracers), f32),
            pltpu.VMEM((1, tracers), jnp.int32),
            pltpu.VMEM((1, tracers), jnp.int32),
            pltpu.VMEM((blocks, 4, 128), f32),
            pltpu.VMEM((count, 4, 128), f32),
            pltpu.VMEM((count, 4, 128), f32),
            pltpu.VMEM((4 * LZ, 128), f32),
            pltpu.VMEM((rows * LZ, 128), f32),
            pltpu.VMEM((nx, ny, nz), f32),
            pltpu.VMEM((pad_rows, nz), f32),
            pltpu.VMEM((pad_rows, nz), f32),
            pltpu.VMEM((FIELDS, 2, DEEP, nx, nz), f32),
            pltpu.VMEM((FIELDS, 2, DEEP, nx, nz), f32),
            pltpu.VMEM((FIELDS, 4, 8, nz), f32),
            pltpu.VMEM((FIELDS, 4, 8, nz), f32),
            dma((FIELDS + 3,)),
            dma((2,)),
            dma((FIELDS,)),
            dma((FIELDS,)),
            dma((2,)),
            dma((FIELDS, 2 * DEEP + 6)),
            dma((FIELDS, 2 * DEEP + 6)),
            dma(()),
        ],
        compiler_params=pltpu.CompilerParams(
            collective_id=1,
            has_side_effects=True,
            vmem_limit_bytes=(24 if count <= 32 else 44) * 1024 * 1024,
        ),
    )(*pinned)


def relax_kernel(
    pad_ref, side_ref, rest_ref, heat_ref, mean_ref,
    velocity_ref, pressure_ref, heat_out_ref, mean_out_ref, pad_1, pad_2, fresh, sems,
):
    nx, ny, nz = heat_ref.shape
    copies = []

    def send(source, target):
        copies.append(pltpu.make_async_copy(source, target, sems.at[len(copies)]))
        copies[-1].start()

    send(heat_ref, heat_out_ref)
    send(mean_ref, mean_out_ref)

    for turn, (old, new) in enumerate(((pad_ref, pad_1), (pad_1, pad_2))):
        first = turn + 1
        slabs = nx + 2 * DEEP - 2 * first

        def rows_on(step, carry, first=first, old=old, new=new):
            for i in range(TOGETHER):
                base = pl.multiple_of(first * PITCH + (step * TOGETHER + i) * STEP, 8)
                moved = relax(base, STEP, old, side_ref, rest_ref)
                for k in range(4):
                    new[k, pl.ds(base, STEP), :] = moved[k]
            return carry

        lax.fori_loop(0, slabs * PITCH // (STEP * TOGETHER), rows_on, 0)

    parts = 4
    thick = nx // parts
    for part in range(parts):

        def slabs_on(step, carry):
            for i in range(2):
                x = part * thick + step * 2 + i
                for half in range(ny // STEP):
                    base = pl.multiple_of((x + DEEP) * PITCH + FIRST + half * STEP, 8)
                    moved = relax(base, STEP, pad_2, side_ref, rest_ref)
                    for k in range(4):
                        fresh[k, x, half * STEP : (half + 1) * STEP, :] = moved[k]
            return carry

        lax.fori_loop(0, thick // 2, slabs_on, 0)
        at = pl.ds(part * thick, thick)
        send(fresh.at[pl.ds(0, 3), at], velocity_ref.at[:, at])
        send(fresh.at[3, at], pressure_ref.at[at])
    for copy in copies:
        copy.wait()


def relax_all(pad, side, rest, heat, means):
    nx, ny, nz = heat.shape
    vmem = pl.BlockSpec(memory_space=pltpu.VMEM)
    hbm = pl.BlockSpec(memory_space=pltpu.HBM)
    return pl.pallas_call(
        relax_kernel,
        out_shape=(
            jax.ShapeDtypeStruct((3, nx, ny, nz), jnp.float32),
            jax.ShapeDtypeStruct((nx, ny, nz), jnp.float32),
            jax.ShapeDtypeStruct(heat.shape, jnp.float32),
            jax.ShapeDtypeStruct(means.shape, jnp.float32),
        ),
        in_specs=[vmem] * 5,
        out_specs=(hbm,) * 4,
        scratch_shapes=[
            pltpu.VMEM(pad.shape, jnp.float32),
            pltpu.VMEM(pad.shape, jnp.float32),
            pltpu.VMEM((4, nx, ny, nz), jnp.float32),
            pltpu.SemaphoreType.DMA((10,)),
        ],
        compiler_params=pltpu.CompilerParams(vmem_limit_bytes=16 * 1024 * 1024),
    )(pad, side, rest, heat, means)


def per_device(
    tile_flow_speed,
    tile_stress_mean,
    tile_heat_state,
    tile_drag_coefficient,
    marker_attributes,
    marker_holding_tile,
    marker_voxel_number,
    prior_slot_of_tile,
):
    tracers = marker_attributes.shape[1]
    results = migrate(
        prior_slot_of_tile,
        tile_flow_speed.transpose(1, 0, 2),
        tile_stress_mean,
        tile_heat_state,
        tile_drag_coefficient,
        marker_attributes,
        marker_holding_tile.reshape(1, tracers),
        marker_voxel_number.reshape(1, tracers),
    )
    return relax_all(*results)


def solution(mesh):
    in_specs = (
        P(("wide", "narrow"), None, None),
        P(("wide", "narrow"), None),
        P(("wide", "narrow"), None),
        P(("wide", "narrow"), None),
        P(None, ("wide", "narrow")),
        P(("wide", "narrow")),
        P(("wide", "narrow")),
        P(("wide", "narrow")),
    )
    out_specs = (
        P(None, "wide", "narrow", None),
        P("wide", "narrow", None),
        P("wide", "narrow", None),
        P(None, "wide", "narrow", None),
    )
    return jax.shard_map(
        per_device, mesh=mesh, in_specs=in_specs, out_specs=out_specs, check_vma=False
    )
```

```python
import functools

import jax
import jax.numpy as jnp
from jax import lax
from jax.experimental import pallas as pl
from jax.experimental.pallas import tpu as pltpu
from jax.sharding import PartitionSpec as P

BS = 16
LX = 1
LY = 2
LZ = 8
SWEEPS = 3
BINS = 64
FIELDS = 6
AHEAD = 3
PITCH = 40
FIRST = 8
DEEP = 3
STEP = 16
TURNS = 1
DRIFT_TURNS = 5

MIX_WEIGHTS = (0.3, -0.25, 0.2, -0.15, 0.35, -0.3, 0.25, -0.2)
RELAX_WEIGHT = 0.7
PRESSURE_WEIGHT = 0.3
HEAT_FACTOR = 2.0
DENSITY_FACTOR = 4.0
MESH = pl.DeviceIdType.MESH


def swap_groups(x):
    row = lax.broadcasted_iota(jnp.int32, x.shape, 1)
    group = lax.broadcasted_iota(jnp.int32, x.shape, 2) // BS
    for bit in (1, 2, 4):
        row_set = (row & bit) != 0
        group_set = (group & bit) != 0
        from_above = pltpu.roll(pltpu.roll(x, 8 - bit, 1), BS * bit, 2)
        from_below = pltpu.roll(pltpu.roll(x, bit, 1), 8 * BS - BS * bit, 2)
        x = jnp.where(
            row_set == group_set, x, jnp.where(group_set, from_above, from_below)
        )
    return x


def bin_sums(base, holder_ref, voxel_ref, attr_ref, blocks, chunk):
    props, tracers = attr_ref.shape
    total_bins = blocks * BINS
    bin_ids = lax.broadcasted_iota(jnp.int32, (total_bins, chunk), 0)

    def step(turn, sums):
        at = pl.ds(pl.multiple_of(turn * chunk, chunk), chunk)
        voxel = voxel_ref[:, at]
        key = (
            (holder_ref[:, at] - base) * BINS
            + (voxel >> 10) * 16
            + ((voxel >> 6) & 3) * 4
            + ((voxel >> 2) & 3)
        )
        table = jnp.where(bin_ids == key, 1.0, 0.0).astype(jnp.bfloat16)
        values = attr_ref[:, at]
        high = values.astype(jnp.bfloat16)
        rest = values - high.astype(jnp.float32)
        middle = rest.astype(jnp.bfloat16)
        low = (rest - middle.astype(jnp.float32)).astype(jnp.bfloat16)
        ones = jnp.ones((props, chunk), jnp.bfloat16)
        rows = jnp.concatenate([high, middle, low, ones], axis=0)
        return sums + lax.dot_general(
            rows, table, (((1,), (1,)), ((), ())), preferred_element_type=jnp.float32
        )

    sums = lax.fori_loop(
        0, tracers // chunk, step, jnp.zeros((4 * props, total_bins), jnp.float32)
    )
    total = sums[:props] + sums[props : 2 * props] + sums[2 * props : 3 * props]
    return total / jnp.maximum(sums[3 * props :], 1.0)


def at_ends(shape):
    column = lax.broadcasted_iota(jnp.int32, shape, 1)
    return column == 0, column == shape[1] - 1


def z_pair(here):
    low_end, high_end = at_ends(here.shape)
    nz = here.shape[1]
    return (
        jnp.where(high_end, 0.0, pltpu.roll(here, nz - 1, 1)),
        jnp.where(low_end, 0.0, pltpu.roll(here, 1, 1)),
    )


def factors(base, rows, eta_ref, heat_ref, side_ref, rest_ref):
    here = eta_ref[pl.ds(base, rows), :]
    around = [
        eta_ref[pl.ds(base + off, rows), :] for off in (PITCH, -PITCH, 1, -1)
    ] + list(z_pair(here))
    face = [0.5 * (here + other) for other in around]
    diagonal = face[0]
    for m in range(1, 6):
        diagonal = diagonal + face[m]
    inside = here > 0.0
    scale = jnp.where(inside, RELAX_WEIGHT / jnp.where(inside, diagonal, 1.0), 0.0)
    low_end, high_end = at_ends(here.shape)
    own = pl.ds(base, rows)
    for m in range(6):
        value = face[m] * scale
        if m == 4:
            value = jnp.where(high_end, 0.0, value)
        elif m == 5:
            value = jnp.where(low_end, 0.0, value)
        side_ref[m, own, :] = value
    rest_ref[0, own, :] = 0.5 * scale
    rest_ref[1, own, :] = (0.5 * PRESSURE_WEIGHT) * here
    rest_ref[2, own, :] = scale * (DENSITY_FACTOR * heat_ref[own, :])


def drift(base, rows, pad, side_ref, rest_ref):
    nz = pad.shape[2]
    own = pl.ds(base, rows)

    def value(k, off=0):
        return pad[k, pl.ds(base + off, rows), :]

    side = [side_ref[m, own, :] for m in range(6)]
    found = []
    divergence = None
    for k in range(3):
        here = value(k)
        if k == 2:
            up_z, down_z = z_pair(here)
        else:
            up_z, down_z = pltpu.roll(here, nz - 1, 1), pltpu.roll(here, 1, 1)
        near = (
            value(k, PITCH), value(k, -PITCH), value(k, 1), value(k, -1), up_z, down_z,
        )
        fresh = (1.0 - RELAX_WEIGHT) * here
        for m in range(6):
            fresh = fresh + side[m] * near[m]
        if k == 2:
            fresh = fresh + rest_ref[2, own, :]
        found.append(fresh)
        flux = near[2 * k] - near[2 * k + 1]
        divergence = flux if divergence is None else divergence + flux
    found.append(rest_ref[1, own, :] * divergence)
    return found


def push(base, rows, pad, rest_ref, drifted):
    own = pl.ds(base, rows)

    def value(off=0):
        return pad[3, pl.ds(base + off, rows), :]

    press = value()
    up_z, down_z = z_pair(press)
    half_scale = rest_ref[0, own, :]
    drops = (value(PITCH) - value(-PITCH), value(1) - value(-1), up_z - down_z)
    return [drifted[k] - half_scale * drops[k] for k in range(3)] + [press - drifted[3]]


def relax(base, rows, pad, side_ref, rest_ref):
    return push(base, rows, pad, rest_ref, drift(base, rows, pad, side_ref, rest_ref))


def over_rows(first, last, turns, act):
    together = (last - first) // (STEP * turns)
    assert together * STEP * turns == last - first

    def step(turn, carry):
        for i in range(together):
            act(pl.multiple_of(first + (turn * together + i) * STEP, 8))
        return carry

    lax.fori_loop(0, turns, step, 0)


def migrate_kernel(
    places_ref, flow_ref, stress_ref, warm_ref, drag_ref, attr_ref, holder_ref, voxel_ref,
    pad_ref, part_ref, side_ref, rest_ref, heat_ref, mean_ref,
    slot_ref, row_ref, table, table_smem, raw, lined, mine, stage_0, stage_1, stage_2, stage_3, stage_4, stage_5,
    land_0, land_1, land_2, land_3, land_4, land_5,
    attr, holder, voxel, mean_mine, mean_stage, mean_land, mean_held, held, drag_grid,
    eta, warm, edge_in, edge_out, corner_in, corner_out,
    raw_sems, table_sems, data_send, data_recv, mean_sems,
    halo_send, halo_recv, small_sem,
    *, wide_count, narrow_count,
):
    count = wide_count * narrow_count
    wide, narrow = lax.axis_index("wide"), lax.axis_index("narrow")
    me = wide * narrow_count + narrow
    blocks = raw.shape[1]
    nx, ny, nz = heat_ref.shape
    stages = (stage_0, stage_1, stage_2, stage_3, stage_4, stage_5)
    lands = (land_0, land_1, land_2, land_3, land_4, land_5)

    to_slots = pltpu.make_async_copy(places_ref, slot_ref, small_sem)
    to_slots.start()
    sources = (
        warm_ref, drag_ref, flow_ref.at[0], flow_ref.at[1], flow_ref.at[2], stress_ref,
    )
    loads = [
        pltpu.make_async_copy(source, raw.at[f], raw_sems.at[f]) for f, source in enumerate(sources)
    ]
    loads.append(pltpu.make_async_copy(attr_ref, attr, raw_sems.at[FIELDS]))
    loads.append(pltpu.make_async_copy(holder_ref, holder, raw_sems.at[FIELDS + 1]))
    loads.append(pltpu.make_async_copy(voxel_ref, voxel, raw_sems.at[FIELDS + 2]))
    for load in loads:
        load.start()

    def flipped(k):
        place, bit = narrow, 1
        while bit < narrow_count:
            if k & bit:
                place = place + bit * (1 - 2 * lax.rem(lax.div(narrow, bit), 2))
            bit *= 2
        return place

    far_first = [*range(narrow_count // 2, narrow_count), *range(1, narrow_count // 2), 0]

    def others(act):
        for k in far_first:
            near = flipped(k)

            def step(a, carry, near=near):
                act(lax.rem(wide + a, wide_count), near)
                return carry

            lax.fori_loop(0 if k else 1, wide_count, step, 0)

    barrier = pltpu.get_barrier_semaphore()
    others(
        lambda w, n: pl.semaphore_signal(
            barrier, inc=1, device_id=(w, n), device_id_type=MESH
        )
    )
    to_slots.wait()
    lane = lax.broadcasted_iota(jnp.int32, (1, 128), 1)
    places = jnp.zeros((1, 128), jnp.int32)
    my_own = jnp.int32(0)
    for r in range(blocks):
        owner = lax.div(slot_ref[r], blocks)
        local = slot_ref[r] - owner * blocks
        places = jnp.where(lane == owner, local, places)
        my_own = jnp.where(owner == me, local, my_own)
    row_ref[...] = places
    table[me] = places
    pl.semaphore_wait(barrier, count - 1)

    def send_row(w, n):
        pltpu.make_async_remote_copy(
            src_ref=row_ref,
            dst_ref=table.at[me],
            send_sem=table_sems.at[0],
            recv_sem=table_sems.at[1],
            device_id=(w, n),
            device_id_type=MESH,
        ).start()

    others(send_row)

    for ref in (pad_ref, eta, warm, edge_in, corner_in, corner_out):
        ref[...] = jnp.zeros(ref.shape, jnp.float32)

    def whole(ref, send_sem, recv_sem):
        part = ref.at[pl.ds(0, count - 1)]
        return pltpu.make_async_remote_copy(
            src_ref=part,
            dst_ref=part,
            send_sem=send_sem,
            recv_sem=recv_sem,
            device_id=(wide, narrow),
            device_id_type=MESH,
        )

    rows = BS * BS * BS // 128
    for f in range(FIELDS):
        loads[f].wait()
        for g in range(blocks // 8):
            for j in range(rows):
                lined[pl.ds(g * 8 * rows + j, 8, stride=rows), :] = raw[
                    f, g * 8 : g * 8 + 8, j * 128 : j * 128 + 128
                ]
        mine[f] = lined[...].reshape(blocks, rows, 128)

    whole(table, table_sems.at[0], table_sems.at[1]).wait_recv()
    to_scalar = pltpu.make_async_copy(table, table_smem, small_sem)
    to_scalar.start()
    to_scalar.wait()

    def wanted(d):
        return table_smem[d, 0, me]

    def send_field(f):
        def send(w, n):
            d = w * narrow_count + n
            stages[f][d] = mine[f, wanted(d)]
            pltpu.make_async_remote_copy(
                src_ref=stages[f].at[d],
                dst_ref=lands[f].at[me],
                send_sem=data_send.at[f],
                recv_sem=data_recv.at[f],
                device_id=(w, n),
                device_id_type=MESH,
            ).start()

        others(send)
        lands[f][me] = mine[f, my_own]

    for f in range(AHEAD):
        send_field(f)

    for load in loads[FIELDS:]:
        load.wait()
    tracers = attr.shape[1]
    chunk = 1024 if tracers % 1024 == 0 else tracers
    means = bin_sums(me * blocks, holder, voxel, attr, blocks, chunk)
    left = lax.broadcasted_iota(jnp.int32, (8, 128), 1) < BINS
    for q in range(blocks // 2):
        pair = means[:, q * 128 : q * 128 + 128]
        across = pltpu.roll(pair, BINS, 1)
        below = pltpu.roll(pair, 4, 0)
        both = pltpu.roll(across, 4, 0)
        mean_mine[2 * q] = jnp.where(left, pair, both)[:4]
        mean_mine[2 * q + 1] = jnp.where(left, across, below)[:4]

    def send_mean(w, n):
        d = w * narrow_count + n
        mean_stage[d] = mean_mine[wanted(d)]
        pltpu.make_async_remote_copy(
            src_ref=mean_stage.at[d],
            dst_ref=mean_land.at[me],
            send_sem=mean_sems.at[0],
            recv_sem=mean_sems.at[1],
            device_id=(w, n),
            device_id_type=MESH,
        ).start()

    others(send_mean)
    mean_land[me] = mean_mine[my_own]

    def source_of(y, z):
        return lax.div(slot_ref[y * LZ + z], blocks)

    def grid_part(f, y):
        for z in range(LZ):
            held[pl.ds(z, rows, stride=LZ), :] = lands[f][source_of(y, z)]
        return swap_groups(held[...].reshape(rows, LZ, 128)).reshape(BS, BS, 128)

    ways = ((-1, 0), (1, 0), (0, -1), (0, 1), (-1, -1), (-1, 1), (1, -1), (1, 1))
    low_side = {-1: (wide > 0, narrow > 0), 1: (wide < wide_count - 1, narrow < narrow_count - 1)}

    def exists(way):
        there = [low_side[step][axis] for axis, step in enumerate(way) if step]
        return there[0] if len(there) == 1 else there[0] & there[1]

    def row_of(x, y):
        return (x + DEEP) * PITCH + FIRST + y

    def grid_rows(g, at):
        if g < 2:
            return (warm, eta)[g].at[at]
        return pad_ref.at[g - 2, at]

    def depth_of(g):
        return DEEP - 1 if g == 0 else DEEP

    def messages(g):
        found = []
        for i in range(DEEP):
            for way, slot in ((-1, i), (1, DEEP + i)):
                mine_x, theirs_x = (i, nx + i) if way < 0 else (nx - DEEP + i, i - DEEP)
                here_x = i - DEEP if way < 0 else nx + i
                rows_at = [
                    grid_rows(g, pl.ds(row_of(x, 0), ny)) for x in (mine_x, theirs_x, here_x)
                ]
                found.append(
                    ((way, 0), slot, rows_at[0], rows_at[1], (slot + DEEP) % (2 * DEEP), rows_at[2])
                )
        deep = pl.ds(0, depth_of(g))
        for side, way in enumerate((-1, 1)):
            slot = 2 * DEEP + side
            found.append(
                (
                    (0, way), slot, edge_out.at[g, side, deep], edge_in.at[g, 1 - side, deep],
                    2 * DEEP + 1 - side, edge_in.at[g, side, deep],
                )
            )
        for c, way in enumerate(ways[4:]):
            found.append(
                (
                    way, 2 * DEEP + 2 + c, corner_out.at[g, c], corner_in.at[g, 3 - c],
                    2 * DEEP + 5 - c, corner_in.at[g, c],
                )
            )
        return found

    def each_message(g, act):
        for way in ways:
            group = [m for m in messages(g) if m[0] == way]

            @pl.when(exists(way))
            def _(way=way, group=group):
                for _, slot, source, target, far_slot, here in group:
                    act(way, slot, source, target, far_slot, here)

    def start_message(g):
        def act(way, slot, source, target, far_slot, here):
            pltpu.make_async_remote_copy(
                src_ref=source, dst_ref=target,
                send_sem=halo_send.at[g, slot], recv_sem=halo_recv.at[g, far_slot],
                device_id=(wide + way[0], narrow + way[1]), device_id_type=MESH,
            ).start()

        return act

    def wait_message(g, sent):
        def act(way, slot, source, target, far_slot, here):
            copy = pltpu.make_async_remote_copy(
                src_ref=source if sent else here, dst_ref=target if sent else here,
                send_sem=halo_send.at[g, slot], recv_sem=halo_recv.at[g, slot],
                device_id=(wide + way[0], narrow + way[1]), device_id_type=MESH,
            )
            copy.wait_send() if sent else copy.wait_recv()

        return act

    def read_rows(g, at):
        return (warm, eta)[g][at, :] if g < 2 else pad_ref[g - 2, at, :]

    def write_rows(g, at, value):
        if g < 2:
            (warm, eta)[g][at, :] = value
        else:
            pad_ref[g - 2, at, :] = value

    def send_halo(g):
        depth = depth_of(g)
        for side in range(2):
            for i in range(depth):
                y = i if side == 0 else ny - depth + i
                edge_out[g, side, i] = read_rows(g, pl.ds(row_of(0, y), nx, stride=PITCH))
        for c, (dx, dy) in enumerate(ways[4:]):
            for i in range(2):
                x = i if dx < 0 else nx - 2 + i
                y = 0 if dy < 0 else ny - 2
                corner_out[g, c, 2 * i : 2 * i + 2, :] = read_rows(g, pl.ds(row_of(x, y), 2))
        each_message(g, start_message(g))

    def take_halo(g):
        depth = depth_of(g)
        each_message(g, wait_message(g, False))
        for side in range(2):
            for i in range(depth):
                y = i - depth if side == 0 else ny + i
                write_rows(g, pl.ds(row_of(0, y), nx, stride=PITCH), edge_in[g, side, i])
        for c, (dx, dy) in enumerate(ways[4:]):
            for i in range(2):
                x = i - 2 if dx < 0 else nx + i
                y = -2 if dy < 0 else ny
                write_rows(g, pl.ds(row_of(x, y), 2), corner_in[g, c, 2 * i : 2 * i + 2, :])

    def viscosity():
        whole(mean_land, mean_sems.at[0], mean_sems.at[1]).wait_recv()
        expand = (
            lax.broadcasted_iota(jnp.int32, (LZ, 32), 0)
            == lax.broadcasted_iota(jnp.int32, (LZ, 32), 1) // 4
        ).astype(jnp.float32)
        same = (
            lax.broadcasted_iota(jnp.int32, (128, 32), 0) % 4
            == lax.broadcasted_iota(jnp.int32, (128, 32), 1) % 4
        )
        gather = (
            lax.broadcasted_iota(jnp.int32, (32, 128), 0)
            == lax.broadcasted_iota(jnp.int32, (32, 128), 1) // 4
        ).astype(jnp.float32)
        for y in range(LY):
            for z in range(LZ):
                mean_held[pl.ds(z, 4, stride=LZ), :] = mean_land[source_of(y, z)]
            for p in range(4):
                tall = jnp.dot(
                    mean_held[p * LZ : p * LZ + LZ].T, expand,
                    precision=lax.Precision.HIGHEST, preferred_element_type=jnp.float32,
                )
                cells = jnp.dot(
                    gather, jnp.where(same, tall, 0.0),
                    precision=lax.Precision.HIGHEST, preferred_element_type=jnp.float32,
                )
                for half in range(2):
                    for layer in range(4):
                        at = half * 16 + layer * 4
                        mean_ref[half * 4 + p, layer, y * 4 : y * 4 + 4, :] = cells[at : at + 4]
        for layer in range(4):
            mixture = MIX_WEIGHTS[0] * mean_ref[0, layer]
            for p in range(1, len(MIX_WEIGHTS)):
                mixture = mixture + MIX_WEIGHTS[p] * mean_ref[p, layer]
            wide_mix = jnp.dot(
                mixture, gather,
                precision=lax.Precision.HIGHEST, preferred_element_type=jnp.float32,
            )
            spread = jnp.concatenate(
                [jnp.broadcast_to(wide_mix[j : j + 1], (4, 128)) for j in range(LY * 4)], axis=0
            )
            for x in range(layer * 4, layer * 4 + 4):
                eta[pl.ds(row_of(x, 0), ny), :] = drag_grid[x] * jnp.exp(
                    HEAT_FACTOR * (0.5 - heat_ref[x]) + spread
                )

    wide_rows = (PITCH, (nx + 2 * DEEP - 1) * PITCH)

    def factor_rows(base):
        factors(base, STEP, eta, warm, side_ref, rest_ref)

    def drift_rows(base):
        found = drift(base, STEP, pad_ref, side_ref, rest_ref)
        for k in range(4):
            part_ref[k, pl.ds(base, STEP), :] = found[k]

    for f in range(FIELDS):
        whole(lands[f], data_send.at[f], data_recv.at[f]).wait_recv()
        if f + AHEAD < FIELDS:
            send_field(f + AHEAD)
        for y in range(LY):
            at = slice(y * BS, (y + 1) * BS)
            part = grid_part(f, y)
            if f == 0:
                heat_ref[:, at, :] = part
            if f == 1:
                drag_grid[:, at, :] = part
            else:
                for x in range(nx):
                    write_rows(f, pl.ds(row_of(x, y * BS), BS), part[x])
        if f == 1:
            viscosity()
        send_halo(f)
        if f == 3:
            take_halo(0)
            take_halo(1)
            over_rows(*wide_rows, 10, factor_rows)
    for f in range(2, FIELDS - 1):
        take_halo(f)
    over_rows(*wide_rows, DRIFT_TURNS, drift_rows)
    take_halo(FIELDS - 1)

    whole(table, table_sems.at[0], table_sems.at[1]).wait_send()
    whole(mean_land, mean_sems.at[0], mean_sems.at[1]).wait_send()
    for f in range(FIELDS):
        whole(lands[f], data_send.at[f], data_recv.at[f]).wait_send()
    for f in range(FIELDS):
        each_message(f, wait_message(f, True))


def migrate(slots, flow, stress, heat, drag, attributes, holder, voxel):
    wide_count, narrow_count = lax.axis_size("wide"), lax.axis_size("narrow")
    count = wide_count * narrow_count
    blocks = slots.shape[0]
    tracers = attributes.shape[1]
    nx, ny, nz = LX * BS, LY * BS, LZ * BS
    rows = BS * BS * BS // 128
    pad_rows = (nx + 2 * DEEP) * PITCH + 8
    vmem = pl.BlockSpec(memory_space=pltpu.VMEM)
    hbm = pl.BlockSpec(memory_space=pltpu.HBM)
    f32 = jnp.float32
    per_field = [pltpu.VMEM((count, rows, 128), f32)] * FIELDS
    dma = pltpu.SemaphoreType.DMA
    pinned = [
        pltpu.with_memory_space_constraint(array, pltpu.HBM)
        for array in (slots, flow, stress, heat, drag, attributes, holder, voxel)
    ]
    return pl.pallas_call(
        functools.partial(migrate_kernel, wide_count=wide_count, narrow_count=narrow_count),
        out_shape=(
            jax.ShapeDtypeStruct((4, pad_rows, nz), f32),
            jax.ShapeDtypeStruct((4, pad_rows, nz), f32),
            jax.ShapeDtypeStruct((6, pad_rows, nz), f32),
            jax.ShapeDtypeStruct((3, pad_rows, nz), f32),
            jax.ShapeDtypeStruct((nx, ny, nz), f32),
            jax.ShapeDtypeStruct((8, LX * 4, LY * 4, LZ * 4), f32),
        ),
        in_specs=[hbm] * 8,
        out_specs=(vmem,) * 6,
        scratch_shapes=[
            pltpu.SMEM((blocks,), jnp.int32),
            pltpu.VMEM((1, 128), jnp.int32),
            pltpu.VMEM((count, 1, 128), jnp.int32),
            pltpu.SMEM((count, 1, 128), jnp.int32),
            pltpu.VMEM((FIELDS, blocks, rows * 128), f32),
            pltpu.VMEM((blocks * rows, 128), f32),
            pltpu.VMEM((FIELDS, blocks, rows, 128), f32),
            *per_field,
            *per_field,
            pltpu.VMEM((8, tracers), f32),
            pltpu.VMEM((1, tracers), jnp.int32),
            pltpu.VMEM((1, tracers), jnp.int32),
            pltpu.VMEM((blocks, 4, 128), f32),
            pltpu.VMEM((count, 4, 128), f32),
            pltpu.VMEM((count, 4, 128), f32),
            pltpu.VMEM((4 * LZ, 128), f32),
            pltpu.VMEM((rows * LZ, 128), f32),
            pltpu.VMEM((nx, ny, nz), f32),
            pltpu.VMEM((pad_rows, nz), f32),
            pltpu.VMEM((pad_rows, nz), f32),
            pltpu.VMEM((FIELDS, 2, DEEP, nx, nz), f32),
            pltpu.VMEM((FIELDS, 2, DEEP, nx, nz), f32),
            pltpu.VMEM((FIELDS, 4, 8, nz), f32),
            pltpu.VMEM((FIELDS, 4, 8, nz), f32),
            dma((FIELDS + 3,)),
            dma((2,)),
            dma((FIELDS,)),
            dma((FIELDS,)),
            dma((2,)),
            dma((FIELDS, 2 * DEEP + 6)),
            dma((FIELDS, 2 * DEEP + 6)),
            dma(()),
        ],
        compiler_params=pltpu.CompilerParams(
            collective_id=1,
            has_side_effects=True,
            vmem_limit_bytes=(24 if count <= 32 else 44) * 1024 * 1024,
        ),
    )(*pinned)


def relax_kernel(
    pad_ref, part_ref, side_ref, rest_ref, heat_ref, mean_ref,
    velocity_ref, pressure_ref, heat_out_ref, mean_out_ref, pad_1, pad_2, fresh, sems,
):
    nx, ny, nz = heat_ref.shape
    copies = []

    def send(source, target):
        copies.append(pltpu.make_async_copy(source, target, sems.at[len(copies)]))
        copies[-1].start()

    send(heat_ref, heat_out_ref)
    send(mean_ref, mean_out_ref)

    def finish_first(base):
        drifted = [part_ref[k, pl.ds(base, STEP), :] for k in range(4)]
        moved = push(base, STEP, pad_ref, rest_ref, drifted)
        for k in range(4):
            pad_1[k, pl.ds(base, STEP), :] = moved[k]

    def second(base):
        moved = relax(base, STEP, pad_1, side_ref, rest_ref)
        for k in range(4):
            pad_2[k, pl.ds(base, STEP), :] = moved[k]

    slabs = nx + 2 * DEEP
    over_rows(PITCH, (slabs - 1) * PITCH, TURNS, finish_first)
    over_rows(2 * PITCH, (slabs - 2) * PITCH, TURNS, second)

    parts = 4
    thick = nx // parts
    for part in range(parts):
        for x in range(part * thick, (part + 1) * thick):
            for half in range(0, ny, STEP):
                base = (x + DEEP) * PITCH + FIRST + half
                moved = relax(base, STEP, pad_2, side_ref, rest_ref)
                for k in range(4):
                    fresh[k, x, half : half + STEP, :] = moved[k]
        at = pl.ds(part * thick, thick)
        send(fresh.at[pl.ds(0, 3), at], velocity_ref.at[:, at])
        send(fresh.at[3, at], pressure_ref.at[at])
    for copy in copies:
        copy.wait()


def relax_all(pad, part, side, rest, heat, means):
    nx, ny, nz = heat.shape
    vmem = pl.BlockSpec(memory_space=pltpu.VMEM)
    hbm = pl.BlockSpec(memory_space=pltpu.HBM)
    return pl.pallas_call(
        relax_kernel,
        out_shape=(
            jax.ShapeDtypeStruct((3, nx, ny, nz), jnp.float32),
            jax.ShapeDtypeStruct((nx, ny, nz), jnp.float32),
            jax.ShapeDtypeStruct(heat.shape, jnp.float32),
            jax.ShapeDtypeStruct(means.shape, jnp.float32),
        ),
        in_specs=[vmem] * 6,
        out_specs=(hbm,) * 4,
        scratch_shapes=[
            pltpu.VMEM(pad.shape, jnp.float32),
            pltpu.VMEM(pad.shape, jnp.float32),
            pltpu.VMEM((4, nx, ny, nz), jnp.float32),
            pltpu.SemaphoreType.DMA((10,)),
        ],
        compiler_params=pltpu.CompilerParams(vmem_limit_bytes=16 * 1024 * 1024),
    )(pad, part, side, rest, heat, means)


def per_device(
    tile_flow_speed,
    tile_stress_mean,
    tile_heat_state,
    tile_drag_coefficient,
    marker_attributes,
    marker_holding_tile,
    marker_voxel_number,
    prior_slot_of_tile,
):
    tracers = marker_attributes.shape[1]
    results = migrate(
        prior_slot_of_tile,
        tile_flow_speed.transpose(1, 0, 2),
        tile_stress_mean,
        tile_heat_state,
        tile_drag_coefficient,
        marker_attributes,
        marker_holding_tile.reshape(1, tracers),
        marker_voxel_number.reshape(1, tracers),
    )
    return relax_all(*results)


def solution(mesh):
    in_specs = (
        P(("wide", "narrow"), None, None),
        P(("wide", "narrow"), None),
        P(("wide", "narrow"), None),
        P(("wide", "narrow"), None),
        P(None, ("wide", "narrow")),
        P(("wide", "narrow")),
        P(("wide", "narrow")),
        P(("wide", "narrow")),
    )
    out_specs = (
        P(None, "wide", "narrow", None),
        P("wide", "narrow", None),
        P("wide", "narrow", None),
        P(None, "wide", "narrow", None),
    )
    return jax.shard_map(
        per_device, mesh=mesh, in_specs=in_specs, out_specs=out_specs, check_vma=False
    )
```

```python
import functools

import jax
import jax.numpy as jnp
from jax import lax
from jax.experimental import pallas as pl
from jax.experimental.pallas import tpu as pltpu
from jax.sharding import PartitionSpec as P

BS = 16
LX = 1
LY = 2
LZ = 8
SWEEPS = 3
BINS = 64
FIELDS = 6
AHEAD = 3
PITCH = 40
FIRST = 8
DEEP = 3
STEP = 16
TURNS = 1
DRIFT_TURNS = 5

MIX_WEIGHTS = (0.3, -0.25, 0.2, -0.15, 0.35, -0.3, 0.25, -0.2)
RELAX_WEIGHT = 0.7
PRESSURE_WEIGHT = 0.3
HEAT_FACTOR = 2.0
DENSITY_FACTOR = 4.0
MESH = pl.DeviceIdType.MESH


def swap_groups(x):
    row = lax.broadcasted_iota(jnp.int32, x.shape, 1)
    group = lax.broadcasted_iota(jnp.int32, x.shape, 2) // BS
    for bit in (1, 2, 4):
        row_set = (row & bit) != 0
        group_set = (group & bit) != 0
        from_above = pltpu.roll(pltpu.roll(x, 8 - bit, 1), BS * bit, 2)
        from_below = pltpu.roll(pltpu.roll(x, bit, 1), 8 * BS - BS * bit, 2)
        x = jnp.where(
            row_set == group_set, x, jnp.where(group_set, from_above, from_below)
        )
    return x


def bin_sums(base, holder_ref, voxel_ref, attr_ref, blocks, chunk):
    props, tracers = attr_ref.shape
    total_bins = blocks * BINS
    bin_ids = lax.broadcasted_iota(jnp.int32, (total_bins, chunk), 0)

    def step(turn, sums):
        at = pl.ds(pl.multiple_of(turn * chunk, chunk), chunk)
        voxel = voxel_ref[:, at]
        key = (
            (holder_ref[:, at] - base) * BINS
            + (voxel >> 10) * 16
            + ((voxel >> 6) & 3) * 4
            + ((voxel >> 2) & 3)
        )
        table = jnp.where(bin_ids == key, 1.0, 0.0).astype(jnp.bfloat16)
        values = attr_ref[:, at]
        high = values.astype(jnp.bfloat16)
        rest = values - high.astype(jnp.float32)
        middle = rest.astype(jnp.bfloat16)
        low = (rest - middle.astype(jnp.float32)).astype(jnp.bfloat16)
        ones = jnp.ones((props, chunk), jnp.bfloat16)
        rows = jnp.concatenate([high, middle, low, ones], axis=0)
        return sums + lax.dot_general(
            rows, table, (((1,), (1,)), ((), ())), preferred_element_type=jnp.float32
        )

    sums = lax.fori_loop(
        0, tracers // chunk, step, jnp.zeros((4 * props, total_bins), jnp.float32)
    )
    total = sums[:props] + sums[props : 2 * props] + sums[2 * props : 3 * props]
    return total / jnp.maximum(sums[3 * props :], 1.0)


def at_ends(shape):
    column = lax.broadcasted_iota(jnp.int32, shape, 1)
    return column == 0, column == shape[1] - 1


def z_pair(here):
    low_end, high_end = at_ends(here.shape)
    nz = here.shape[1]
    return (
        jnp.where(high_end, 0.0, pltpu.roll(here, nz - 1, 1)),
        jnp.where(low_end, 0.0, pltpu.roll(here, 1, 1)),
    )


def factors(base, rows, eta_ref, heat_ref, side_ref, rest_ref):
    here = eta_ref[pl.ds(base, rows), :]
    around = [
        eta_ref[pl.ds(base + off, rows), :] for off in (PITCH, -PITCH, 1, -1)
    ] + list(z_pair(here))
    face = [0.5 * (here + other) for other in around]
    diagonal = face[0]
    for m in range(1, 6):
        diagonal = diagonal + face[m]
    inside = here > 0.0
    scale = jnp.where(inside, RELAX_WEIGHT / jnp.where(inside, diagonal, 1.0), 0.0)
    low_end, high_end = at_ends(here.shape)
    own = pl.ds(base, rows)
    for m in range(6):
        value = face[m] * scale
        if m == 4:
            value = jnp.where(high_end, 0.0, value)
        elif m == 5:
            value = jnp.where(low_end, 0.0, value)
        side_ref[m, own, :] = value
    rest_ref[0, own, :] = 0.5 * scale
    rest_ref[1, own, :] = (0.5 * PRESSURE_WEIGHT) * here
    rest_ref[2, own, :] = scale * (DENSITY_FACTOR * heat_ref[own, :])


def drift(base, rows, pad, side_ref, rest_ref):
    nz = pad.shape[2]
    own = pl.ds(base, rows)

    def value(k, off=0):
        return pad[k, pl.ds(base + off, rows), :]

    side = [side_ref[m, own, :] for m in range(6)]
    found = []
    divergence = None
    for k in range(3):
        here = value(k)
        if k == 2:
            up_z, down_z = z_pair(here)
        else:
            up_z, down_z = pltpu.roll(here, nz - 1, 1), pltpu.roll(here, 1, 1)
        near = (
            value(k, PITCH), value(k, -PITCH), value(k, 1), value(k, -1), up_z, down_z,
        )
        fresh = (1.0 - RELAX_WEIGHT) * here
        for m in range(6):
            fresh = fresh + side[m] * near[m]
        if k == 2:
            fresh = fresh + rest_ref[2, own, :]
        found.append(fresh)
        flux = near[2 * k] - near[2 * k + 1]
        divergence = flux if divergence is None else divergence + flux
    found.append(rest_ref[1, own, :] * divergence)
    return found


def push(base, rows, pad, rest_ref, drifted):
    own = pl.ds(base, rows)

    def value(off=0):
        return pad[3, pl.ds(base + off, rows), :]

    press = value()
    up_z, down_z = z_pair(press)
    half_scale = rest_ref[0, own, :]
    drops = (value(PITCH) - value(-PITCH), value(1) - value(-1), up_z - down_z)
    return [drifted[k] - half_scale * drops[k] for k in range(3)] + [press - drifted[3]]


def relax(base, rows, pad, side_ref, rest_ref):
    return push(base, rows, pad, rest_ref, drift(base, rows, pad, side_ref, rest_ref))


def over_rows(first, last, turns, act):
    together = (last - first) // (STEP * turns)
    assert together * STEP * turns == last - first

    def step(turn, carry):
        for i in range(together):
            act(pl.multiple_of(first + (turn * together + i) * STEP, 8))
        return carry

    lax.fori_loop(0, turns, step, 0)


def migrate_kernel(
    places_ref, flow_ref, stress_ref, warm_ref, drag_ref, attr_ref, holder_ref, voxel_ref,
    pad_ref, part_ref, side_ref, rest_ref, heat_ref, mean_ref,
    slot_ref, row_ref, table, table_smem, raw, lined, mine, stage_0, stage_1, stage_2, stage_3, stage_4, stage_5,
    land_0, land_1, land_2, land_3, land_4, land_5,
    attr, holder, voxel, mean_mine, mean_stage, mean_land, mean_held, held, drag_grid,
    eta, warm, edge_in, edge_out, corner_in, corner_out,
    raw_sems, table_send, table_recv, data_send, data_recv, mean_sems,
    halo_send, halo_recv, small_sem,
    *, wide_count, narrow_count,
):
    count = wide_count * narrow_count
    wide, narrow = lax.axis_index("wide"), lax.axis_index("narrow")
    me = wide * narrow_count + narrow
    blocks = raw.shape[1]
    nx, ny, nz = heat_ref.shape
    stages = (stage_0, stage_1, stage_2, stage_3, stage_4, stage_5)
    lands = (land_0, land_1, land_2, land_3, land_4, land_5)

    to_slots = pltpu.make_async_copy(places_ref, slot_ref, small_sem)
    to_slots.start()
    def flipped(k):
        place, bit = narrow, 1
        while bit < narrow_count:
            if k & bit:
                place = place + bit * (1 - 2 * lax.rem(lax.div(narrow, bit), 2))
            bit *= 2
        return place

    middle = narrow_count // 2
    upper = lax.div(narrow, middle)
    across = [(middle + i) * (1 - upper) + (middle - 1 - i) * upper for i in range(middle)]
    planes = across + [flipped(k) for k in range(1, middle)] + [narrow]
    farthest_first = across[::-1] + planes[middle:]

    def to_plane(plane, act):
        def step(a, carry):
            act(lax.rem(wide + a, wide_count), plane)
            return carry

        lax.fori_loop(1 if plane is narrow else 0, wide_count, step, 0)

    def others(act, order=planes):
        for plane in order:
            to_plane(plane, act)

    barrier = pltpu.get_barrier_semaphore()
    others(
        lambda w, n: pl.semaphore_signal(
            barrier, inc=1, device_id=(w, n), device_id_type=MESH
        ),
        farthest_first,
    )

    sources = (
        warm_ref, drag_ref, flow_ref.at[0], flow_ref.at[1], flow_ref.at[2], stress_ref,
    )
    loads = [
        pltpu.make_async_copy(source, raw.at[f], raw_sems.at[f]) for f, source in enumerate(sources)
    ]
    loads.append(pltpu.make_async_copy(attr_ref, attr, raw_sems.at[FIELDS]))
    loads.append(pltpu.make_async_copy(holder_ref, holder, raw_sems.at[FIELDS + 1]))
    loads.append(pltpu.make_async_copy(voxel_ref, voxel, raw_sems.at[FIELDS + 2]))
    for load in loads:
        load.start()

    to_slots.wait()
    lane = lax.broadcasted_iota(jnp.int32, (1, 128), 1)
    places = jnp.zeros((1, 128), jnp.int32)
    my_own = jnp.int32(0)
    for r in range(blocks):
        owner = lax.div(slot_ref[r], blocks)
        local = slot_ref[r] - owner * blocks
        places = jnp.where(lane == owner, local, places)
        my_own = jnp.where(owner == me, local, my_own)
    row_ref[...] = places
    table[narrow * wide_count + wide] = places
    pl.semaphore_wait(barrier, count - 1)

    def send_row(w, n):
        pltpu.make_async_remote_copy(
            src_ref=row_ref,
            dst_ref=table.at[narrow * wide_count + wide],
            send_sem=table_send,
            recv_sem=table_recv.at[narrow],
            device_id=(w, n),
            device_id_type=MESH,
        ).start()

    others(send_row)

    for ref in (pad_ref, eta, warm, edge_in, corner_in, corner_out):
        ref[...] = jnp.zeros(ref.shape, jnp.float32)

    def whole(ref, send_sem, recv_sem):
        part = ref.at[pl.ds(0, count - 1)]
        return pltpu.make_async_remote_copy(
            src_ref=part,
            dst_ref=part,
            send_sem=send_sem,
            recv_sem=recv_sem,
            device_id=(wide, narrow),
            device_id_type=MESH,
        )

    rows = BS * BS * BS // 128
    for f in range(FIELDS):
        loads[f].wait()
        for g in range(blocks // 8):
            for j in range(rows):
                lined[pl.ds(g * 8 * rows + j, 8, stride=rows), :] = raw[
                    f, g * 8 : g * 8 + 8, j * 128 : j * 128 + 128
                ]
        mine[f] = lined[...].reshape(blocks, rows, 128)

    def take_rows(plane):
        rows_at = pl.ds(plane * wide_count, wide_count - 1 if plane is narrow else wide_count)
        part = table.at[rows_at]
        pltpu.make_async_remote_copy(
            src_ref=part, dst_ref=part, send_sem=table_send, recv_sem=table_recv.at[plane],
            device_id=(wide, narrow), device_id_type=MESH,
        ).wait_recv()
        rows_at = pl.ds(plane * wide_count, wide_count)
        to_scalar = pltpu.make_async_copy(table.at[rows_at], table_smem.at[rows_at], small_sem)
        to_scalar.start()
        to_scalar.wait()

    def wanted(w, n):
        return table_smem[n * wide_count + w, 0, me]

    def send_part(f):
        def send(w, n):
            d = w * narrow_count + n
            stages[f][d] = mine[f, wanted(w, n)]
            pltpu.make_async_remote_copy(
                src_ref=stages[f].at[d],
                dst_ref=lands[f].at[me],
                send_sem=data_send.at[f],
                recv_sem=data_recv.at[f],
                device_id=(w, n),
                device_id_type=MESH,
            ).start()

        return send

    def send_field(f):
        others(send_part(f))
        lands[f][me] = mine[f, my_own]

    for plane in planes:
        take_rows(plane)
        to_plane(plane, send_part(0))
    lands[0][me] = mine[0, my_own]
    for f in range(1, AHEAD):
        send_field(f)

    for load in loads[FIELDS:]:
        load.wait()
    tracers = attr.shape[1]
    chunk = 1024 if tracers % 1024 == 0 else tracers
    means = bin_sums(me * blocks, holder, voxel, attr, blocks, chunk)
    left = lax.broadcasted_iota(jnp.int32, (8, 128), 1) < BINS
    for q in range(blocks // 2):
        pair = means[:, q * 128 : q * 128 + 128]
        across = pltpu.roll(pair, BINS, 1)
        below = pltpu.roll(pair, 4, 0)
        both = pltpu.roll(across, 4, 0)
        mean_mine[2 * q] = jnp.where(left, pair, both)[:4]
        mean_mine[2 * q + 1] = jnp.where(left, across, below)[:4]

    def send_mean(w, n):
        d = w * narrow_count + n
        mean_stage[d] = mean_mine[wanted(w, n)]
        pltpu.make_async_remote_copy(
            src_ref=mean_stage.at[d],
            dst_ref=mean_land.at[me],
            send_sem=mean_sems.at[0],
            recv_sem=mean_sems.at[1],
            device_id=(w, n),
            device_id_type=MESH,
        ).start()

    others(send_mean)
    mean_land[me] = mean_mine[my_own]

    def source_of(y, z):
        return lax.div(slot_ref[y * LZ + z], blocks)

    def grid_part(f, y):
        for z in range(LZ):
            held[pl.ds(z, rows, stride=LZ), :] = lands[f][source_of(y, z)]
        return swap_groups(held[...].reshape(rows, LZ, 128)).reshape(BS, BS, 128)

    ways = ((-1, 0), (1, 0), (0, -1), (0, 1), (-1, -1), (-1, 1), (1, -1), (1, 1))
    low_side = {-1: (wide > 0, narrow > 0), 1: (wide < wide_count - 1, narrow < narrow_count - 1)}

    def exists(way):
        there = [low_side[step][axis] for axis, step in enumerate(way) if step]
        return there[0] if len(there) == 1 else there[0] & there[1]

    def row_of(x, y):
        return (x + DEEP) * PITCH + FIRST + y

    def grid_rows(g, at):
        if g < 2:
            return (warm, eta)[g].at[at]
        return pad_ref.at[g - 2, at]

    def depth_of(g):
        return DEEP - 1 if g == 0 else DEEP

    def messages(g):
        found = []
        for i in range(DEEP):
            for way, slot in ((-1, i), (1, DEEP + i)):
                mine_x, theirs_x = (i, nx + i) if way < 0 else (nx - DEEP + i, i - DEEP)
                here_x = i - DEEP if way < 0 else nx + i
                rows_at = [
                    grid_rows(g, pl.ds(row_of(x, 0), ny)) for x in (mine_x, theirs_x, here_x)
                ]
                found.append(
                    ((way, 0), slot, rows_at[0], rows_at[1], (slot + DEEP) % (2 * DEEP), rows_at[2])
                )
        deep = pl.ds(0, depth_of(g))
        for side, way in enumerate((-1, 1)):
            slot = 2 * DEEP + side
            found.append(
                (
                    (0, way), slot, edge_out.at[g, side, deep], edge_in.at[g, 1 - side, deep],
                    2 * DEEP + 1 - side, edge_in.at[g, side, deep],
                )
            )
        for c, way in enumerate(ways[4:]):
            found.append(
                (
                    way, 2 * DEEP + 2 + c, corner_out.at[g, c], corner_in.at[g, 3 - c],
                    2 * DEEP + 5 - c, corner_in.at[g, c],
                )
            )
        return found

    def each_message(g, act):
        for way in ways:
            group = [m for m in messages(g) if m[0] == way]

            @pl.when(exists(way))
            def _(way=way, group=group):
                for _, slot, source, target, far_slot, here in group:
                    act(way, slot, source, target, far_slot, here)

    def start_message(g):
        def act(way, slot, source, target, far_slot, here):
            pltpu.make_async_remote_copy(
                src_ref=source, dst_ref=target,
                send_sem=halo_send.at[g, slot], recv_sem=halo_recv.at[g, far_slot],
                device_id=(wide + way[0], narrow + way[1]), device_id_type=MESH,
            ).start()

        return act

    def wait_message(g, sent):
        def act(way, slot, source, target, far_slot, here):
            copy = pltpu.make_async_remote_copy(
                src_ref=source if sent else here, dst_ref=target if sent else here,
                send_sem=halo_send.at[g, slot], recv_sem=halo_recv.at[g, slot],
                device_id=(wide + way[0], narrow + way[1]), device_id_type=MESH,
            )
            copy.wait_send() if sent else copy.wait_recv()

        return act

    def read_rows(g, at):
        return (warm, eta)[g][at, :] if g < 2 else pad_ref[g - 2, at, :]

    def write_rows(g, at, value):
        if g < 2:
            (warm, eta)[g][at, :] = value
        else:
            pad_ref[g - 2, at, :] = value

    def send_halo(g):
        depth = depth_of(g)
        for side in range(2):
            for i in range(depth):
                y = i if side == 0 else ny - depth + i
                edge_out[g, side, i] = read_rows(g, pl.ds(row_of(0, y), nx, stride=PITCH))
        for c, (dx, dy) in enumerate(ways[4:]):
            for i in range(2):
                x = i if dx < 0 else nx - 2 + i
                y = 0 if dy < 0 else ny - 2
                corner_out[g, c, 2 * i : 2 * i + 2, :] = read_rows(g, pl.ds(row_of(x, y), 2))
        each_message(g, start_message(g))

    def take_halo(g):
        depth = depth_of(g)
        each_message(g, wait_message(g, False))
        for side in range(2):
            for i in range(depth):
                y = i - depth if side == 0 else ny + i
                write_rows(g, pl.ds(row_of(0, y), nx, stride=PITCH), edge_in[g, side, i])
        for c, (dx, dy) in enumerate(ways[4:]):
            for i in range(2):
                x = i - 2 if dx < 0 else nx + i
                y = -2 if dy < 0 else ny
                write_rows(g, pl.ds(row_of(x, y), 2), corner_in[g, c, 2 * i : 2 * i + 2, :])

    def viscosity():
        whole(mean_land, mean_sems.at[0], mean_sems.at[1]).wait_recv()
        expand = (
            lax.broadcasted_iota(jnp.int32, (LZ, 32), 0)
            == lax.broadcasted_iota(jnp.int32, (LZ, 32), 1) // 4
        ).astype(jnp.float32)
        same = (
            lax.broadcasted_iota(jnp.int32, (128, 32), 0) % 4
            == lax.broadcasted_iota(jnp.int32, (128, 32), 1) % 4
        )
        gather = (
            lax.broadcasted_iota(jnp.int32, (32, 128), 0)
            == lax.broadcasted_iota(jnp.int32, (32, 128), 1) // 4
        ).astype(jnp.float32)
        for y in range(LY):
            for z in range(LZ):
                mean_held[pl.ds(z, 4, stride=LZ), :] = mean_land[source_of(y, z)]
            for p in range(4):
                tall = jnp.dot(
                    mean_held[p * LZ : p * LZ + LZ].T, expand,
                    precision=lax.Precision.HIGHEST, preferred_element_type=jnp.float32,
                )
                cells = jnp.dot(
                    gather, jnp.where(same, tall, 0.0),
                    precision=lax.Precision.HIGHEST, preferred_element_type=jnp.float32,
                )
                for half in range(2):
                    for layer in range(4):
                        at = half * 16 + layer * 4
                        mean_ref[half * 4 + p, layer, y * 4 : y * 4 + 4, :] = cells[at : at + 4]
        for layer in range(4):
            mixture = MIX_WEIGHTS[0] * mean_ref[0, layer]
            for p in range(1, len(MIX_WEIGHTS)):
                mixture = mixture + MIX_WEIGHTS[p] * mean_ref[p, layer]
            wide_mix = jnp.dot(
                mixture, gather,
                precision=lax.Precision.HIGHEST, preferred_element_type=jnp.float32,
            )
            spread = jnp.concatenate(
                [jnp.broadcast_to(wide_mix[j : j + 1], (4, 128)) for j in range(LY * 4)], axis=0
            )
            for x in range(layer * 4, layer * 4 + 4):
                eta[pl.ds(row_of(x, 0), ny), :] = drag_grid[x] * jnp.exp(
                    HEAT_FACTOR * (0.5 - heat_ref[x]) + spread
                )

    wide_rows = (PITCH, (nx + 2 * DEEP - 1) * PITCH)

    def factor_rows(base):
        factors(base, STEP, eta, warm, side_ref, rest_ref)

    def drift_rows(base):
        found = drift(base, STEP, pad_ref, side_ref, rest_ref)
        for k in range(4):
            part_ref[k, pl.ds(base, STEP), :] = found[k]

    for f in range(FIELDS):
        whole(lands[f], data_send.at[f], data_recv.at[f]).wait_recv()
        if f + AHEAD < FIELDS:
            send_field(f + AHEAD)
        for y in range(LY):
            at = slice(y * BS, (y + 1) * BS)
            part = grid_part(f, y)
            if f == 0:
                heat_ref[:, at, :] = part
            if f == 1:
                drag_grid[:, at, :] = part
            else:
                for x in range(nx):
                    write_rows(f, pl.ds(row_of(x, y * BS), BS), part[x])
        if f == 1:
            viscosity()
        send_halo(f)
        if f == 3:
            take_halo(0)
            take_halo(1)
            over_rows(*wide_rows, 10, factor_rows)
    for f in range(2, FIELDS - 1):
        take_halo(f)
    over_rows(*wide_rows, DRIFT_TURNS, drift_rows)
    take_halo(FIELDS - 1)

    whole(table, table_send, table_recv.at[0]).wait_send()
    whole(mean_land, mean_sems.at[0], mean_sems.at[1]).wait_send()
    for f in range(FIELDS):
        whole(lands[f], data_send.at[f], data_recv.at[f]).wait_send()
    for f in range(FIELDS):
        each_message(f, wait_message(f, True))


def migrate(slots, flow, stress, heat, drag, attributes, holder, voxel):
    wide_count, narrow_count = lax.axis_size("wide"), lax.axis_size("narrow")
    count = wide_count * narrow_count
    blocks = slots.shape[0]
    tracers = attributes.shape[1]
    nx, ny, nz = LX * BS, LY * BS, LZ * BS
    rows = BS * BS * BS // 128
    pad_rows = (nx + 2 * DEEP) * PITCH + 8
    vmem = pl.BlockSpec(memory_space=pltpu.VMEM)
    hbm = pl.BlockSpec(memory_space=pltpu.HBM)
    f32 = jnp.float32
    per_field = [pltpu.VMEM((count, rows, 128), f32)] * FIELDS
    dma = pltpu.SemaphoreType.DMA
    pinned = [
        pltpu.with_memory_space_constraint(array, pltpu.HBM)
        for array in (slots, flow, stress, heat, drag, attributes, holder, voxel)
    ]
    return pl.pallas_call(
        functools.partial(migrate_kernel, wide_count=wide_count, narrow_count=narrow_count),
        out_shape=(
            jax.ShapeDtypeStruct((4, pad_rows, nz), f32),
            jax.ShapeDtypeStruct((4, pad_rows, nz), f32),
            jax.ShapeDtypeStruct((6, pad_rows, nz), f32),
            jax.ShapeDtypeStruct((3, pad_rows, nz), f32),
            jax.ShapeDtypeStruct((nx, ny, nz), f32),
            jax.ShapeDtypeStruct((8, LX * 4, LY * 4, LZ * 4), f32),
        ),
        in_specs=[hbm] * 8,
        out_specs=(vmem,) * 6,
        scratch_shapes=[
            pltpu.SMEM((blocks,), jnp.int32),
            pltpu.VMEM((1, 128), jnp.int32),
            pltpu.VMEM((count, 1, 128), jnp.int32),
            pltpu.SMEM((count, 1, 128), jnp.int32),
            pltpu.VMEM((FIELDS, blocks, rows * 128), f32),
            pltpu.VMEM((blocks * rows, 128), f32),
            pltpu.VMEM((FIELDS, blocks, rows, 128), f32),
            *per_field,
            *per_field,
            pltpu.VMEM((8, tracers), f32),
            pltpu.VMEM((1, tracers), jnp.int32),
            pltpu.VMEM((1, tracers), jnp.int32),
            pltpu.VMEM((blocks, 4, 128), f32),
            pltpu.VMEM((count, 4, 128), f32),
            pltpu.VMEM((count, 4, 128), f32),
            pltpu.VMEM((4 * LZ, 128), f32),
            pltpu.VMEM((rows * LZ, 128), f32),
            pltpu.VMEM((nx, ny, nz), f32),
            pltpu.VMEM((pad_rows, nz), f32),
            pltpu.VMEM((pad_rows, nz), f32),
            pltpu.VMEM((FIELDS, 2, DEEP, nx, nz), f32),
            pltpu.VMEM((FIELDS, 2, DEEP, nx, nz), f32),
            pltpu.VMEM((FIELDS, 4, 8, nz), f32),
            pltpu.VMEM((FIELDS, 4, 8, nz), f32),
            dma((FIELDS + 3,)),
            dma(()),
            dma((narrow_count,)),
            dma((FIELDS,)),
            dma((FIELDS,)),
            dma((2,)),
            dma((FIELDS, 2 * DEEP + 6)),
            dma((FIELDS, 2 * DEEP + 6)),
            dma(()),
        ],
        compiler_params=pltpu.CompilerParams(
            collective_id=1,
            has_side_effects=True,
            vmem_limit_bytes=(24 if count <= 32 else 44) * 1024 * 1024,
        ),
    )(*pinned)


def relax_kernel(
    pad_ref, part_ref, side_ref, rest_ref, heat_ref, mean_ref,
    velocity_ref, pressure_ref, heat_out_ref, mean_out_ref, pad_1, pad_2, fresh, sems,
):
    nx, ny, nz = heat_ref.shape
    copies = []

    def send(source, target):
        copies.append(pltpu.make_async_copy(source, target, sems.at[len(copies)]))
        copies[-1].start()

    send(heat_ref, heat_out_ref)
    send(mean_ref, mean_out_ref)

    def finish_first(base):
        drifted = [part_ref[k, pl.ds(base, STEP), :] for k in range(4)]
        moved = push(base, STEP, pad_ref, rest_ref, drifted)
        for k in range(4):
            pad_1[k, pl.ds(base, STEP), :] = moved[k]

    def second(base):
        moved = relax(base, STEP, pad_1, side_ref, rest_ref)
        for k in range(4):
            pad_2[k, pl.ds(base, STEP), :] = moved[k]

    slabs = nx + 2 * DEEP
    over_rows(PITCH, (slabs - 1) * PITCH, TURNS, finish_first)
    over_rows(2 * PITCH, (slabs - 2) * PITCH, TURNS, second)

    parts = 4
    thick = nx // parts
    for part in range(parts):
        for x in range(part * thick, (part + 1) * thick):
            for half in range(0, ny, STEP):
                base = (x + DEEP) * PITCH + FIRST + half
                moved = relax(base, STEP, pad_2, side_ref, rest_ref)
                for k in range(4):
                    fresh[k, x, half : half + STEP, :] = moved[k]
        at = pl.ds(part * thick, thick)
        send(fresh.at[pl.ds(0, 3), at], velocity_ref.at[:, at])
        send(fresh.at[3, at], pressure_ref.at[at])
    for copy in copies:
        copy.wait()


def relax_all(pad, part, side, rest, heat, means):
    nx, ny, nz = heat.shape
    vmem = pl.BlockSpec(memory_space=pltpu.VMEM)
    hbm = pl.BlockSpec(memory_space=pltpu.HBM)
    return pl.pallas_call(
        relax_kernel,
        out_shape=(
            jax.ShapeDtypeStruct((3, nx, ny, nz), jnp.float32),
            jax.ShapeDtypeStruct((nx, ny, nz), jnp.float32),
            jax.ShapeDtypeStruct(heat.shape, jnp.float32),
            jax.ShapeDtypeStruct(means.shape, jnp.float32),
        ),
        in_specs=[vmem] * 6,
        out_specs=(hbm,) * 4,
        scratch_shapes=[
            pltpu.VMEM(pad.shape, jnp.float32),
            pltpu.VMEM(pad.shape, jnp.float32),
            pltpu.VMEM((4, nx, ny, nz), jnp.float32),
            pltpu.SemaphoreType.DMA((10,)),
        ],
        compiler_params=pltpu.CompilerParams(vmem_limit_bytes=16 * 1024 * 1024),
    )(pad, part, side, rest, heat, means)


def per_device(
    tile_flow_speed,
    tile_stress_mean,
    tile_heat_state,
    tile_drag_coefficient,
    marker_attributes,
    marker_holding_tile,
    marker_voxel_number,
    prior_slot_of_tile,
):
    tracers = marker_attributes.shape[1]
    results = migrate(
        prior_slot_of_tile,
        tile_flow_speed.transpose(1, 0, 2),
        tile_stress_mean,
        tile_heat_state,
        tile_drag_coefficient,
        marker_attributes,
        marker_holding_tile.reshape(1, tracers),
        marker_voxel_number.reshape(1, tracers),
    )
    return relax_all(*results)


def solution(mesh):
    in_specs = (
        P(("wide", "narrow"), None, None),
        P(("wide", "narrow"), None),
        P(("wide", "narrow"), None),
        P(("wide", "narrow"), None),
        P(None, ("wide", "narrow")),
        P(("wide", "narrow")),
        P(("wide", "narrow")),
        P(("wide", "narrow")),
    )
    out_specs = (
        P(None, "wide", "narrow", None),
        P("wide", "narrow", None),
        P("wide", "narrow", None),
        P(None, "wide", "narrow", None),
    )
    return jax.shard_map(
        per_device, mesh=mesh, in_specs=in_specs, out_specs=out_specs, check_vma=False
    )
```

```python
import functools

import jax
import jax.numpy as jnp
from jax import lax
from jax.experimental import pallas as pl
from jax.experimental.pallas import tpu as pltpu
from jax.sharding import PartitionSpec as P

BS = 16
LX = 1
LY = 2
LZ = 8
SWEEPS = 3
BINS = 64
FIELDS = 6
AHEAD = 3
PITCH = 40
FIRST = 8
DEEP = 3
STEP = 16
TURNS = 1
DRIFT_TURNS = 5

MIX_WEIGHTS = (0.3, -0.25, 0.2, -0.15, 0.35, -0.3, 0.25, -0.2)
RELAX_WEIGHT = 0.7
PRESSURE_WEIGHT = 0.3
HEAT_FACTOR = 2.0
DENSITY_FACTOR = 4.0
MESH = pl.DeviceIdType.MESH


def swap_groups(x):
    row = lax.broadcasted_iota(jnp.int32, x.shape, 1)
    group = lax.broadcasted_iota(jnp.int32, x.shape, 2) // BS
    for bit in (1, 2, 4):
        row_set = (row & bit) != 0
        group_set = (group & bit) != 0
        from_above = pltpu.roll(pltpu.roll(x, 8 - bit, 1), BS * bit, 2)
        from_below = pltpu.roll(pltpu.roll(x, bit, 1), 8 * BS - BS * bit, 2)
        x = jnp.where(
            row_set == group_set, x, jnp.where(group_set, from_above, from_below)
        )
    return x


def bin_sums(base, holder_ref, voxel_ref, attr_ref, blocks, chunk):
    props, tracers = attr_ref.shape
    total_bins = blocks * BINS
    bin_ids = lax.broadcasted_iota(jnp.int32, (total_bins, chunk), 0)

    def step(turn, sums):
        at = pl.ds(pl.multiple_of(turn * chunk, chunk), chunk)
        voxel = voxel_ref[:, at]
        key = (
            (holder_ref[:, at] - base) * BINS
            + (voxel >> 10) * 16
            + ((voxel >> 6) & 3) * 4
            + ((voxel >> 2) & 3)
        )
        table = jnp.where(bin_ids == key, 1.0, 0.0).astype(jnp.bfloat16)
        values = attr_ref[:, at]
        high = values.astype(jnp.bfloat16)
        rest = values - high.astype(jnp.float32)
        middle = rest.astype(jnp.bfloat16)
        low = (rest - middle.astype(jnp.float32)).astype(jnp.bfloat16)
        ones = jnp.ones((props, chunk), jnp.bfloat16)
        rows = jnp.concatenate([high, middle, low, ones], axis=0)
        return sums + lax.dot_general(
            rows, table, (((1,), (1,)), ((), ())), preferred_element_type=jnp.float32
        )

    sums = lax.fori_loop(
        0, tracers // chunk, step, jnp.zeros((4 * props, total_bins), jnp.float32)
    )
    total = sums[:props] + sums[props : 2 * props] + sums[2 * props : 3 * props]
    return total / jnp.maximum(sums[3 * props :], 1.0)


def at_ends(shape):
    column = lax.broadcasted_iota(jnp.int32, shape, 1)
    return column == 0, column == shape[1] - 1


def z_pair(here):
    low_end, high_end = at_ends(here.shape)
    nz = here.shape[1]
    return (
        jnp.where(high_end, 0.0, pltpu.roll(here, nz - 1, 1)),
        jnp.where(low_end, 0.0, pltpu.roll(here, 1, 1)),
    )


def factors(base, rows, eta_ref, heat_ref, side_ref, rest_ref):
    here = eta_ref[pl.ds(base, rows), :]
    around = [
        eta_ref[pl.ds(base + off, rows), :] for off in (PITCH, -PITCH, 1, -1)
    ] + list(z_pair(here))
    face = [0.5 * (here + other) for other in around]
    diagonal = face[0]
    for m in range(1, 6):
        diagonal = diagonal + face[m]
    inside = here > 0.0
    scale = jnp.where(inside, RELAX_WEIGHT / jnp.where(inside, diagonal, 1.0), 0.0)
    low_end, high_end = at_ends(here.shape)
    own = pl.ds(base, rows)
    for m in range(6):
        value = face[m] * scale
        if m == 4:
            value = jnp.where(high_end, 0.0, value)
        elif m == 5:
            value = jnp.where(low_end, 0.0, value)
        side_ref[m, own, :] = value
    rest_ref[0, own, :] = 0.5 * scale
    rest_ref[1, own, :] = (0.5 * PRESSURE_WEIGHT) * here
    rest_ref[2, own, :] = scale * (DENSITY_FACTOR * heat_ref[own, :])


def drift(base, rows, pad, side_ref, rest_ref):
    nz = pad.shape[2]
    own = pl.ds(base, rows)

    def value(k, off=0):
        return pad[k, pl.ds(base + off, rows), :]

    side = [side_ref[m, own, :] for m in range(6)]
    found = []
    divergence = None
    for k in range(3):
        here = value(k)
        if k == 2:
            up_z, down_z = z_pair(here)
        else:
            up_z, down_z = pltpu.roll(here, nz - 1, 1), pltpu.roll(here, 1, 1)
        near = (
            value(k, PITCH), value(k, -PITCH), value(k, 1), value(k, -1), up_z, down_z,
        )
        fresh = (1.0 - RELAX_WEIGHT) * here
        for m in range(6):
            fresh = fresh + side[m] * near[m]
        if k == 2:
            fresh = fresh + rest_ref[2, own, :]
        found.append(fresh)
        flux = near[2 * k] - near[2 * k + 1]
        divergence = flux if divergence is None else divergence + flux
    found.append(rest_ref[1, own, :] * divergence)
    return found


def push(base, rows, pad, rest_ref, drifted):
    own = pl.ds(base, rows)

    def value(off=0):
        return pad[3, pl.ds(base + off, rows), :]

    press = value()
    up_z, down_z = z_pair(press)
    half_scale = rest_ref[0, own, :]
    drops = (value(PITCH) - value(-PITCH), value(1) - value(-1), up_z - down_z)
    return [drifted[k] - half_scale * drops[k] for k in range(3)] + [press - drifted[3]]


def relax(base, rows, pad, side_ref, rest_ref):
    return push(base, rows, pad, rest_ref, drift(base, rows, pad, side_ref, rest_ref))


def over_rows(first, last, turns, act):
    together = (last - first) // (STEP * turns)
    assert together * STEP * turns == last - first

    def step(turn, carry):
        for i in range(together):
            act(pl.multiple_of(first + (turn * together + i) * STEP, 8))
        return carry

    lax.fori_loop(0, turns, step, 0)


def migrate_kernel(
    places_ref, flow_ref, stress_ref, warm_ref, drag_ref, attr_ref, holder_ref, voxel_ref,
    pad_ref, part_ref, side_ref, rest_ref, heat_ref, mean_ref,
    slot_ref, row_ref, table, table_smem, raw, lined, mine, stage_0, stage_1, stage_2, stage_3, stage_4, stage_5,
    land_0, land_1, land_2, land_3, land_4, land_5,
    attr, holder, voxel, mean_mine, mean_stage, mean_land, mean_held, held, drag_grid,
    eta, warm, edge_in, edge_out, corner_in, corner_out,
    raw_sems, table_send, table_recv, data_send, data_recv, mean_sems,
    halo_send, halo_recv, small_sem,
    *, wide_count, narrow_count,
):
    count = wide_count * narrow_count
    wide, narrow = lax.axis_index("wide"), lax.axis_index("narrow")
    me = wide * narrow_count + narrow
    blocks = raw.shape[1]
    nx, ny, nz = heat_ref.shape
    stages = (stage_0, stage_1, stage_2, stage_3, stage_4, stage_5)
    lands = (land_0, land_1, land_2, land_3, land_4, land_5)

    to_slots = pltpu.make_async_copy(places_ref, slot_ref, small_sem)
    to_slots.start()
    def flipped(k):
        place, bit = narrow, 1
        while bit < narrow_count:
            if k & bit:
                place = place + bit * (1 - 2 * lax.rem(lax.div(narrow, bit), 2))
            bit *= 2
        return place

    middle = narrow_count // 2
    upper = lax.div(narrow, middle)
    across = [(middle + i) * (1 - upper) + (middle - 1 - i) * upper for i in range(middle)]
    planes = across + [flipped(k) for k in range(1, middle)] + [narrow]
    farthest_first = across[::-1] + planes[middle:]

    def to_plane(plane, act):
        def step(a, carry):
            act(lax.rem(wide + a, wide_count), plane)
            return carry

        lax.fori_loop(1 if plane is narrow else 0, wide_count, step, 0)

    def others(act, order=planes):
        for plane in order:
            to_plane(plane, act)

    barrier = pltpu.get_barrier_semaphore()
    others(
        lambda w, n: pl.semaphore_signal(
            barrier, inc=1, device_id=(w, n), device_id_type=MESH
        ),
        farthest_first,
    )

    sources = (
        warm_ref, drag_ref, flow_ref.at[0], flow_ref.at[1], flow_ref.at[2], stress_ref,
    )
    loads = [
        pltpu.make_async_copy(source, raw.at[f], raw_sems.at[f]) for f, source in enumerate(sources)
    ]
    loads.append(pltpu.make_async_copy(attr_ref, attr, raw_sems.at[FIELDS]))
    loads.append(pltpu.make_async_copy(holder_ref, holder, raw_sems.at[FIELDS + 1]))
    loads.append(pltpu.make_async_copy(voxel_ref, voxel, raw_sems.at[FIELDS + 2]))
    for load in loads:
        load.start()

    to_slots.wait()
    lane = lax.broadcasted_iota(jnp.int32, (1, 128), 1)
    places = jnp.zeros((1, 128), jnp.int32)
    my_own = jnp.int32(0)
    for r in range(blocks):
        owner = lax.div(slot_ref[r], blocks)
        local = slot_ref[r] - owner * blocks
        places = jnp.where(lane == owner, local, places)
        my_own = jnp.where(owner == me, local, my_own)
    row_ref[...] = places
    table[narrow * wide_count + wide] = places
    pl.semaphore_wait(barrier, count - 1)

    def send_row(w, n):
        pltpu.make_async_remote_copy(
            src_ref=row_ref,
            dst_ref=table.at[narrow * wide_count + wide],
            send_sem=table_send,
            recv_sem=table_recv.at[narrow],
            device_id=(w, n),
            device_id_type=MESH,
        ).start()

    others(send_row)

    def whole(ref, send_sem, recv_sem):
        part = ref.at[pl.ds(0, count - 1)]
        return pltpu.make_async_remote_copy(
            src_ref=part,
            dst_ref=part,
            send_sem=send_sem,
            recv_sem=recv_sem,
            device_id=(wide, narrow),
            device_id_type=MESH,
        )

    rows = BS * BS * BS // 128
    def lay_out(f):
        loads[f].wait()
        for g in range(blocks // 8):
            for j in range(rows):
                lined[pl.ds(g * 8 * rows + j, 8, stride=rows), :] = raw[
                    f, g * 8 : g * 8 + 8, j * 128 : j * 128 + 128
                ]
        mine[f] = lined[...].reshape(blocks, rows, 128)

    lay_out(0)

    def take_rows(plane):
        rows_at = pl.ds(plane * wide_count, wide_count - 1 if plane is narrow else wide_count)
        part = table.at[rows_at]
        pltpu.make_async_remote_copy(
            src_ref=part, dst_ref=part, send_sem=table_send, recv_sem=table_recv.at[plane],
            device_id=(wide, narrow), device_id_type=MESH,
        ).wait_recv()
        rows_at = pl.ds(plane * wide_count, wide_count)
        to_scalar = pltpu.make_async_copy(table.at[rows_at], table_smem.at[rows_at], small_sem)
        to_scalar.start()
        to_scalar.wait()

    def wanted(w, n):
        return table_smem[n * wide_count + w, 0, me]

    def send_part(f):
        def send(w, n):
            d = w * narrow_count + n
            stages[f][d] = mine[f, wanted(w, n)]
            pltpu.make_async_remote_copy(
                src_ref=stages[f].at[d],
                dst_ref=lands[f].at[me],
                send_sem=data_send.at[f],
                recv_sem=data_recv.at[f],
                device_id=(w, n),
                device_id_type=MESH,
            ).start()

        return send

    def send_field(f):
        others(send_part(f), farthest_first)
        lands[f][me] = mine[f, my_own]

    for plane in planes:
        take_rows(plane)
        to_plane(plane, send_part(0))
    lands[0][me] = mine[0, my_own]
    for ref in (pad_ref, eta, warm, edge_in, corner_in, corner_out):
        ref[...] = jnp.zeros(ref.shape, jnp.float32)
    for f in range(1, FIELDS):
        lay_out(f)
        if f < AHEAD:
            send_field(f)

    for load in loads[FIELDS:]:
        load.wait()
    tracers = attr.shape[1]
    chunk = 1024 if tracers % 1024 == 0 else tracers
    means = bin_sums(me * blocks, holder, voxel, attr, blocks, chunk)
    left = lax.broadcasted_iota(jnp.int32, (8, 128), 1) < BINS
    for q in range(blocks // 2):
        pair = means[:, q * 128 : q * 128 + 128]
        across = pltpu.roll(pair, BINS, 1)
        below = pltpu.roll(pair, 4, 0)
        both = pltpu.roll(across, 4, 0)
        mean_mine[2 * q] = jnp.where(left, pair, both)[:4]
        mean_mine[2 * q + 1] = jnp.where(left, across, below)[:4]

    def send_mean(w, n):
        d = w * narrow_count + n
        mean_stage[d] = mean_mine[wanted(w, n)]
        pltpu.make_async_remote_copy(
            src_ref=mean_stage.at[d],
            dst_ref=mean_land.at[me],
            send_sem=mean_sems.at[0],
            recv_sem=mean_sems.at[1],
            device_id=(w, n),
            device_id_type=MESH,
        ).start()

    others(send_mean)
    mean_land[me] = mean_mine[my_own]

    def source_of(y, z):
        return lax.div(slot_ref[y * LZ + z], blocks)

    def grid_part(f, y):
        for z in range(LZ):
            held[pl.ds(z, rows, stride=LZ), :] = lands[f][source_of(y, z)]
        return swap_groups(held[...].reshape(rows, LZ, 128)).reshape(BS, BS, 128)

    ways = ((-1, 0), (1, 0), (0, -1), (0, 1), (-1, -1), (-1, 1), (1, -1), (1, 1))
    low_side = {-1: (wide > 0, narrow > 0), 1: (wide < wide_count - 1, narrow < narrow_count - 1)}

    def exists(way):
        there = [low_side[step][axis] for axis, step in enumerate(way) if step]
        return there[0] if len(there) == 1 else there[0] & there[1]

    def row_of(x, y):
        return (x + DEEP) * PITCH + FIRST + y

    def grid_rows(g, at):
        if g < 2:
            return (warm, eta)[g].at[at]
        return pad_ref.at[g - 2, at]

    def depth_of(g):
        return DEEP - 1 if g == 0 else DEEP

    def messages(g):
        found = []
        for i in range(DEEP):
            for way, slot in ((-1, i), (1, DEEP + i)):
                mine_x, theirs_x = (i, nx + i) if way < 0 else (nx - DEEP + i, i - DEEP)
                here_x = i - DEEP if way < 0 else nx + i
                rows_at = [
                    grid_rows(g, pl.ds(row_of(x, 0), ny)) for x in (mine_x, theirs_x, here_x)
                ]
                found.append(
                    ((way, 0), slot, rows_at[0], rows_at[1], (slot + DEEP) % (2 * DEEP), rows_at[2])
                )
        deep = pl.ds(0, depth_of(g))
        for side, way in enumerate((-1, 1)):
            slot = 2 * DEEP + side
            found.append(
                (
                    (0, way), slot, edge_out.at[g, side, deep], edge_in.at[g, 1 - side, deep],
                    2 * DEEP + 1 - side, edge_in.at[g, side, deep],
                )
            )
        for c, way in enumerate(ways[4:]):
            found.append(
                (
                    way, 2 * DEEP + 2 + c, corner_out.at[g, c], corner_in.at[g, 3 - c],
                    2 * DEEP + 5 - c, corner_in.at[g, c],
                )
            )
        return found

    def each_message(g, act):
        for way in ways[4:] + ways[:4]:
            group = [m for m in messages(g) if m[0] == way]

            @pl.when(exists(way))
            def _(way=way, group=group):
                for _, slot, source, target, far_slot, here in group:
                    act(way, slot, source, target, far_slot, here)

    def start_message(g):
        def act(way, slot, source, target, far_slot, here):
            pltpu.make_async_remote_copy(
                src_ref=source, dst_ref=target,
                send_sem=halo_send.at[g, slot], recv_sem=halo_recv.at[g, far_slot],
                device_id=(wide + way[0], narrow + way[1]), device_id_type=MESH,
            ).start()

        return act

    def wait_message(g, sent):
        def act(way, slot, source, target, far_slot, here):
            copy = pltpu.make_async_remote_copy(
                src_ref=source if sent else here, dst_ref=target if sent else here,
                send_sem=halo_send.at[g, slot], recv_sem=halo_recv.at[g, slot],
                device_id=(wide + way[0], narrow + way[1]), device_id_type=MESH,
            )
            copy.wait_send() if sent else copy.wait_recv()

        return act

    def read_rows(g, at):
        return (warm, eta)[g][at, :] if g < 2 else pad_ref[g - 2, at, :]

    def write_rows(g, at, value):
        if g < 2:
            (warm, eta)[g][at, :] = value
        else:
            pad_ref[g - 2, at, :] = value

    def send_halo(g):
        depth = depth_of(g)
        for side in range(2):
            for i in range(depth):
                y = i if side == 0 else ny - depth + i
                edge_out[g, side, i] = read_rows(g, pl.ds(row_of(0, y), nx, stride=PITCH))
        for c, (dx, dy) in enumerate(ways[4:]):
            for i in range(2):
                x = i if dx < 0 else nx - 2 + i
                y = 0 if dy < 0 else ny - 2
                corner_out[g, c, 2 * i : 2 * i + 2, :] = read_rows(g, pl.ds(row_of(x, y), 2))
        each_message(g, start_message(g))

    def take_halo(g):
        depth = depth_of(g)
        each_message(g, wait_message(g, False))
        for side in range(2):
            for i in range(depth):
                y = i - depth if side == 0 else ny + i
                write_rows(g, pl.ds(row_of(0, y), nx, stride=PITCH), edge_in[g, side, i])
        for c, (dx, dy) in enumerate(ways[4:]):
            for i in range(2):
                x = i - 2 if dx < 0 else nx + i
                y = -2 if dy < 0 else ny
                write_rows(g, pl.ds(row_of(x, y), 2), corner_in[g, c, 2 * i : 2 * i + 2, :])

    def viscosity():
        whole(mean_land, mean_sems.at[0], mean_sems.at[1]).wait_recv()
        expand = (
            lax.broadcasted_iota(jnp.int32, (LZ, 32), 0)
            == lax.broadcasted_iota(jnp.int32, (LZ, 32), 1) // 4
        ).astype(jnp.float32)
        same = (
            lax.broadcasted_iota(jnp.int32, (128, 32), 0) % 4
            == lax.broadcasted_iota(jnp.int32, (128, 32), 1) % 4
        )
        gather = (
            lax.broadcasted_iota(jnp.int32, (32, 128), 0)
            == lax.broadcasted_iota(jnp.int32, (32, 128), 1) // 4
        ).astype(jnp.float32)
        for y in range(LY):
            for z in range(LZ):
                mean_held[pl.ds(z, 4, stride=LZ), :] = mean_land[source_of(y, z)]
            for p in range(4):
                tall = jnp.dot(
                    mean_held[p * LZ : p * LZ + LZ].T, expand,
                    precision=lax.Precision.HIGHEST, preferred_element_type=jnp.float32,
                )
                cells = jnp.dot(
                    gather, jnp.where(same, tall, 0.0),
                    precision=lax.Precision.HIGHEST, preferred_element_type=jnp.float32,
                )
                for half in range(2):
                    for layer in range(4):
                        at = half * 16 + layer * 4
                        mean_ref[half * 4 + p, layer, y * 4 : y * 4 + 4, :] = cells[at : at + 4]
        for layer in range(4):
            mixture = MIX_WEIGHTS[0] * mean_ref[0, layer]
            for p in range(1, len(MIX_WEIGHTS)):
                mixture = mixture + MIX_WEIGHTS[p] * mean_ref[p, layer]
            wide_mix = jnp.dot(
                mixture, gather,
                precision=lax.Precision.HIGHEST, preferred_element_type=jnp.float32,
            )
            spread = jnp.concatenate(
                [jnp.broadcast_to(wide_mix[j : j + 1], (4, 128)) for j in range(LY * 4)], axis=0
            )
            for x in range(layer * 4, layer * 4 + 4):
                eta[pl.ds(row_of(x, 0), ny), :] = drag_grid[x] * jnp.exp(
                    HEAT_FACTOR * (0.5 - heat_ref[x]) + spread
                )

    wide_rows = (PITCH, (nx + 2 * DEEP - 1) * PITCH)

    def factor_rows(base):
        factors(base, STEP, eta, warm, side_ref, rest_ref)

    def drift_rows(base):
        found = drift(base, STEP, pad_ref, side_ref, rest_ref)
        for k in range(4):
            part_ref[k, pl.ds(base, STEP), :] = found[k]

    for f in range(FIELDS):
        whole(lands[f], data_send.at[f], data_recv.at[f]).wait_recv()
        if f + AHEAD < FIELDS:
            send_field(f + AHEAD)
        for y in range(LY):
            at = slice(y * BS, (y + 1) * BS)
            part = grid_part(f, y)
            if f == 0:
                heat_ref[:, at, :] = part
            if f == 1:
                drag_grid[:, at, :] = part
            else:
                for x in range(nx):
                    write_rows(f, pl.ds(row_of(x, y * BS), BS), part[x])
        if f == 1:
            viscosity()
            send_halo(0)
        if f > 0:
            send_halo(f)
        if f == 3:
            take_halo(0)
            take_halo(1)
            over_rows(*wide_rows, 10, factor_rows)
    for f in range(2, FIELDS - 1):
        take_halo(f)
    over_rows(*wide_rows, DRIFT_TURNS, drift_rows)
    take_halo(FIELDS - 1)

    whole(table, table_send, table_recv.at[0]).wait_send()
    whole(mean_land, mean_sems.at[0], mean_sems.at[1]).wait_send()
    for f in range(FIELDS):
        whole(lands[f], data_send.at[f], data_recv.at[f]).wait_send()
    for f in range(FIELDS):
        each_message(f, wait_message(f, True))


def migrate(slots, flow, stress, heat, drag, attributes, holder, voxel):
    wide_count, narrow_count = lax.axis_size("wide"), lax.axis_size("narrow")
    count = wide_count * narrow_count
    blocks = slots.shape[0]
    tracers = attributes.shape[1]
    nx, ny, nz = LX * BS, LY * BS, LZ * BS
    rows = BS * BS * BS // 128
    pad_rows = (nx + 2 * DEEP) * PITCH + 8
    vmem = pl.BlockSpec(memory_space=pltpu.VMEM)
    hbm = pl.BlockSpec(memory_space=pltpu.HBM)
    f32 = jnp.float32
    per_field = [pltpu.VMEM((count, rows, 128), f32)] * FIELDS
    dma = pltpu.SemaphoreType.DMA
    pinned = [
        pltpu.with_memory_space_constraint(array, pltpu.HBM)
        for array in (slots, flow, stress, heat, drag, attributes, holder, voxel)
    ]
    return pl.pallas_call(
        functools.partial(migrate_kernel, wide_count=wide_count, narrow_count=narrow_count),
        out_shape=(
            jax.ShapeDtypeStruct((4, pad_rows, nz), f32),
            jax.ShapeDtypeStruct((4, pad_rows, nz), f32),
            jax.ShapeDtypeStruct((6, pad_rows, nz), f32),
            jax.ShapeDtypeStruct((3, pad_rows, nz), f32),
            jax.ShapeDtypeStruct((nx, ny, nz), f32),
            jax.ShapeDtypeStruct((8, LX * 4, LY * 4, LZ * 4), f32),
        ),
        in_specs=[hbm] * 8,
        out_specs=(vmem,) * 6,
        scratch_shapes=[
            pltpu.SMEM((blocks,), jnp.int32),
            pltpu.VMEM((1, 128), jnp.int32),
            pltpu.VMEM((count, 1, 128), jnp.int32),
            pltpu.SMEM((count, 1, 128), jnp.int32),
            pltpu.VMEM((FIELDS, blocks, rows * 128), f32),
            pltpu.VMEM((blocks * rows, 128), f32),
            pltpu.VMEM((FIELDS, blocks, rows, 128), f32),
            *per_field,
            *per_field,
            pltpu.VMEM((8, tracers), f32),
            pltpu.VMEM((1, tracers), jnp.int32),
            pltpu.VMEM((1, tracers), jnp.int32),
            pltpu.VMEM((blocks, 4, 128), f32),
            pltpu.VMEM((count, 4, 128), f32),
            pltpu.VMEM((count, 4, 128), f32),
            pltpu.VMEM((4 * LZ, 128), f32),
            pltpu.VMEM((rows * LZ, 128), f32),
            pltpu.VMEM((nx, ny, nz), f32),
            pltpu.VMEM((pad_rows, nz), f32),
            pltpu.VMEM((pad_rows, nz), f32),
            pltpu.VMEM((FIELDS, 2, DEEP, nx, nz), f32),
            pltpu.VMEM((FIELDS, 2, DEEP, nx, nz), f32),
            pltpu.VMEM((FIELDS, 4, 8, nz), f32),
            pltpu.VMEM((FIELDS, 4, 8, nz), f32),
            dma((FIELDS + 3,)),
            dma(()),
            dma((narrow_count,)),
            dma((FIELDS,)),
            dma((FIELDS,)),
            dma((2,)),
            dma((FIELDS, 2 * DEEP + 6)),
            dma((FIELDS, 2 * DEEP + 6)),
            dma(()),
        ],
        compiler_params=pltpu.CompilerParams(
            collective_id=1,
            has_side_effects=True,
            vmem_limit_bytes=(24 if count <= 32 else 44) * 1024 * 1024,
        ),
    )(*pinned)


def relax_kernel(
    pad_ref, part_ref, side_ref, rest_ref, heat_ref, mean_ref,
    velocity_ref, pressure_ref, heat_out_ref, mean_out_ref, pad_1, pad_2, fresh, sems,
):
    nx, ny, nz = heat_ref.shape
    copies = []

    def send(source, target):
        copies.append(pltpu.make_async_copy(source, target, sems.at[len(copies)]))
        copies[-1].start()

    send(heat_ref, heat_out_ref)
    send(mean_ref, mean_out_ref)

    def finish_first(base):
        drifted = [part_ref[k, pl.ds(base, STEP), :] for k in range(4)]
        moved = push(base, STEP, pad_ref, rest_ref, drifted)
        for k in range(4):
            pad_1[k, pl.ds(base, STEP), :] = moved[k]

    def second(base):
        moved = relax(base, STEP, pad_1, side_ref, rest_ref)
        for k in range(4):
            pad_2[k, pl.ds(base, STEP), :] = moved[k]

    slabs = nx + 2 * DEEP
    over_rows(PITCH, (slabs - 1) * PITCH, TURNS, finish_first)
    over_rows(2 * PITCH, (slabs - 2) * PITCH, TURNS, second)

    parts = 4
    thick = nx // parts
    for part in range(parts):
        for x in range(part * thick, (part + 1) * thick):
            for half in range(0, ny, STEP):
                base = (x + DEEP) * PITCH + FIRST + half
                moved = relax(base, STEP, pad_2, side_ref, rest_ref)
                for k in range(4):
                    fresh[k, x, half : half + STEP, :] = moved[k]
        at = pl.ds(part * thick, thick)
        send(fresh.at[pl.ds(0, 3), at], velocity_ref.at[:, at])
        send(fresh.at[3, at], pressure_ref.at[at])
    for copy in copies:
        copy.wait()


def relax_all(pad, part, side, rest, heat, means):
    nx, ny, nz = heat.shape
    vmem = pl.BlockSpec(memory_space=pltpu.VMEM)
    hbm = pl.BlockSpec(memory_space=pltpu.HBM)
    return pl.pallas_call(
        relax_kernel,
        out_shape=(
            jax.ShapeDtypeStruct((3, nx, ny, nz), jnp.float32),
            jax.ShapeDtypeStruct((nx, ny, nz), jnp.float32),
            jax.ShapeDtypeStruct(heat.shape, jnp.float32),
            jax.ShapeDtypeStruct(means.shape, jnp.float32),
        ),
        in_specs=[vmem] * 6,
        out_specs=(hbm,) * 4,
        scratch_shapes=[
            pltpu.VMEM(pad.shape, jnp.float32),
            pltpu.VMEM(pad.shape, jnp.float32),
            pltpu.VMEM((4, nx, ny, nz), jnp.float32),
            pltpu.SemaphoreType.DMA((10,)),
        ],
        compiler_params=pltpu.CompilerParams(vmem_limit_bytes=16 * 1024 * 1024),
    )(pad, part, side, rest, heat, means)


def per_device(
    tile_flow_speed,
    tile_stress_mean,
    tile_heat_state,
    tile_drag_coefficient,
    marker_attributes,
    marker_holding_tile,
    marker_voxel_number,
    prior_slot_of_tile,
):
    tracers = marker_attributes.shape[1]
    results = migrate(
        prior_slot_of_tile,
        tile_flow_speed.transpose(1, 0, 2),
        tile_stress_mean,
        tile_heat_state,
        tile_drag_coefficient,
        marker_attributes,
        marker_holding_tile.reshape(1, tracers),
        marker_voxel_number.reshape(1, tracers),
    )
    return relax_all(*results)


def solution(mesh):
    in_specs = (
        P(("wide", "narrow"), None, None),
        P(("wide", "narrow"), None),
        P(("wide", "narrow"), None),
        P(("wide", "narrow"), None),
        P(None, ("wide", "narrow")),
        P(("wide", "narrow")),
        P(("wide", "narrow")),
        P(("wide", "narrow")),
    )
    out_specs = (
        P(None, "wide", "narrow", None),
        P("wide", "narrow", None),
        P("wide", "narrow", None),
        P(None, "wide", "narrow", None),
    )
    return jax.shard_map(
        per_device, mesh=mesh, in_specs=in_specs, out_specs=out_specs, check_vma=False
    )
```

```python
import functools

import jax
import jax.numpy as jnp
from jax import lax
from jax.experimental import pallas as pl
from jax.experimental.pallas import tpu as pltpu
from jax.sharding import PartitionSpec as P

BS = 16
LX = 1
LY = 2
LZ = 8
SWEEPS = 3
BINS = 64
FIELDS = 6
AHEAD = 3
PITCH = 40
FIRST = 8
DEEP = 3
STEP = 16
TURNS = 1
DRIFT_TURNS = 5

MIX_WEIGHTS = (0.3, -0.25, 0.2, -0.15, 0.35, -0.3, 0.25, -0.2)
RELAX_WEIGHT = 0.7
PRESSURE_WEIGHT = 0.3
HEAT_FACTOR = 2.0
DENSITY_FACTOR = 4.0
MESH = pl.DeviceIdType.MESH


def swap_groups(x):
    row = lax.broadcasted_iota(jnp.int32, x.shape, 1)
    group = lax.broadcasted_iota(jnp.int32, x.shape, 2) // BS
    for bit in (1, 2, 4):
        row_set = (row & bit) != 0
        group_set = (group & bit) != 0
        from_above = pltpu.roll(pltpu.roll(x, 8 - bit, 1), BS * bit, 2)
        from_below = pltpu.roll(pltpu.roll(x, bit, 1), 8 * BS - BS * bit, 2)
        x = jnp.where(
            row_set == group_set, x, jnp.where(group_set, from_above, from_below)
        )
    return x


def bin_sums(base, holder_ref, voxel_ref, attr_ref, blocks, chunk):
    props, tracers = attr_ref.shape
    total_bins = blocks * BINS
    bin_ids = lax.broadcasted_iota(jnp.int32, (total_bins, chunk), 0)

    def step(turn, sums):
        at = pl.ds(pl.multiple_of(turn * chunk, chunk), chunk)
        voxel = voxel_ref[:, at]
        key = (
            (holder_ref[:, at] - base) * BINS
            + (voxel >> 10) * 16
            + ((voxel >> 6) & 3) * 4
            + ((voxel >> 2) & 3)
        )
        table = jnp.where(bin_ids == key, 1.0, 0.0).astype(jnp.bfloat16)
        values = attr_ref[:, at]
        high = values.astype(jnp.bfloat16)
        rest = values - high.astype(jnp.float32)
        middle = rest.astype(jnp.bfloat16)
        low = (rest - middle.astype(jnp.float32)).astype(jnp.bfloat16)
        ones = jnp.ones((props, chunk), jnp.bfloat16)
        rows = jnp.concatenate([high, middle, low, ones], axis=0)
        return sums + lax.dot_general(
            rows, table, (((1,), (1,)), ((), ())), preferred_element_type=jnp.float32
        )

    sums = lax.fori_loop(
        0, tracers // chunk, step, jnp.zeros((4 * props, total_bins), jnp.float32)
    )
    total = sums[:props] + sums[props : 2 * props] + sums[2 * props : 3 * props]
    return total / jnp.maximum(sums[3 * props :], 1.0)


def at_ends(shape):
    column = lax.broadcasted_iota(jnp.int32, shape, 1)
    return column == 0, column == shape[1] - 1


def z_pair(here):
    low_end, high_end = at_ends(here.shape)
    nz = here.shape[1]
    return (
        jnp.where(high_end, 0.0, pltpu.roll(here, nz - 1, 1)),
        jnp.where(low_end, 0.0, pltpu.roll(here, 1, 1)),
    )


def factors(base, rows, eta_ref, heat_ref, side_ref, rest_ref):
    here = eta_ref[pl.ds(base, rows), :]
    around = [
        eta_ref[pl.ds(base + off, rows), :] for off in (PITCH, -PITCH, 1, -1)
    ] + list(z_pair(here))
    face = [0.5 * (here + other) for other in around]
    diagonal = face[0]
    for m in range(1, 6):
        diagonal = diagonal + face[m]
    inside = here > 0.0
    scale = jnp.where(inside, RELAX_WEIGHT / jnp.where(inside, diagonal, 1.0), 0.0)
    low_end, high_end = at_ends(here.shape)
    own = pl.ds(base, rows)
    for m in range(6):
        value = face[m] * scale
        if m == 4:
            value = jnp.where(high_end, 0.0, value)
        elif m == 5:
            value = jnp.where(low_end, 0.0, value)
        side_ref[m, own, :] = value
    rest_ref[0, own, :] = 0.5 * scale
    rest_ref[1, own, :] = (0.5 * PRESSURE_WEIGHT) * here
    rest_ref[2, own, :] = scale * (DENSITY_FACTOR * heat_ref[own, :])


def drift(base, rows, pad, side_ref, rest_ref):
    nz = pad.shape[2]
    own = pl.ds(base, rows)

    def value(k, off=0):
        return pad[k, pl.ds(base + off, rows), :]

    side = [side_ref[m, own, :] for m in range(6)]
    found = []
    divergence = None
    for k in range(3):
        here = value(k)
        if k == 2:
            up_z, down_z = z_pair(here)
        else:
            up_z, down_z = pltpu.roll(here, nz - 1, 1), pltpu.roll(here, 1, 1)
        near = (
            value(k, PITCH), value(k, -PITCH), value(k, 1), value(k, -1), up_z, down_z,
        )
        fresh = (1.0 - RELAX_WEIGHT) * here
        for m in range(6):
            fresh = fresh + side[m] * near[m]
        if k == 2:
            fresh = fresh + rest_ref[2, own, :]
        found.append(fresh)
        flux = near[2 * k] - near[2 * k + 1]
        divergence = flux if divergence is None else divergence + flux
    found.append(rest_ref[1, own, :] * divergence)
    return found


def push(base, rows, pad, rest_ref, drifted):
    own = pl.ds(base, rows)

    def value(off=0):
        return pad[3, pl.ds(base + off, rows), :]

    press = value()
    up_z, down_z = z_pair(press)
    half_scale = rest_ref[0, own, :]
    drops = (value(PITCH) - value(-PITCH), value(1) - value(-1), up_z - down_z)
    return [drifted[k] - half_scale * drops[k] for k in range(3)] + [press - drifted[3]]


def relax(base, rows, pad, side_ref, rest_ref):
    return push(base, rows, pad, rest_ref, drift(base, rows, pad, side_ref, rest_ref))


def over_rows(first, last, turns, act):
    together = (last - first) // (STEP * turns)
    assert together * STEP * turns == last - first

    def step(turn, carry):
        for i in range(together):
            act(pl.multiple_of(first + (turn * together + i) * STEP, 8))
        return carry

    lax.fori_loop(0, turns, step, 0)


def migrate_kernel(
    places_ref, flow_ref, stress_ref, warm_ref, drag_ref, attr_ref, holder_ref, voxel_ref,
    pad_ref, part_ref, side_ref, rest_ref, heat_ref, mean_ref,
    slot_ref, row_ref, table, table_smem, raw, lined, mine, stage_0, stage_1, stage_2, stage_3, stage_4, stage_5,
    land_0, land_1, land_2, land_3, land_4, land_5,
    attr, holder, voxel, mean_mine, mean_stage, mean_land, mean_held, held, drag_grid,
    eta, warm, edge_in, edge_out, corner_in, corner_out,
    raw_sems, table_send, table_recv, data_send, data_recv, mean_sems,
    halo_send, halo_recv, small_sem,
    *, wide_count, narrow_count,
):
    count = wide_count * narrow_count
    wide, narrow = lax.axis_index("wide"), lax.axis_index("narrow")
    me = wide * narrow_count + narrow
    blocks = raw.shape[1]
    nx, ny, nz = heat_ref.shape
    stages = (stage_0, stage_1, stage_2, stage_3, stage_4, stage_5)
    lands = (land_0, land_1, land_2, land_3, land_4, land_5)

    to_slots = pltpu.make_async_copy(places_ref, slot_ref, small_sem)
    to_slots.start()
    def flipped(k):
        place, bit = narrow, 1
        while bit < narrow_count:
            if k & bit:
                place = place + bit * (1 - 2 * lax.rem(lax.div(narrow, bit), 2))
            bit *= 2
        return place

    middle = narrow_count // 2
    upper = lax.div(narrow, middle)
    across = [(middle + i) * (1 - upper) + (middle - 1 - i) * upper for i in range(middle)]
    planes = across + [flipped(k) for k in range(1, middle)] + [narrow]
    farthest_first = across[::-1] + planes[middle:]

    def to_plane(plane, act):
        def step(a, carry):
            act(lax.rem(wide + a, wide_count), plane)
            return carry

        lax.fori_loop(1 if plane is narrow else 0, wide_count, step, 0)

    def others(act, order=planes):
        for plane in order:
            to_plane(plane, act)

    barrier = pltpu.get_barrier_semaphore()
    others(
        lambda w, n: pl.semaphore_signal(
            barrier, inc=1, device_id=(w, n), device_id_type=MESH
        ),
        farthest_first,
    )

    sources = (
        warm_ref, drag_ref, flow_ref.at[0], flow_ref.at[1], flow_ref.at[2], stress_ref,
    )
    loads = [
        pltpu.make_async_copy(source, raw.at[f], raw_sems.at[f]) for f, source in enumerate(sources)
    ]
    loads.append(pltpu.make_async_copy(attr_ref, attr, raw_sems.at[FIELDS]))
    loads.append(pltpu.make_async_copy(holder_ref, holder, raw_sems.at[FIELDS + 1]))
    loads.append(pltpu.make_async_copy(voxel_ref, voxel, raw_sems.at[FIELDS + 2]))
    for load in loads:
        load.start()

    to_slots.wait()
    lane = lax.broadcasted_iota(jnp.int32, (1, 128), 1)
    places = jnp.zeros((1, 128), jnp.int32)
    my_own = jnp.int32(0)
    for r in range(blocks):
        owner = lax.div(slot_ref[r], blocks)
        local = slot_ref[r] - owner * blocks
        places = jnp.where(lane == owner, local, places)
        my_own = jnp.where(owner == me, local, my_own)
    row_ref[...] = places
    table[narrow * wide_count + wide] = places
    pl.semaphore_wait(barrier, count - 1)

    def send_row(w, n):
        pltpu.make_async_remote_copy(
            src_ref=row_ref,
            dst_ref=table.at[narrow * wide_count + wide],
            send_sem=table_send,
            recv_sem=table_recv.at[narrow],
            device_id=(w, n),
            device_id_type=MESH,
        ).start()

    others(send_row)

    def whole(ref, send_sem, recv_sem):
        part = ref.at[pl.ds(0, count - 1)]
        return pltpu.make_async_remote_copy(
            src_ref=part,
            dst_ref=part,
            send_sem=send_sem,
            recv_sem=recv_sem,
            device_id=(wide, narrow),
            device_id_type=MESH,
        )

    rows = BS * BS * BS // 128
    def lay_out(f):
        loads[f].wait()
        for g in range(blocks // 8):
            for j in range(rows):
                lined[pl.ds(g * 8 * rows + j, 8, stride=rows), :] = raw[
                    f, g * 8 : g * 8 + 8, j * 128 : j * 128 + 128
                ]
        mine[f] = lined[: blocks * rows].reshape(blocks, rows, 128)

    lay_out(0)

    def take_rows(plane):
        rows_at = pl.ds(plane * wide_count, wide_count - 1 if plane is narrow else wide_count)
        part = table.at[rows_at]
        pltpu.make_async_remote_copy(
            src_ref=part, dst_ref=part, send_sem=table_send, recv_sem=table_recv.at[plane],
            device_id=(wide, narrow), device_id_type=MESH,
        ).wait_recv()
        rows_at = pl.ds(plane * wide_count, wide_count)
        to_scalar = pltpu.make_async_copy(table.at[rows_at], table_smem.at[rows_at], small_sem)
        to_scalar.start()
        to_scalar.wait()

    def wanted(w, n):
        return table_smem[n * wide_count + w, 0, me]

    def send_part(f):
        def send(w, n):
            d = w * narrow_count + n
            stages[f][d] = mine[f, wanted(w, n)]
            pltpu.make_async_remote_copy(
                src_ref=stages[f].at[d],
                dst_ref=lands[f].at[me],
                send_sem=data_send.at[f],
                recv_sem=data_recv.at[f],
                device_id=(w, n),
                device_id_type=MESH,
            ).start()

        return send

    def send_field(f):
        others(send_part(f), farthest_first)
        lands[f][me] = mine[f, my_own]

    for plane in planes:
        take_rows(plane)
        to_plane(plane, send_part(0))
    lands[0][me] = mine[0, my_own]
    for ref in (pad_ref, eta, warm, edge_in, corner_in, corner_out):
        ref[...] = jnp.zeros(ref.shape, jnp.float32)
    for f in range(1, FIELDS):
        lay_out(f)
        if f < AHEAD:
            send_field(f)

    for load in loads[FIELDS:]:
        load.wait()
    tracers = attr.shape[1]
    chunk = 1024 if tracers % 1024 == 0 else tracers
    means = bin_sums(me * blocks, holder, voxel, attr, blocks, chunk)
    left = lax.broadcasted_iota(jnp.int32, (8, 128), 1) < BINS
    for q in range(blocks // 2):
        pair = means[:, q * 128 : q * 128 + 128]
        across = pltpu.roll(pair, BINS, 1)
        below = pltpu.roll(pair, 4, 0)
        both = pltpu.roll(across, 4, 0)
        mean_mine[2 * q] = jnp.where(left, pair, both)[:4]
        mean_mine[2 * q + 1] = jnp.where(left, across, below)[:4]

    def send_mean(w, n):
        d = w * narrow_count + n
        mean_stage[d] = mean_mine[wanted(w, n)]
        pltpu.make_async_remote_copy(
            src_ref=mean_stage.at[d],
            dst_ref=mean_land.at[me],
            send_sem=mean_sems.at[0],
            recv_sem=mean_sems.at[1],
            device_id=(w, n),
            device_id_type=MESH,
        ).start()

    others(send_mean)
    mean_land[me] = mean_mine[my_own]

    def source_of(y, z):
        return lax.div(slot_ref[y * LZ + z], blocks)

    def grid_part(f, y):
        for z in range(LZ):
            held[pl.ds(z, rows, stride=LZ), :] = lands[f][source_of(y, z)]
        return swap_groups(held[: rows * LZ].reshape(rows, LZ, 128)).reshape(BS, BS, 128)

    ways = ((-1, 0), (1, 0), (0, -1), (0, 1), (-1, -1), (-1, 1), (1, -1), (1, 1))
    low_side = {-1: (wide > 0, narrow > 0), 1: (wide < wide_count - 1, narrow < narrow_count - 1)}

    def exists(way):
        there = [low_side[step][axis] for axis, step in enumerate(way) if step]
        return there[0] if len(there) == 1 else there[0] & there[1]

    def row_of(x, y):
        return (x + DEEP) * PITCH + FIRST + y

    def grid_rows(g, at):
        if g < 2:
            return (warm, eta)[g].at[at]
        return pad_ref.at[g - 2, at]

    def depth_of(g):
        return DEEP - 1 if g == 0 else DEEP

    def messages(g):
        found = []
        for i in range(DEEP):
            for way, slot in ((-1, i), (1, DEEP + i)):
                mine_x, theirs_x = (i, nx + i) if way < 0 else (nx - DEEP + i, i - DEEP)
                here_x = i - DEEP if way < 0 else nx + i
                rows_at = [
                    grid_rows(g, pl.ds(row_of(x, 0), ny)) for x in (mine_x, theirs_x, here_x)
                ]
                found.append(
                    ((way, 0), slot, rows_at[0], rows_at[1], (slot + DEEP) % (2 * DEEP), rows_at[2])
                )
        deep = pl.ds(0, depth_of(g))
        for side, way in enumerate((-1, 1)):
            slot = 2 * DEEP + side
            found.append(
                (
                    (0, way), slot, edge_out.at[g, side, deep], edge_in.at[g, 1 - side, deep],
                    2 * DEEP + 1 - side, edge_in.at[g, side, deep],
                )
            )
        for c, way in enumerate(ways[4:]):
            found.append(
                (
                    way, 2 * DEEP + 2 + c, corner_out.at[g, c], corner_in.at[g, 3 - c],
                    2 * DEEP + 5 - c, corner_in.at[g, c],
                )
            )
        return found

    def each_message(g, act):
        for way in ways[4:] + ways[:4]:
            group = [m for m in messages(g) if m[0] == way]

            @pl.when(exists(way))
            def _(way=way, group=group):
                for _, slot, source, target, far_slot, here in group:
                    act(way, slot, source, target, far_slot, here)

    def start_message(g):
        def act(way, slot, source, target, far_slot, here):
            pltpu.make_async_remote_copy(
                src_ref=source, dst_ref=target,
                send_sem=halo_send.at[g, slot], recv_sem=halo_recv.at[g, far_slot],
                device_id=(wide + way[0], narrow + way[1]), device_id_type=MESH,
            ).start()

        return act

    def wait_message(g, sent):
        def act(way, slot, source, target, far_slot, here):
            copy = pltpu.make_async_remote_copy(
                src_ref=source if sent else here, dst_ref=target if sent else here,
                send_sem=halo_send.at[g, slot], recv_sem=halo_recv.at[g, slot],
                device_id=(wide + way[0], narrow + way[1]), device_id_type=MESH,
            )
            copy.wait_send() if sent else copy.wait_recv()

        return act

    def read_rows(g, at):
        return (warm, eta)[g][at, :] if g < 2 else pad_ref[g - 2, at, :]

    def write_rows(g, at, value):
        if g < 2:
            (warm, eta)[g][at, :] = value
        else:
            pad_ref[g - 2, at, :] = value

    def send_halo(g):
        depth = depth_of(g)
        for side in range(2):
            for i in range(depth):
                y = i if side == 0 else ny - depth + i
                edge_out[g, side, i] = read_rows(g, pl.ds(row_of(0, y), nx, stride=PITCH))
        for c, (dx, dy) in enumerate(ways[4:]):
            for i in range(2):
                x = i if dx < 0 else nx - 2 + i
                y = 0 if dy < 0 else ny - 2
                corner_out[g, c, 2 * i : 2 * i + 2, :] = read_rows(g, pl.ds(row_of(x, y), 2))
        each_message(g, start_message(g))

    def take_halo(g):
        depth = depth_of(g)
        each_message(g, wait_message(g, False))
        for side in range(2):
            for i in range(depth):
                y = i - depth if side == 0 else ny + i
                write_rows(g, pl.ds(row_of(0, y), nx, stride=PITCH), edge_in[g, side, i])
        for c, (dx, dy) in enumerate(ways[4:]):
            for i in range(2):
                x = i - 2 if dx < 0 else nx + i
                y = -2 if dy < 0 else ny
                write_rows(g, pl.ds(row_of(x, y), 2), corner_in[g, c, 2 * i : 2 * i + 2, :])

    def viscosity():
        whole(mean_land, mean_sems.at[0], mean_sems.at[1]).wait_recv()
        expand = (
            lax.broadcasted_iota(jnp.int32, (LZ, 32), 0)
            == lax.broadcasted_iota(jnp.int32, (LZ, 32), 1) // 4
        ).astype(jnp.float32)
        same = (
            lax.broadcasted_iota(jnp.int32, (128, 32), 0) % 4
            == lax.broadcasted_iota(jnp.int32, (128, 32), 1) % 4
        )
        gather = (
            lax.broadcasted_iota(jnp.int32, (32, 128), 0)
            == lax.broadcasted_iota(jnp.int32, (32, 128), 1) // 4
        ).astype(jnp.float32)
        for y in range(LY):
            for z in range(LZ):
                mean_held[pl.ds(z, 4, stride=LZ), :] = mean_land[source_of(y, z)]
            for p in range(4):
                tall = jnp.dot(
                    mean_held[p * LZ : p * LZ + LZ].T, expand,
                    precision=lax.Precision.HIGHEST, preferred_element_type=jnp.float32,
                )
                cells = jnp.dot(
                    gather, jnp.where(same, tall, 0.0),
                    precision=lax.Precision.HIGHEST, preferred_element_type=jnp.float32,
                )
                for half in range(2):
                    for layer in range(4):
                        at = half * 16 + layer * 4
                        mean_ref[half * 4 + p, layer, y * 4 : y * 4 + 4, :] = cells[at : at + 4]
        for layer in range(4):
            mixture = MIX_WEIGHTS[0] * mean_ref[0, layer]
            for p in range(1, len(MIX_WEIGHTS)):
                mixture = mixture + MIX_WEIGHTS[p] * mean_ref[p, layer]
            wide_mix = jnp.dot(
                mixture, gather,
                precision=lax.Precision.HIGHEST, preferred_element_type=jnp.float32,
            )
            spread = jnp.concatenate(
                [jnp.broadcast_to(wide_mix[j : j + 1], (4, 128)) for j in range(LY * 4)], axis=0
            )
            for x in range(layer * 4, layer * 4 + 4):
                eta[pl.ds(row_of(x, 0), ny), :] = drag_grid[x] * jnp.exp(
                    HEAT_FACTOR * (0.5 - heat_ref[x]) + spread
                )

    wide_rows = (PITCH, (nx + 2 * DEEP - 1) * PITCH)

    def factor_rows(base):
        factors(base, STEP, eta, warm, side_ref, rest_ref)

    def drift_rows(base):
        found = drift(base, STEP, pad_ref, side_ref, rest_ref)
        for k in range(4):
            part_ref[k, pl.ds(base, STEP), :] = found[k]

    for f in range(FIELDS):
        whole(lands[f], data_send.at[f], data_recv.at[f]).wait_recv()
        if f + AHEAD < FIELDS:
            send_field(f + AHEAD)
        for y in range(LY):
            at = slice(y * BS, (y + 1) * BS)
            part = grid_part(f, y)
            if f == 0:
                heat_ref[:, at, :] = part
            if f == 1:
                drag_grid[:, at, :] = part
            else:
                for x in range(nx):
                    write_rows(f, pl.ds(row_of(x, y * BS), BS), part[x])
        if f == 1:
            viscosity()
            send_halo(0)
        if f > 0:
            send_halo(f)
        if f == 3:
            take_halo(0)
            take_halo(1)
            over_rows(*wide_rows, 10, factor_rows)
    for f in range(2, FIELDS - 1):
        take_halo(f)
    over_rows(*wide_rows, DRIFT_TURNS, drift_rows)
    whole(table, table_send, table_recv.at[0]).wait_send()
    whole(mean_land, mean_sems.at[0], mean_sems.at[1]).wait_send()
    for f in range(FIELDS):
        whole(lands[f], data_send.at[f], data_recv.at[f]).wait_send()
        each_message(f, wait_message(f, True))
    take_halo(FIELDS - 1)

def migrate(slots, flow, stress, heat, drag, attributes, holder, voxel):
    wide_count, narrow_count = lax.axis_size("wide"), lax.axis_size("narrow")
    count = wide_count * narrow_count
    blocks = slots.shape[0]
    tracers = attributes.shape[1]
    nx, ny, nz = LX * BS, LY * BS, LZ * BS
    rows = BS * BS * BS // 128
    pad_rows = (nx + 2 * DEEP) * PITCH + 8
    vmem = pl.BlockSpec(memory_space=pltpu.VMEM)
    hbm = pl.BlockSpec(memory_space=pltpu.HBM)
    f32 = jnp.float32
    per_field = [pltpu.VMEM((count, rows, 128), f32)] * FIELDS
    dma = pltpu.SemaphoreType.DMA
    pinned = [
        pltpu.with_memory_space_constraint(array, pltpu.HBM)
        for array in (slots, flow, stress, heat, drag, attributes, holder, voxel)
    ]
    return pl.pallas_call(
        functools.partial(migrate_kernel, wide_count=wide_count, narrow_count=narrow_count),
        out_shape=(
            jax.ShapeDtypeStruct((4, pad_rows, nz), f32),
            jax.ShapeDtypeStruct((4, pad_rows, nz), f32),
            jax.ShapeDtypeStruct((6, pad_rows, nz), f32),
            jax.ShapeDtypeStruct((3, pad_rows, nz), f32),
            jax.ShapeDtypeStruct((nx, ny, nz), f32),
            jax.ShapeDtypeStruct((8, LX * 4, LY * 4, LZ * 4), f32),
        ),
        in_specs=[hbm] * 8,
        out_specs=(vmem,) * 6,
        scratch_shapes=[
            pltpu.SMEM((blocks,), jnp.int32),
            pltpu.VMEM((1, 128), jnp.int32),
            pltpu.VMEM((count, 1, 128), jnp.int32),
            pltpu.SMEM((count, 1, 128), jnp.int32),
            pltpu.VMEM((FIELDS, blocks, rows * 128), f32),
            pltpu.VMEM((blocks * rows + rows, 128), f32),
            pltpu.VMEM((FIELDS, blocks, rows, 128), f32),
            *per_field,
            *per_field,
            pltpu.VMEM((8, tracers), f32),
            pltpu.VMEM((1, tracers), jnp.int32),
            pltpu.VMEM((1, tracers), jnp.int32),
            pltpu.VMEM((blocks, 4, 128), f32),
            pltpu.VMEM((count, 4, 128), f32),
            pltpu.VMEM((count, 4, 128), f32),
            pltpu.VMEM((4 * LZ + LZ, 128), f32),
            pltpu.VMEM((rows * LZ + LZ, 128), f32),
            pltpu.VMEM((nx, ny, nz), f32),
            pltpu.VMEM((pad_rows, nz), f32),
            pltpu.VMEM((pad_rows, nz), f32),
            pltpu.VMEM((FIELDS, 2, DEEP, nx, nz), f32),
            pltpu.VMEM((FIELDS, 2, DEEP, nx, nz), f32),
            pltpu.VMEM((FIELDS, 4, 8, nz), f32),
            pltpu.VMEM((FIELDS, 4, 8, nz), f32),
            dma((FIELDS + 3,)),
            dma(()),
            dma((narrow_count,)),
            dma((FIELDS,)),
            dma((FIELDS,)),
            dma((2,)),
            dma((FIELDS, 2 * DEEP + 6)),
            dma((FIELDS, 2 * DEEP + 6)),
            dma(()),
        ],
        compiler_params=pltpu.CompilerParams(
            collective_id=1,
            has_side_effects=True,
            vmem_limit_bytes=(24 if count <= 32 else 44) * 1024 * 1024,
        ),
    )(*pinned)


def relax_kernel(
    pad_ref, part_ref, side_ref, rest_ref, heat_ref, mean_ref,
    velocity_ref, pressure_ref, heat_out_ref, mean_out_ref, pad_1, pad_2, fresh, sems,
):
    nx, ny, nz = heat_ref.shape
    copies = []

    def send(source, target):
        copies.append(pltpu.make_async_copy(source, target, sems.at[len(copies)]))
        copies[-1].start()

    send(heat_ref, heat_out_ref)
    send(mean_ref, mean_out_ref)

    def finish_first(base):
        drifted = [part_ref[k, pl.ds(base, STEP), :] for k in range(4)]
        moved = push(base, STEP, pad_ref, rest_ref, drifted)
        for k in range(4):
            pad_1[k, pl.ds(base, STEP), :] = moved[k]

    def second(base):
        moved = relax(base, STEP, pad_1, side_ref, rest_ref)
        for k in range(4):
            pad_2[k, pl.ds(base, STEP), :] = moved[k]

    slabs = nx + 2 * DEEP
    over_rows(PITCH, (slabs - 1) * PITCH, TURNS, finish_first)
    over_rows(2 * PITCH, (slabs - 2) * PITCH, TURNS, second)

    parts = 4
    thick = nx // parts
    for part in range(parts):
        for x in range(part * thick, (part + 1) * thick):
            for half in range(0, ny, STEP):
                base = (x + DEEP) * PITCH + FIRST + half
                moved = relax(base, STEP, pad_2, side_ref, rest_ref)
                for k in range(4):
                    fresh[k, x, half : half + STEP, :] = moved[k]
        at = pl.ds(part * thick, thick)
        send(fresh.at[pl.ds(0, 3), at], velocity_ref.at[:, at])
        send(fresh.at[3, at], pressure_ref.at[at])
    for copy in copies:
        copy.wait()


def relax_all(pad, part, side, rest, heat, means):
    nx, ny, nz = heat.shape
    vmem = pl.BlockSpec(memory_space=pltpu.VMEM)
    hbm = pl.BlockSpec(memory_space=pltpu.HBM)
    return pl.pallas_call(
        relax_kernel,
        out_shape=(
            jax.ShapeDtypeStruct((3, nx, ny, nz), jnp.float32),
            jax.ShapeDtypeStruct((nx, ny, nz), jnp.float32),
            jax.ShapeDtypeStruct(heat.shape, jnp.float32),
            jax.ShapeDtypeStruct(means.shape, jnp.float32),
        ),
        in_specs=[vmem] * 6,
        out_specs=(hbm,) * 4,
        scratch_shapes=[
            pltpu.VMEM(pad.shape, jnp.float32),
            pltpu.VMEM(pad.shape, jnp.float32),
            pltpu.VMEM((4, nx, ny, nz), jnp.float32),
            pltpu.SemaphoreType.DMA((10,)),
        ],
        compiler_params=pltpu.CompilerParams(vmem_limit_bytes=16 * 1024 * 1024),
    )(pad, part, side, rest, heat, means)


def per_device(
    tile_flow_speed,
    tile_stress_mean,
    tile_heat_state,
    tile_drag_coefficient,
    marker_attributes,
    marker_holding_tile,
    marker_voxel_number,
    prior_slot_of_tile,
):
    tracers = marker_attributes.shape[1]
    results = migrate(
        prior_slot_of_tile,
        tile_flow_speed.transpose(1, 0, 2),
        tile_stress_mean,
        tile_heat_state,
        tile_drag_coefficient,
        marker_attributes,
        marker_holding_tile.reshape(1, tracers),
        marker_voxel_number.reshape(1, tracers),
    )
    return relax_all(*results)


def solution(mesh):
    in_specs = (
        P(("wide", "narrow"), None, None),
        P(("wide", "narrow"), None),
        P(("wide", "narrow"), None),
        P(("wide", "narrow"), None),
        P(None, ("wide", "narrow")),
        P(("wide", "narrow")),
        P(("wide", "narrow")),
        P(("wide", "narrow")),
    )
    out_specs = (
        P(None, "wide", "narrow", None),
        P("wide", "narrow", None),
        P("wide", "narrow", None),
        P(None, "wide", "narrow", None),
    )
    return jax.shard_map(
        per_device, mesh=mesh, in_specs=in_specs, out_specs=out_specs, check_vma=False
    )
```

```python
import functools

import jax
import jax.numpy as jnp
from jax import lax
from jax.experimental import pallas as pl
from jax.experimental.pallas import tpu as pltpu
from jax.sharding import PartitionSpec as P

BS = 16
LX = 1
LY = 2
LZ = 8
SWEEPS = 3
BINS = 64
FIELDS = 6
AHEAD = 3
PITCH = 40
FIRST = 8
DEEP = 3
STEP = 16
TURNS = 1
DRIFT_TURNS = 5

MIX_WEIGHTS = (0.3, -0.25, 0.2, -0.15, 0.35, -0.3, 0.25, -0.2)
RELAX_WEIGHT = 0.7
PRESSURE_WEIGHT = 0.3
HEAT_FACTOR = 2.0
DENSITY_FACTOR = 4.0
MESH = pl.DeviceIdType.MESH


def swap_groups(x):
    row = lax.broadcasted_iota(jnp.int32, x.shape, 1)
    group = lax.broadcasted_iota(jnp.int32, x.shape, 2) // BS
    for bit in (1, 2, 4):
        row_set = (row & bit) != 0
        group_set = (group & bit) != 0
        from_above = pltpu.roll(pltpu.roll(x, 8 - bit, 1), BS * bit, 2)
        from_below = pltpu.roll(pltpu.roll(x, bit, 1), 8 * BS - BS * bit, 2)
        x = jnp.where(
            row_set == group_set, x, jnp.where(group_set, from_above, from_below)
        )
    return x


def bin_sums(base, holder_ref, voxel_ref, attr_ref, blocks, chunk):
    props, tracers = attr_ref.shape
    total_bins = blocks * BINS
    bin_ids = lax.broadcasted_iota(jnp.int32, (total_bins, chunk), 0)

    def step(turn, sums):
        at = pl.ds(pl.multiple_of(turn * chunk, chunk), chunk)
        voxel = voxel_ref[:, at]
        key = (
            (holder_ref[:, at] - base) * BINS
            + (voxel >> 10) * 16
            + ((voxel >> 6) & 3) * 4
            + ((voxel >> 2) & 3)
        )
        table = jnp.where(bin_ids == key, 1.0, 0.0).astype(jnp.bfloat16)
        values = attr_ref[:, at]
        high = values.astype(jnp.bfloat16)
        rest = values - high.astype(jnp.float32)
        middle = rest.astype(jnp.bfloat16)
        low = (rest - middle.astype(jnp.float32)).astype(jnp.bfloat16)
        ones = jnp.ones((props, chunk), jnp.bfloat16)
        rows = jnp.concatenate([high, middle, low, ones], axis=0)
        return sums + lax.dot_general(
            rows, table, (((1,), (1,)), ((), ())), preferred_element_type=jnp.float32
        )

    sums = lax.fori_loop(
        0, tracers // chunk, step, jnp.zeros((4 * props, total_bins), jnp.float32)
    )
    total = sums[:props] + sums[props : 2 * props] + sums[2 * props : 3 * props]
    return total / jnp.maximum(sums[3 * props :], 1.0)


def at_ends(shape):
    column = lax.broadcasted_iota(jnp.int32, shape, 1)
    return column == 0, column == shape[1] - 1


def z_pair(here):
    low_end, high_end = at_ends(here.shape)
    nz = here.shape[1]
    return (
        jnp.where(high_end, 0.0, pltpu.roll(here, nz - 1, 1)),
        jnp.where(low_end, 0.0, pltpu.roll(here, 1, 1)),
    )


def factors(base, rows, eta_ref, heat_ref, side_ref, rest_ref):
    here = eta_ref[pl.ds(base, rows), :]
    around = [
        eta_ref[pl.ds(base + off, rows), :] for off in (PITCH, -PITCH, 1, -1)
    ] + list(z_pair(here))
    face = [0.5 * (here + other) for other in around]
    diagonal = face[0]
    for m in range(1, 6):
        diagonal = diagonal + face[m]
    inside = here > 0.0
    scale = jnp.where(inside, RELAX_WEIGHT / jnp.where(inside, diagonal, 1.0), 0.0)
    low_end, high_end = at_ends(here.shape)
    own = pl.ds(base, rows)
    for m in range(6):
        value = face[m] * scale
        if m == 4:
            value = jnp.where(high_end, 0.0, value)
        elif m == 5:
            value = jnp.where(low_end, 0.0, value)
        side_ref[m, own, :] = value
    rest_ref[0, own, :] = 0.5 * scale
    rest_ref[1, own, :] = (0.5 * PRESSURE_WEIGHT) * here
    rest_ref[2, own, :] = scale * (DENSITY_FACTOR * heat_ref[own, :])


def drift(base, rows, pad, side_ref, rest_ref):
    nz = pad.shape[2]
    own = pl.ds(base, rows)

    def value(k, off=0):
        return pad[k, pl.ds(base + off, rows), :]

    side = [side_ref[m, own, :] for m in range(6)]
    found = []
    divergence = None
    for k in range(3):
        here = value(k)
        if k == 2:
            up_z, down_z = z_pair(here)
        else:
            up_z, down_z = pltpu.roll(here, nz - 1, 1), pltpu.roll(here, 1, 1)
        near = (
            value(k, PITCH), value(k, -PITCH), value(k, 1), value(k, -1), up_z, down_z,
        )
        fresh = (1.0 - RELAX_WEIGHT) * here
        for m in range(6):
            fresh = fresh + side[m] * near[m]
        if k == 2:
            fresh = fresh + rest_ref[2, own, :]
        found.append(fresh)
        flux = near[2 * k] - near[2 * k + 1]
        divergence = flux if divergence is None else divergence + flux
    found.append(rest_ref[1, own, :] * divergence)
    return found


def push(base, rows, pad, rest_ref, drifted):
    own = pl.ds(base, rows)

    def value(off=0):
        return pad[3, pl.ds(base + off, rows), :]

    press = value()
    up_z, down_z = z_pair(press)
    half_scale = rest_ref[0, own, :]
    drops = (value(PITCH) - value(-PITCH), value(1) - value(-1), up_z - down_z)
    return [drifted[k] - half_scale * drops[k] for k in range(3)] + [press - drifted[3]]


def relax(base, rows, pad, side_ref, rest_ref):
    return push(base, rows, pad, rest_ref, drift(base, rows, pad, side_ref, rest_ref))


def over_rows(first, last, turns, act):
    together = (last - first) // (STEP * turns)
    assert together * STEP * turns == last - first

    def step(turn, carry):
        for i in range(together):
            act(pl.multiple_of(first + (turn * together + i) * STEP, 8))
        return carry

    lax.fori_loop(0, turns, step, 0)


def migrate_kernel(
    places_ref, flow_ref, stress_ref, warm_ref, drag_ref, attr_ref, holder_ref, voxel_ref,
    pad_ref, part_ref, side_ref, rest_ref, heat_ref, mean_ref,
    slot_ref, row_ref, table, table_smem, raw, lined, mine, stage_0, stage_1, stage_2, stage_3, stage_4, stage_5,
    land_0, land_1, land_2, land_3, land_4, land_5,
    attr, holder, voxel, mean_mine, mean_stage, mean_land, mean_held, held, drag_grid,
    eta, warm, edge_in, edge_out, corner_in, corner_out,
    raw_sems, table_send, table_recv, data_send, data_recv, mean_sems,
    halo_send, halo_recv, small_sem,
    *, wide_count, narrow_count,
):
    count = wide_count * narrow_count
    wide, narrow = lax.axis_index("wide"), lax.axis_index("narrow")
    me = wide * narrow_count + narrow
    blocks = raw.shape[1]
    nx, ny, nz = heat_ref.shape
    stages = (stage_0, stage_1, stage_2, stage_3, stage_4, stage_5)
    lands = (land_0, land_1, land_2, land_3, land_4, land_5)

    to_slots = pltpu.make_async_copy(places_ref, slot_ref, small_sem)
    to_slots.start()
    def flipped(k):
        place, bit = narrow, 1
        while bit < narrow_count:
            if k & bit:
                place = place + bit * (1 - 2 * lax.rem(lax.div(narrow, bit), 2))
            bit *= 2
        return place

    middle = narrow_count // 2
    upper = lax.div(narrow, middle)
    across = [(middle + i) * (1 - upper) + (middle - 1 - i) * upper for i in range(middle)]
    planes = across + [flipped(k) for k in range(1, middle)] + [narrow]
    farthest_first = across[::-1] + planes[middle:]

    def to_plane(plane, act):
        def step(a, carry):
            act(lax.rem(wide + a, wide_count), plane)
            return carry

        lax.fori_loop(1 if plane is narrow else 0, wide_count, step, 0)

    def others(act, order=planes):
        for plane in order:
            to_plane(plane, act)

    barrier = pltpu.get_barrier_semaphore()
    others(
        lambda w, n: pl.semaphore_signal(
            barrier, inc=1, device_id=(w, n), device_id_type=MESH
        ),
        farthest_first,
    )

    sources = (
        warm_ref, drag_ref, flow_ref.at[0], flow_ref.at[1], flow_ref.at[2], stress_ref,
    )
    loads = [
        pltpu.make_async_copy(source, raw.at[f], raw_sems.at[f]) for f, source in enumerate(sources)
    ]
    loads.append(pltpu.make_async_copy(attr_ref, attr, raw_sems.at[FIELDS]))
    loads.append(pltpu.make_async_copy(holder_ref, holder, raw_sems.at[FIELDS + 1]))
    loads.append(pltpu.make_async_copy(voxel_ref, voxel, raw_sems.at[FIELDS + 2]))
    for load in loads:
        load.start()

    to_slots.wait()
    lane = lax.broadcasted_iota(jnp.int32, (1, 128), 1)
    places = jnp.zeros((1, 128), jnp.int32)
    my_own = jnp.int32(0)
    for r in range(blocks):
        owner = lax.div(slot_ref[r], blocks)
        local = slot_ref[r] - owner * blocks
        places = jnp.where(lane == owner, local, places)
        my_own = jnp.where(owner == me, local, my_own)
    row_ref[...] = places
    table[narrow * wide_count + wide] = places
    pl.semaphore_wait(barrier, count - 1)

    def send_row(w, n):
        pltpu.make_async_remote_copy(
            src_ref=row_ref,
            dst_ref=table.at[narrow * wide_count + wide],
            send_sem=table_send,
            recv_sem=table_recv.at[narrow],
            device_id=(w, n),
            device_id_type=MESH,
        ).start()

    others(send_row)

    def whole(ref, send_sem, recv_sem):
        part = ref.at[pl.ds(0, count - 1)]
        return pltpu.make_async_remote_copy(
            src_ref=part,
            dst_ref=part,
            send_sem=send_sem,
            recv_sem=recv_sem,
            device_id=(wide, narrow),
            device_id_type=MESH,
        )

    rows = BS * BS * BS // 128
    def lay_out(f):
        loads[f].wait()
        for g in range(blocks // 8):
            for j in range(rows):
                lined[pl.ds(g * 8 * rows + j, 8, stride=rows), :] = raw[
                    f, g * 8 : g * 8 + 8, j * 128 : j * 128 + 128
                ]
        mine[f] = lined[: blocks * rows].reshape(blocks, rows, 128)

    lay_out(0)

    def take_rows(plane):
        rows_at = pl.ds(plane * wide_count, wide_count - 1 if plane is narrow else wide_count)
        part = table.at[rows_at]
        pltpu.make_async_remote_copy(
            src_ref=part, dst_ref=part, send_sem=table_send, recv_sem=table_recv.at[plane],
            device_id=(wide, narrow), device_id_type=MESH,
        ).wait_recv()
        rows_at = pl.ds(plane * wide_count, wide_count)
        to_scalar = pltpu.make_async_copy(table.at[rows_at], table_smem.at[rows_at], small_sem)
        to_scalar.start()
        to_scalar.wait()

    def wanted(w, n):
        return table_smem[n * wide_count + w, 0, me]

    def send_part(f):
        def send(w, n):
            d = w * narrow_count + n
            stages[f][d] = mine[f, wanted(w, n)]
            pltpu.make_async_remote_copy(
                src_ref=stages[f].at[d],
                dst_ref=lands[f].at[me],
                send_sem=data_send.at[f],
                recv_sem=data_recv.at[f],
                device_id=(w, n),
                device_id_type=MESH,
            ).start()

        return send

    def send_field(f):
        others(send_part(f), farthest_first)
        lands[f][me] = mine[f, my_own]

    for plane in planes:
        take_rows(plane)
        to_plane(plane, send_part(0))
    lands[0][me] = mine[0, my_own]
    for ref in (pad_ref, eta, warm, edge_in, corner_in, corner_out):
        ref[...] = jnp.zeros(ref.shape, jnp.float32)
    for f in range(1, FIELDS):
        lay_out(f)
        if f < AHEAD:
            send_field(f)

    for load in loads[FIELDS:]:
        load.wait()
    tracers = attr.shape[1]
    chunk = 1024 if tracers % 1024 == 0 else tracers
    means = bin_sums(me * blocks, holder, voxel, attr, blocks, chunk)
    left = lax.broadcasted_iota(jnp.int32, (8, 128), 1) < BINS
    for q in range(blocks // 2):
        pair = means[:, q * 128 : q * 128 + 128]
        across = pltpu.roll(pair, BINS, 1)
        below = pltpu.roll(pair, 4, 0)
        both = pltpu.roll(across, 4, 0)
        mean_mine[2 * q] = jnp.where(left, pair, both)[:4]
        mean_mine[2 * q + 1] = jnp.where(left, across, below)[:4]

    def send_mean(w, n):
        d = w * narrow_count + n
        mean_stage[d] = mean_mine[wanted(w, n)]
        pltpu.make_async_remote_copy(
            src_ref=mean_stage.at[d],
            dst_ref=mean_land.at[me],
            send_sem=mean_sems.at[0],
            recv_sem=mean_sems.at[1],
            device_id=(w, n),
            device_id_type=MESH,
        ).start()

    others(send_mean)
    mean_land[me] = mean_mine[my_own]

    def source_of(y, z):
        return lax.div(slot_ref[y * LZ + z], blocks)

    def grid_part(f, y):
        for z in range(LZ):
            held[pl.ds(z, rows, stride=LZ), :] = lands[f][source_of(y, z)]
        return swap_groups(held[: rows * LZ].reshape(rows, LZ, 128)).reshape(BS, BS, 128)

    ways = ((-1, 0), (1, 0), (0, -1), (0, 1), (-1, -1), (-1, 1), (1, -1), (1, 1))
    low_side = {-1: (wide > 0, narrow > 0), 1: (wide < wide_count - 1, narrow < narrow_count - 1)}

    def exists(way):
        there = [low_side[step][axis] for axis, step in enumerate(way) if step]
        return there[0] if len(there) == 1 else there[0] & there[1]

    def row_of(x, y):
        return (x + DEEP) * PITCH + FIRST + y

    def grid_rows(g, at):
        if g < 2:
            return (warm, eta)[g].at[at]
        return pad_ref.at[g - 2, at]

    def depth_of(g):
        return DEEP - 1 if g == 0 else DEEP

    def messages(g):
        found = []
        for i in range(DEEP):
            for way, slot in ((-1, i), (1, DEEP + i)):
                mine_x, theirs_x = (i, nx + i) if way < 0 else (nx - DEEP + i, i - DEEP)
                here_x = i - DEEP if way < 0 else nx + i
                rows_at = [
                    grid_rows(g, pl.ds(row_of(x, 0), ny)) for x in (mine_x, theirs_x, here_x)
                ]
                found.append(
                    ((way, 0), slot, rows_at[0], rows_at[1], (slot + DEEP) % (2 * DEEP), rows_at[2])
                )
        deep = pl.ds(0, depth_of(g))
        for side, way in enumerate((-1, 1)):
            slot = 2 * DEEP + side
            found.append(
                (
                    (0, way), slot, edge_out.at[g, side, deep], edge_in.at[g, 1 - side, deep],
                    2 * DEEP + 1 - side, edge_in.at[g, side, deep],
                )
            )
        for c, way in enumerate(ways[4:]):
            found.append(
                (
                    way, 2 * DEEP + 2 + c, corner_out.at[g, c], corner_in.at[g, 3 - c],
                    2 * DEEP + 5 - c, corner_in.at[g, c],
                )
            )
        return found

    def each_message(g, act):
        for way in ways[4:] + ways[:4]:
            group = [m for m in messages(g) if m[0] == way]

            @pl.when(exists(way))
            def _(way=way, group=group):
                for _, slot, source, target, far_slot, here in group:
                    act(way, slot, source, target, far_slot, here)

    def start_message(g):
        def act(way, slot, source, target, far_slot, here):
            pltpu.make_async_remote_copy(
                src_ref=source, dst_ref=target,
                send_sem=halo_send.at[g, slot], recv_sem=halo_recv.at[g, far_slot],
                device_id=(wide + way[0], narrow + way[1]), device_id_type=MESH,
            ).start()

        return act

    def wait_message(g, sent):
        def act(way, slot, source, target, far_slot, here):
            copy = pltpu.make_async_remote_copy(
                src_ref=source if sent else here, dst_ref=target if sent else here,
                send_sem=halo_send.at[g, slot], recv_sem=halo_recv.at[g, slot],
                device_id=(wide + way[0], narrow + way[1]), device_id_type=MESH,
            )
            copy.wait_send() if sent else copy.wait_recv()

        return act

    def read_rows(g, at):
        return (warm, eta)[g][at, :] if g < 2 else pad_ref[g - 2, at, :]

    def write_rows(g, at, value):
        if g < 2:
            (warm, eta)[g][at, :] = value
        else:
            pad_ref[g - 2, at, :] = value

    def send_halo(g):
        depth = depth_of(g)
        for side in range(2):
            for i in range(depth):
                y = i if side == 0 else ny - depth + i
                edge_out[g, side, i] = read_rows(g, pl.ds(row_of(0, y), nx, stride=PITCH))
        for c, (dx, dy) in enumerate(ways[4:]):
            for i in range(2):
                x = i if dx < 0 else nx - 2 + i
                y = 0 if dy < 0 else ny - 2
                corner_out[g, c, 2 * i : 2 * i + 2, :] = read_rows(g, pl.ds(row_of(x, y), 2))
        each_message(g, start_message(g))

    def take_halo(g):
        depth = depth_of(g)
        each_message(g, wait_message(g, False))
        for side in range(2):
            for i in range(depth):
                y = i - depth if side == 0 else ny + i
                write_rows(g, pl.ds(row_of(0, y), nx, stride=PITCH), edge_in[g, side, i])
        for c, (dx, dy) in enumerate(ways[4:]):
            for i in range(2):
                x = i - 2 if dx < 0 else nx + i
                y = -2 if dy < 0 else ny
                write_rows(g, pl.ds(row_of(x, y), 2), corner_in[g, c, 2 * i : 2 * i + 2, :])

    def viscosity():
        whole(mean_land, mean_sems.at[0], mean_sems.at[1]).wait_recv()
        expand = (
            lax.broadcasted_iota(jnp.int32, (LZ, 32), 0)
            == lax.broadcasted_iota(jnp.int32, (LZ, 32), 1) // 4
        ).astype(jnp.float32)
        same = (
            lax.broadcasted_iota(jnp.int32, (128, 32), 0) % 4
            == lax.broadcasted_iota(jnp.int32, (128, 32), 1) % 4
        )
        gather = (
            lax.broadcasted_iota(jnp.int32, (32, 128), 0)
            == lax.broadcasted_iota(jnp.int32, (32, 128), 1) // 4
        ).astype(jnp.float32)
        for y in range(LY):
            for z in range(LZ):
                mean_held[pl.ds(z, 4, stride=LZ), :] = mean_land[source_of(y, z)]
            for p in range(4):
                tall = jnp.dot(
                    mean_held[p * LZ : p * LZ + LZ].T, expand,
                    precision=lax.Precision.HIGHEST, preferred_element_type=jnp.float32,
                )
                cells = jnp.dot(
                    gather, jnp.where(same, tall, 0.0),
                    precision=lax.Precision.HIGHEST, preferred_element_type=jnp.float32,
                )
                for half in range(2):
                    for layer in range(4):
                        at = half * 16 + layer * 4
                        mean_ref[half * 4 + p, layer, y * 4 : y * 4 + 4, :] = cells[at : at + 4]
        for layer in range(4):
            mixture = MIX_WEIGHTS[0] * mean_ref[0, layer]
            for p in range(1, len(MIX_WEIGHTS)):
                mixture = mixture + MIX_WEIGHTS[p] * mean_ref[p, layer]
            wide_mix = jnp.dot(
                mixture, gather,
                precision=lax.Precision.HIGHEST, preferred_element_type=jnp.float32,
            )
            spread = jnp.concatenate(
                [jnp.broadcast_to(wide_mix[j : j + 1], (4, 128)) for j in range(LY * 4)], axis=0
            )
            for x in range(layer * 4, layer * 4 + 4):
                eta[pl.ds(row_of(x, 0), ny), :] = drag_grid[x] * jnp.exp(
                    HEAT_FACTOR * (0.5 - heat_ref[x]) + spread
                )

    wide_rows = (PITCH, (nx + 2 * DEEP - 1) * PITCH)

    def factor_rows(base):
        factors(base, STEP, eta, warm, side_ref, rest_ref)

    def drift_rows(base):
        found = drift(base, STEP, pad_ref, side_ref, rest_ref)
        for k in range(4):
            part_ref[k, pl.ds(base, STEP), :] = found[k]

    for f in range(FIELDS):
        whole(lands[f], data_send.at[f], data_recv.at[f]).wait_recv()
        if f + AHEAD < FIELDS:
            send_field(f + AHEAD)
        for y in range(LY):
            at = slice(y * BS, (y + 1) * BS)
            part = grid_part(f, y)
            if f == 0:
                heat_ref[:, at, :] = part
            if f == 1:
                drag_grid[:, at, :] = part
            else:
                for x in range(nx):
                    write_rows(f, pl.ds(row_of(x, y * BS), BS), part[x])
        if f == 1:
            viscosity()
            send_halo(0)
        if f > 0:
            send_halo(f)
        if f == 3:
            take_halo(0)
            take_halo(1)
            over_rows(*wide_rows, 10, factor_rows)
    for f in range(2, FIELDS - 1):
        take_halo(f)
    over_rows(*wide_rows, DRIFT_TURNS, drift_rows)
    whole(table, table_send, table_recv.at[0]).wait_send()
    whole(mean_land, mean_sems.at[0], mean_sems.at[1]).wait_send()
    for f in range(FIELDS):
        whole(lands[f], data_send.at[f], data_recv.at[f]).wait_send()
        each_message(f, wait_message(f, True))
    take_halo(FIELDS - 1)

def migrate(slots, flow, stress, heat, drag, attributes, holder, voxel):
    wide_count, narrow_count = lax.axis_size("wide"), lax.axis_size("narrow")
    count = wide_count * narrow_count
    blocks = slots.shape[0]
    tracers = attributes.shape[1]
    nx, ny, nz = LX * BS, LY * BS, LZ * BS
    rows = BS * BS * BS // 128
    pad_rows = (nx + 2 * DEEP) * PITCH + 8
    vmem = pl.BlockSpec(memory_space=pltpu.VMEM)
    hbm = pl.BlockSpec(memory_space=pltpu.HBM)
    f32 = jnp.float32
    per_field = [pltpu.VMEM((count, rows, 128), f32)] * FIELDS
    dma = pltpu.SemaphoreType.DMA
    pinned = [
        pltpu.with_memory_space_constraint(array, pltpu.HBM)
        for array in (slots, flow, stress, heat, drag, attributes, holder, voxel)
    ]
    return pl.pallas_call(
        functools.partial(migrate_kernel, wide_count=wide_count, narrow_count=narrow_count),
        out_shape=(
            jax.ShapeDtypeStruct((4, pad_rows, nz), f32),
            jax.ShapeDtypeStruct((4, pad_rows, nz), f32),
            jax.ShapeDtypeStruct((6, pad_rows, nz), f32),
            jax.ShapeDtypeStruct((3, pad_rows, nz), f32),
            jax.ShapeDtypeStruct((nx, ny, nz), f32),
            jax.ShapeDtypeStruct((8, LX * 4, LY * 4, LZ * 4), f32),
        ),
        in_specs=[hbm] * 8,
        out_specs=(vmem,) * 6,
        scratch_shapes=[
            pltpu.SMEM((blocks,), jnp.int32),
            pltpu.VMEM((1, 128), jnp.int32),
            pltpu.VMEM((count, 1, 128), jnp.int32),
            pltpu.SMEM((count, 1, 128), jnp.int32),
            pltpu.VMEM((FIELDS, blocks, rows * 128), f32),
            pltpu.VMEM((blocks * rows + rows, 128), f32),
            pltpu.VMEM((FIELDS, blocks, rows, 128), f32),
            *per_field,
            *per_field,
            pltpu.VMEM((8, tracers), f32),
            pltpu.VMEM((1, tracers), jnp.int32),
            pltpu.VMEM((1, tracers), jnp.int32),
            pltpu.VMEM((blocks, 4, 128), f32),
            pltpu.VMEM((count, 4, 128), f32),
            pltpu.VMEM((count, 4, 128), f32),
            pltpu.VMEM((4 * LZ + LZ, 128), f32),
            pltpu.VMEM((rows * LZ + LZ, 128), f32),
            pltpu.VMEM((nx, ny, nz), f32),
            pltpu.VMEM((pad_rows, nz), f32),
            pltpu.VMEM((pad_rows, nz), f32),
            pltpu.VMEM((FIELDS, 2, DEEP, nx, nz), f32),
            pltpu.VMEM((FIELDS, 2, DEEP, nx, nz), f32),
            pltpu.VMEM((FIELDS, 4, 4, nz), f32),
            pltpu.VMEM((FIELDS, 4, 4, nz), f32),
            dma((FIELDS + 3,)),
            dma(()),
            dma((narrow_count,)),
            dma((FIELDS,)),
            dma((FIELDS,)),
            dma((2,)),
            dma((FIELDS, 2 * DEEP + 6)),
            dma((FIELDS, 2 * DEEP + 6)),
            dma(()),
        ],
        compiler_params=pltpu.CompilerParams(
            collective_id=1,
            has_side_effects=True,
            vmem_limit_bytes=(24 if count <= 32 else 44) * 1024 * 1024,
        ),
    )(*pinned)


def relax_kernel(
    pad_ref, part_ref, side_ref, rest_ref, heat_ref, mean_ref,
    velocity_ref, pressure_ref, heat_out_ref, mean_out_ref, pad_1, pad_2, fresh, sems,
):
    nx, ny, nz = heat_ref.shape
    copies = []

    def send(source, target):
        copies.append(pltpu.make_async_copy(source, target, sems.at[len(copies)]))
        copies[-1].start()

    send(heat_ref, heat_out_ref)
    send(mean_ref, mean_out_ref)

    def finish_first(base):
        drifted = [part_ref[k, pl.ds(base, STEP), :] for k in range(4)]
        moved = push(base, STEP, pad_ref, rest_ref, drifted)
        for k in range(4):
            pad_1[k, pl.ds(base, STEP), :] = moved[k]

    def second(base):
        moved = relax(base, STEP, pad_1, side_ref, rest_ref)
        for k in range(4):
            pad_2[k, pl.ds(base, STEP), :] = moved[k]

    slabs = nx + 2 * DEEP
    over_rows(PITCH, (slabs - 1) * PITCH, TURNS, finish_first)
    over_rows(2 * PITCH, (slabs - 2) * PITCH, TURNS, second)

    parts = 4
    thick = nx // parts
    for part in range(parts):
        for x in range(part * thick, (part + 1) * thick):
            for half in range(0, ny, STEP):
                base = (x + DEEP) * PITCH + FIRST + half
                moved = relax(base, STEP, pad_2, side_ref, rest_ref)
                for k in range(4):
                    fresh[k, x, half : half + STEP, :] = moved[k]
        at = pl.ds(part * thick, thick)
        send(fresh.at[pl.ds(0, 3), at], velocity_ref.at[:, at])
        send(fresh.at[3, at], pressure_ref.at[at])
    for copy in copies:
        copy.wait()


def relax_all(pad, part, side, rest, heat, means):
    nx, ny, nz = heat.shape
    vmem = pl.BlockSpec(memory_space=pltpu.VMEM)
    hbm = pl.BlockSpec(memory_space=pltpu.HBM)
    return pl.pallas_call(
        relax_kernel,
        out_shape=(
            jax.ShapeDtypeStruct((3, nx, ny, nz), jnp.float32),
            jax.ShapeDtypeStruct((nx, ny, nz), jnp.float32),
            jax.ShapeDtypeStruct(heat.shape, jnp.float32),
            jax.ShapeDtypeStruct(means.shape, jnp.float32),
        ),
        in_specs=[vmem] * 6,
        out_specs=(hbm,) * 4,
        scratch_shapes=[
            pltpu.VMEM(pad.shape, jnp.float32),
            pltpu.VMEM(pad.shape, jnp.float32),
            pltpu.VMEM((4, nx, ny, nz), jnp.float32),
            pltpu.SemaphoreType.DMA((10,)),
        ],
        compiler_params=pltpu.CompilerParams(vmem_limit_bytes=16 * 1024 * 1024),
    )(pad, part, side, rest, heat, means)


def per_device(
    tile_flow_speed,
    tile_stress_mean,
    tile_heat_state,
    tile_drag_coefficient,
    marker_attributes,
    marker_holding_tile,
    marker_voxel_number,
    prior_slot_of_tile,
):
    tracers = marker_attributes.shape[1]
    results = migrate(
        prior_slot_of_tile,
        tile_flow_speed.transpose(1, 0, 2),
        tile_stress_mean,
        tile_heat_state,
        tile_drag_coefficient,
        marker_attributes,
        marker_holding_tile.reshape(1, tracers),
        marker_voxel_number.reshape(1, tracers),
    )
    return relax_all(*results)


def solution(mesh):
    in_specs = (
        P(("wide", "narrow"), None, None),
        P(("wide", "narrow"), None),
        P(("wide", "narrow"), None),
        P(("wide", "narrow"), None),
        P(None, ("wide", "narrow")),
        P(("wide", "narrow")),
        P(("wide", "narrow")),
        P(("wide", "narrow")),
    )
    out_specs = (
        P(None, "wide", "narrow", None),
        P("wide", "narrow", None),
        P("wide", "narrow", None),
        P(None, "wide", "narrow", None),
    )
    return jax.shard_map(
        per_device, mesh=mesh, in_specs=in_specs, out_specs=out_specs, check_vma=False
    )
```

```python
import functools

import jax
import jax.numpy as jnp
from jax import lax
from jax.experimental import pallas as pl
from jax.experimental.pallas import tpu as pltpu
from jax.sharding import PartitionSpec as P

BS = 16
LX = 1
LY = 2
LZ = 8
SWEEPS = 3
BINS = 64
FIELDS = 6
AHEAD = 3
PITCH = 40
FIRST = 8
DEEP = 3
STEP = 16
TURNS = 1
DRIFT_TURNS = 5

MIX_WEIGHTS = (0.3, -0.25, 0.2, -0.15, 0.35, -0.3, 0.25, -0.2)
RELAX_WEIGHT = 0.7
PRESSURE_WEIGHT = 0.3
HEAT_FACTOR = 2.0
DENSITY_FACTOR = 4.0
MESH = pl.DeviceIdType.MESH


def swap_groups(x):
    row = lax.broadcasted_iota(jnp.int32, x.shape, 1)
    group = lax.broadcasted_iota(jnp.int32, x.shape, 2) // BS
    for bit in (1, 2, 4):
        row_set = (row & bit) != 0
        group_set = (group & bit) != 0
        from_above = pltpu.roll(pltpu.roll(x, 8 - bit, 1), BS * bit, 2)
        from_below = pltpu.roll(pltpu.roll(x, bit, 1), 8 * BS - BS * bit, 2)
        x = jnp.where(
            row_set == group_set, x, jnp.where(group_set, from_above, from_below)
        )
    return x


def bin_sums(base, holder_ref, voxel_ref, attr_ref, blocks, chunk):
    props, tracers = attr_ref.shape
    total_bins = blocks * BINS
    bin_ids = lax.broadcasted_iota(jnp.int32, (total_bins, chunk), 0)

    def step(turn, sums):
        at = pl.ds(pl.multiple_of(turn * chunk, chunk), chunk)
        voxel = voxel_ref[:, at]
        key = (
            (holder_ref[:, at] - base) * BINS
            + (voxel >> 10) * 16
            + ((voxel >> 6) & 3) * 4
            + ((voxel >> 2) & 3)
        )
        table = jnp.where(bin_ids == key, 1.0, 0.0).astype(jnp.bfloat16)
        values = attr_ref[:, at]
        high = values.astype(jnp.bfloat16)
        rest = values - high.astype(jnp.float32)
        middle = rest.astype(jnp.bfloat16)
        low = (rest - middle.astype(jnp.float32)).astype(jnp.bfloat16)
        ones = jnp.ones((props, chunk), jnp.bfloat16)
        rows = jnp.concatenate([high, middle, low, ones], axis=0)
        return sums + lax.dot_general(
            rows, table, (((1,), (1,)), ((), ())), preferred_element_type=jnp.float32
        )

    sums = lax.fori_loop(
        0, tracers // chunk, step, jnp.zeros((4 * props, total_bins), jnp.float32)
    )
    total = sums[:props] + sums[props : 2 * props] + sums[2 * props : 3 * props]
    return total / jnp.maximum(sums[3 * props :], 1.0)


def at_ends(shape):
    column = lax.broadcasted_iota(jnp.int32, shape, 1)
    return column == 0, column == shape[1] - 1


def z_pair(here):
    low_end, high_end = at_ends(here.shape)
    nz = here.shape[1]
    return (
        jnp.where(high_end, 0.0, pltpu.roll(here, nz - 1, 1)),
        jnp.where(low_end, 0.0, pltpu.roll(here, 1, 1)),
    )


def factors(base, rows, eta_ref, heat_ref, side_ref, rest_ref):
    here = eta_ref[pl.ds(base, rows), :]
    around = [
        eta_ref[pl.ds(base + off, rows), :] for off in (PITCH, -PITCH, 1, -1)
    ] + list(z_pair(here))
    face = [0.5 * (here + other) for other in around]
    diagonal = face[0]
    for m in range(1, 6):
        diagonal = diagonal + face[m]
    inside = here > 0.0
    scale = jnp.where(inside, RELAX_WEIGHT / jnp.where(inside, diagonal, 1.0), 0.0)
    low_end, high_end = at_ends(here.shape)
    own = pl.ds(base, rows)
    for m in range(6):
        value = face[m] * scale
        if m == 4:
            value = jnp.where(high_end, 0.0, value)
        elif m == 5:
            value = jnp.where(low_end, 0.0, value)
        side_ref[m, own, :] = value
    rest_ref[0, own, :] = 0.5 * scale
    rest_ref[1, own, :] = (0.5 * PRESSURE_WEIGHT) * here
    rest_ref[2, own, :] = scale * (DENSITY_FACTOR * heat_ref[own, :])


def drift(base, rows, pad, side_ref, rest_ref):
    nz = pad.shape[2]
    own = pl.ds(base, rows)

    def value(k, off=0):
        return pad[k, pl.ds(base + off, rows), :]

    side = [side_ref[m, own, :] for m in range(6)]
    found = []
    divergence = None
    for k in range(3):
        here = value(k)
        if k == 2:
            up_z, down_z = z_pair(here)
        else:
            up_z, down_z = pltpu.roll(here, nz - 1, 1), pltpu.roll(here, 1, 1)
        near = (
            value(k, PITCH), value(k, -PITCH), value(k, 1), value(k, -1), up_z, down_z,
        )
        fresh = (1.0 - RELAX_WEIGHT) * here
        for m in range(6):
            fresh = fresh + side[m] * near[m]
        if k == 2:
            fresh = fresh + rest_ref[2, own, :]
        found.append(fresh)
        flux = near[2 * k] - near[2 * k + 1]
        divergence = flux if divergence is None else divergence + flux
    found.append(rest_ref[1, own, :] * divergence)
    return found


def push(base, rows, pad, rest_ref, drifted):
    own = pl.ds(base, rows)

    def value(off=0):
        return pad[3, pl.ds(base + off, rows), :]

    press = value()
    up_z, down_z = z_pair(press)
    half_scale = rest_ref[0, own, :]
    drops = (value(PITCH) - value(-PITCH), value(1) - value(-1), up_z - down_z)
    return [drifted[k] - half_scale * drops[k] for k in range(3)] + [press - drifted[3]]


def relax(base, rows, pad, side_ref, rest_ref):
    return push(base, rows, pad, rest_ref, drift(base, rows, pad, side_ref, rest_ref))


def over_rows(first, last, turns, act):
    together = (last - first) // (STEP * turns)
    assert together * STEP * turns == last - first

    def step(turn, carry):
        for i in range(together):
            act(pl.multiple_of(first + (turn * together + i) * STEP, 8))
        return carry

    lax.fori_loop(0, turns, step, 0)


def migrate_kernel(
    places_ref, flow_ref, stress_ref, warm_ref, drag_ref, attr_ref, holder_ref, voxel_ref,
    pad_ref, part_ref, side_ref, rest_ref, heat_ref, mean_ref,
    slot_ref, row_ref, table, table_smem, raw, lined, mine, stage_0, stage_1, stage_2, stage_3, stage_4, stage_5,
    land_0, land_1, land_2, land_3, land_4, land_5,
    attr, holder, voxel, mean_mine, mean_stage, mean_land, mean_held, held, drag_grid,
    eta, warm, edge_in, edge_out, corner_in, corner_out,
    raw_sems, table_send, table_recv, data_send, data_recv, mean_sems,
    halo_send, halo_recv, small_sem,
    *, wide_count, narrow_count,
):
    count = wide_count * narrow_count
    wide, narrow = lax.axis_index("wide"), lax.axis_index("narrow")
    me = wide * narrow_count + narrow
    blocks = raw.shape[1]
    nx, ny, nz = heat_ref.shape
    stages = (stage_0, stage_1, stage_2, stage_3, stage_4, stage_5)
    lands = (land_0, land_1, land_2, land_3, land_4, land_5)

    to_slots = pltpu.make_async_copy(places_ref, slot_ref, small_sem)
    to_slots.start()
    def flipped(k):
        place, bit = narrow, 1
        while bit < narrow_count:
            if k & bit:
                place = place + bit * (1 - 2 * lax.rem(lax.div(narrow, bit), 2))
            bit *= 2
        return place

    middle = narrow_count // 2
    upper = lax.div(narrow, middle)
    across = [(middle + i) * (1 - upper) + (middle - 1 - i) * upper for i in range(middle)]
    planes = across + [flipped(k) for k in range(1, middle)] + [narrow]
    farthest_first = across[::-1] + planes[middle:]

    def to_plane(plane, act):
        def step(a, carry):
            act(lax.rem(wide + a, wide_count), plane)
            return carry

        lax.fori_loop(1 if plane is narrow else 0, wide_count, step, 0)

    def others(act, order=planes):
        for plane in order:
            to_plane(plane, act)

    barrier = pltpu.get_barrier_semaphore()
    others(
        lambda w, n: pl.semaphore_signal(
            barrier, inc=1, device_id=(w, n), device_id_type=MESH
        ),
        farthest_first,
    )

    sources = (
        warm_ref, drag_ref, flow_ref.at[0], flow_ref.at[1], flow_ref.at[2], stress_ref,
    )
    loads = [
        pltpu.make_async_copy(source, raw.at[f], raw_sems.at[f]) for f, source in enumerate(sources)
    ]
    loads.append(pltpu.make_async_copy(attr_ref, attr, raw_sems.at[FIELDS]))
    loads.append(pltpu.make_async_copy(holder_ref, holder, raw_sems.at[FIELDS + 1]))
    loads.append(pltpu.make_async_copy(voxel_ref, voxel, raw_sems.at[FIELDS + 2]))
    for load in loads:
        load.start()

    to_slots.wait()
    lane = lax.broadcasted_iota(jnp.int32, (1, 128), 1)
    places = jnp.zeros((1, 128), jnp.int32)
    my_own = jnp.int32(0)
    for r in range(blocks):
        owner = lax.div(slot_ref[r], blocks)
        local = slot_ref[r] - owner * blocks
        places = jnp.where(lane == owner, local, places)
        my_own = jnp.where(owner == me, local, my_own)
    row_ref[...] = places
    table[narrow * wide_count + wide] = places
    pl.semaphore_wait(barrier, count - 1)

    def send_row(w, n):
        pltpu.make_async_remote_copy(
            src_ref=row_ref,
            dst_ref=table.at[narrow * wide_count + wide],
            send_sem=table_send,
            recv_sem=table_recv.at[narrow],
            device_id=(w, n),
            device_id_type=MESH,
        ).start()

    others(send_row)

    def whole(ref, send_sem, recv_sem):
        part = ref.at[pl.ds(0, count - 1)]
        return pltpu.make_async_remote_copy(
            src_ref=part,
            dst_ref=part,
            send_sem=send_sem,
            recv_sem=recv_sem,
            device_id=(wide, narrow),
            device_id_type=MESH,
        )

    rows = BS * BS * BS // 128
    def lay_out(f):
        loads[f].wait()
        for g in range(blocks // 8):
            for j in range(rows):
                lined[pl.ds(g * 8 * rows + j, 8, stride=rows), :] = raw[
                    f, g * 8 : g * 8 + 8, j * 128 : j * 128 + 128
                ]
        mine[f] = lined[: blocks * rows].reshape(blocks, rows, 128)

    lay_out(0)

    def take_rows(plane):
        rows_at = pl.ds(plane * wide_count, wide_count - 1 if plane is narrow else wide_count)
        part = table.at[rows_at]
        pltpu.make_async_remote_copy(
            src_ref=part, dst_ref=part, send_sem=table_send, recv_sem=table_recv.at[plane],
            device_id=(wide, narrow), device_id_type=MESH,
        ).wait_recv()
        rows_at = pl.ds(plane * wide_count, wide_count)
        to_scalar = pltpu.make_async_copy(table.at[rows_at], table_smem.at[rows_at], small_sem)
        to_scalar.start()
        to_scalar.wait()

    def wanted(w, n):
        return table_smem[n * wide_count + w, 0, me]

    def send_part(f):
        def send(w, n):
            d = w * narrow_count + n
            stages[f][d] = mine[f, wanted(w, n)]
            pltpu.make_async_remote_copy(
                src_ref=stages[f].at[d],
                dst_ref=lands[f].at[me],
                send_sem=data_send.at[f],
                recv_sem=data_recv.at[f],
                device_id=(w, n),
                device_id_type=MESH,
            ).start()

        return send

    def send_field(f):
        others(send_part(f), farthest_first)
        lands[f][me] = mine[f, my_own]

    for plane in planes:
        take_rows(plane)
        to_plane(plane, send_part(0))
    lands[0][me] = mine[0, my_own]
    for ref in (pad_ref, eta, warm, edge_in, corner_in, corner_out):
        ref[...] = jnp.zeros(ref.shape, jnp.float32)
    for f in range(1, FIELDS):
        lay_out(f)
        if f < AHEAD:
            send_field(f)

    for load in loads[FIELDS:]:
        load.wait()
    tracers = attr.shape[1]
    chunk = 1024 if tracers % 1024 == 0 else tracers
    means = bin_sums(me * blocks, holder, voxel, attr, blocks, chunk)
    left = lax.broadcasted_iota(jnp.int32, (8, 128), 1) < BINS
    for q in range(blocks // 2):
        pair = means[:, q * 128 : q * 128 + 128]
        across = pltpu.roll(pair, BINS, 1)
        below = pltpu.roll(pair, 4, 0)
        both = pltpu.roll(across, 4, 0)
        mean_mine[2 * q] = jnp.where(left, pair, both)[:4]
        mean_mine[2 * q + 1] = jnp.where(left, across, below)[:4]

    def send_mean(w, n):
        d = w * narrow_count + n
        mean_stage[d] = mean_mine[wanted(w, n)]
        pltpu.make_async_remote_copy(
            src_ref=mean_stage.at[d],
            dst_ref=mean_land.at[me],
            send_sem=mean_sems.at[0],
            recv_sem=mean_sems.at[1],
            device_id=(w, n),
            device_id_type=MESH,
        ).start()

    others(send_mean)
    mean_land[me] = mean_mine[my_own]

    def source_of(y, z):
        return lax.div(slot_ref[y * LZ + z], blocks)

    def grid_part(f, y):
        for z in range(LZ):
            held[pl.ds(z, rows, stride=LZ), :] = lands[f][source_of(y, z)]
        return swap_groups(held[: rows * LZ].reshape(rows, LZ, 128)).reshape(BS, BS, 128)

    ways = ((-1, 0), (1, 0), (0, -1), (0, 1), (-1, -1), (-1, 1), (1, -1), (1, 1))
    low_side = {-1: (wide > 0, narrow > 0), 1: (wide < wide_count - 1, narrow < narrow_count - 1)}

    def exists(way):
        there = [low_side[step][axis] for axis, step in enumerate(way) if step]
        return there[0] if len(there) == 1 else there[0] & there[1]

    def row_of(x, y):
        return (x + DEEP) * PITCH + FIRST + y

    def grid_rows(g, at):
        if g < 2:
            return (warm, eta)[g].at[at]
        return pad_ref.at[g - 2, at]

    def depth_of(g):
        return DEEP - 1 if g == 0 else DEEP

    def messages(g):
        found = []
        for i in range(DEEP):
            for way, slot in ((-1, i), (1, DEEP + i)):
                mine_x, theirs_x = (i, nx + i) if way < 0 else (nx - DEEP + i, i - DEEP)
                here_x = i - DEEP if way < 0 else nx + i
                rows_at = [
                    grid_rows(g, pl.ds(row_of(x, 0), ny)) for x in (mine_x, theirs_x, here_x)
                ]
                found.append(
                    ((way, 0), slot, rows_at[0], rows_at[1], (slot + DEEP) % (2 * DEEP), rows_at[2])
                )
        deep = pl.ds(0, depth_of(g))
        for side, way in enumerate((-1, 1)):
            slot = 2 * DEEP + side
            found.append(
                (
                    (0, way), slot, edge_out.at[g, side, deep], edge_in.at[g, 1 - side, deep],
                    2 * DEEP + 1 - side, edge_in.at[g, side, deep],
                )
            )
        for c, way in enumerate(ways[4:]):
            found.append(
                (
                    way, 2 * DEEP + 2 + c, corner_out.at[g, c], corner_in.at[g, 3 - c],
                    2 * DEEP + 5 - c, corner_in.at[g, c],
                )
            )
        return found

    def each_message(g, act):
        for way in ways[4:] + ways[:4]:
            group = [m for m in messages(g) if m[0] == way]

            @pl.when(exists(way))
            def _(way=way, group=group):
                for _, slot, source, target, far_slot, here in group:
                    act(way, slot, source, target, far_slot, here)

    def start_message(g):
        def act(way, slot, source, target, far_slot, here):
            pltpu.make_async_remote_copy(
                src_ref=source, dst_ref=target,
                send_sem=halo_send.at[g, slot], recv_sem=halo_recv.at[g, far_slot],
                device_id=(wide + way[0], narrow + way[1]), device_id_type=MESH,
            ).start()

        return act

    def wait_message(g, sent):
        def act(way, slot, source, target, far_slot, here):
            copy = pltpu.make_async_remote_copy(
                src_ref=source if sent else here, dst_ref=target if sent else here,
                send_sem=halo_send.at[g, slot], recv_sem=halo_recv.at[g, slot],
                device_id=(wide + way[0], narrow + way[1]), device_id_type=MESH,
            )
            copy.wait_send() if sent else copy.wait_recv()

        return act

    def read_rows(g, at):
        return (warm, eta)[g][at, :] if g < 2 else pad_ref[g - 2, at, :]

    def write_rows(g, at, value):
        if g < 2:
            (warm, eta)[g][at, :] = value
        else:
            pad_ref[g - 2, at, :] = value

    def send_halo(g):
        depth = depth_of(g)
        for side in range(2):
            for i in range(depth):
                y = i if side == 0 else ny - depth + i
                edge_out[g, side, i] = read_rows(g, pl.ds(row_of(0, y), nx, stride=PITCH))
        for c, (dx, dy) in enumerate(ways[4:]):
            for i in range(2):
                x = i if dx < 0 else nx - 2 + i
                y = 0 if dy < 0 else ny - 2
                corner_out[g, c, 2 * i : 2 * i + 2, :] = read_rows(g, pl.ds(row_of(x, y), 2))
        each_message(g, start_message(g))

    def take_halo(g):
        depth = depth_of(g)
        each_message(g, wait_message(g, False))
        for side in range(2):
            for i in range(depth):
                y = i - depth if side == 0 else ny + i
                write_rows(g, pl.ds(row_of(0, y), nx, stride=PITCH), edge_in[g, side, i])
        for c, (dx, dy) in enumerate(ways[4:]):
            for i in range(2):
                x = i - 2 if dx < 0 else nx + i
                y = -2 if dy < 0 else ny
                write_rows(g, pl.ds(row_of(x, y), 2), corner_in[g, c, 2 * i : 2 * i + 2, :])

    def viscosity():
        whole(mean_land, mean_sems.at[0], mean_sems.at[1]).wait_recv()
        expand = (
            lax.broadcasted_iota(jnp.int32, (LZ, 32), 0)
            == lax.broadcasted_iota(jnp.int32, (LZ, 32), 1) // 4
        ).astype(jnp.float32)
        same = (
            lax.broadcasted_iota(jnp.int32, (128, 32), 0) % 4
            == lax.broadcasted_iota(jnp.int32, (128, 32), 1) % 4
        )
        gather = (
            lax.broadcasted_iota(jnp.int32, (32, 128), 0)
            == lax.broadcasted_iota(jnp.int32, (32, 128), 1) // 4
        ).astype(jnp.float32)
        for y in range(LY):
            for z in range(LZ):
                mean_held[pl.ds(z, 4, stride=LZ), :] = mean_land[source_of(y, z)]
            for p in range(4):
                tall = jnp.dot(
                    mean_held[p * LZ : p * LZ + LZ].T, expand,
                    precision=lax.Precision.HIGHEST, preferred_element_type=jnp.float32,
                )
                cells = jnp.dot(
                    gather, jnp.where(same, tall, 0.0),
                    precision=lax.Precision.HIGHEST, preferred_element_type=jnp.float32,
                )
                for half in range(2):
                    for layer in range(4):
                        at = half * 16 + layer * 4
                        mean_ref[half * 4 + p, layer, y * 4 : y * 4 + 4, :] = cells[at : at + 4]
        for layer in range(4):
            mixture = MIX_WEIGHTS[0] * mean_ref[0, layer]
            for p in range(1, len(MIX_WEIGHTS)):
                mixture = mixture + MIX_WEIGHTS[p] * mean_ref[p, layer]
            wide_mix = jnp.dot(
                mixture, gather,
                precision=lax.Precision.HIGHEST, preferred_element_type=jnp.float32,
            )
            spread = jnp.concatenate(
                [jnp.broadcast_to(wide_mix[j : j + 1], (4, 128)) for j in range(LY * 4)], axis=0
            )
            for x in range(layer * 4, layer * 4 + 4):
                eta[pl.ds(row_of(x, 0), ny), :] = drag_grid[x] * jnp.exp(
                    HEAT_FACTOR * (0.5 - heat_ref[x]) + spread
                )

    wide_rows = (PITCH, (nx + 2 * DEEP - 1) * PITCH)

    def factor_rows(base):
        factors(base, STEP, eta, warm, side_ref, rest_ref)

    def drift_rows(base):
        found = drift(base, STEP, pad_ref, side_ref, rest_ref)
        for k in range(4):
            part_ref[k, pl.ds(base, STEP), :] = found[k]

    for f in range(FIELDS):
        whole(lands[f], data_send.at[f], data_recv.at[f]).wait_recv()
        if f + AHEAD < FIELDS:
            send_field(f + AHEAD)
        for y in range(LY):
            at = slice(y * BS, (y + 1) * BS)
            part = grid_part(f, y)
            if f == 0:
                heat_ref[:, at, :] = part
            if f == 1:
                drag_grid[:, at, :] = part
            else:
                for x in range(nx):
                    write_rows(f, pl.ds(row_of(x, y * BS), BS), part[x])
        if f == 1:
            viscosity()
            send_halo(0)
        if f > 0:
            send_halo(f)
        if f == 3:
            take_halo(0)
            take_halo(1)
            over_rows(*wide_rows, 10, factor_rows)
    for f in range(2, FIELDS - 1):
        take_halo(f)
    over_rows(*wide_rows, DRIFT_TURNS, drift_rows)
    whole(table, table_send, table_recv.at[0]).wait_send()
    whole(mean_land, mean_sems.at[0], mean_sems.at[1]).wait_send()
    for f in range(FIELDS):
        whole(lands[f], data_send.at[f], data_recv.at[f]).wait_send()
        each_message(f, wait_message(f, True))
    take_halo(FIELDS - 1)

def migrate(slots, flow, stress, heat, drag, attributes, holder, voxel):
    wide_count, narrow_count = lax.axis_size("wide"), lax.axis_size("narrow")
    count = wide_count * narrow_count
    blocks = slots.shape[0]
    tracers = attributes.shape[1]
    nx, ny, nz = LX * BS, LY * BS, LZ * BS
    rows = BS * BS * BS // 128
    pad_rows = (nx + 2 * DEEP) * PITCH + 8
    vmem = pl.BlockSpec(memory_space=pltpu.VMEM)
    hbm = pl.BlockSpec(memory_space=pltpu.HBM)
    f32 = jnp.float32
    per_field = [pltpu.VMEM((count, rows, 128), f32)] * FIELDS
    dma = pltpu.SemaphoreType.DMA
    pinned = [
        pltpu.with_memory_space_constraint(array, pltpu.HBM)
        for array in (slots, flow, stress, heat, drag, attributes, holder, voxel)
    ]
    return pl.pallas_call(
        functools.partial(migrate_kernel, wide_count=wide_count, narrow_count=narrow_count),
        out_shape=(
            jax.ShapeDtypeStruct((4, pad_rows, nz), f32),
            jax.ShapeDtypeStruct((4, pad_rows, nz), f32),
            jax.ShapeDtypeStruct((6, pad_rows, nz), f32),
            jax.ShapeDtypeStruct((3, pad_rows, nz), f32),
            jax.ShapeDtypeStruct((nx, ny, nz), f32),
            jax.ShapeDtypeStruct((8, LX * 4, LY * 4, LZ * 4), f32),
        ),
        in_specs=[hbm] * 8,
        out_specs=(vmem,) * 6,
        scratch_shapes=[
            pltpu.SMEM((blocks,), jnp.int32),
            pltpu.VMEM((1, 128), jnp.int32),
            pltpu.VMEM((count, 1, 128), jnp.int32),
            pltpu.SMEM((count, 1, 128), jnp.int32),
            pltpu.VMEM((FIELDS, blocks, rows * 128), f32),
            pltpu.VMEM((blocks * rows + rows, 128), f32),
            pltpu.VMEM((FIELDS, blocks, rows, 128), f32),
            *per_field,
            *per_field,
            pltpu.VMEM((8, tracers), f32),
            pltpu.VMEM((1, tracers), jnp.int32),
            pltpu.VMEM((1, tracers), jnp.int32),
            pltpu.VMEM((blocks, 4, 128), f32),
            pltpu.VMEM((count, 4, 128), f32),
            pltpu.VMEM((count, 4, 128), f32),
            pltpu.VMEM((4 * LZ + LZ, 128), f32),
            pltpu.VMEM((rows * LZ + LZ, 128), f32),
            pltpu.VMEM((nx, ny, nz), f32),
            pltpu.VMEM((pad_rows, nz), f32),
            pltpu.VMEM((pad_rows, nz), f32),
            pltpu.VMEM((FIELDS, 2, DEEP, nx, nz), f32),
            pltpu.VMEM((FIELDS, 2, DEEP, nx, nz), f32),
            pltpu.VMEM((FIELDS, 4, 4, nz), f32),
            pltpu.VMEM((FIELDS, 4, 4, nz), f32),
            dma((FIELDS + 3,)),
            dma(()),
            dma((narrow_count,)),
            dma((FIELDS,)),
            dma((FIELDS,)),
            dma((2,)),
            dma((FIELDS, 2 * DEEP + 6)),
            dma((FIELDS, 2 * DEEP + 6)),
            dma(()),
        ],
        compiler_params=pltpu.CompilerParams(
            collective_id=1,
            has_side_effects=True,
            vmem_limit_bytes=(24 if count <= 32 else 44) * 1024 * 1024,
        ),
    )(*pinned)


def relax_kernel(
    pad_ref, part_ref, side_ref, rest_ref, heat_ref, mean_ref,
    velocity_ref, pressure_ref, heat_out_ref, mean_out_ref, pad_1, pad_2, fresh, sems,
):
    nx, ny, nz = heat_ref.shape
    copies = []

    def send(source, target):
        copies.append(pltpu.make_async_copy(source, target, sems.at[len(copies)]))
        copies[-1].start()

    send(heat_ref, heat_out_ref)
    send(mean_ref, mean_out_ref)

    def finish_first(base):
        drifted = [part_ref[k, pl.ds(base, STEP), :] for k in range(4)]
        moved = push(base, STEP, pad_ref, rest_ref, drifted)
        for k in range(4):
            pad_1[k, pl.ds(base, STEP), :] = moved[k]

    def second(base):
        moved = relax(base, STEP, pad_1, side_ref, rest_ref)
        for k in range(4):
            pad_2[k, pl.ds(base, STEP), :] = moved[k]

    slabs = nx + 2 * DEEP
    over_rows(PITCH, (slabs - 1) * PITCH, TURNS, finish_first)
    over_rows(2 * PITCH, (slabs - 2) * PITCH, TURNS, second)

    parts = 8
    thick = nx // parts
    for part in range(parts):
        for x in range(part * thick, (part + 1) * thick):
            for half in range(0, ny, STEP):
                base = (x + DEEP) * PITCH + FIRST + half
                moved = relax(base, STEP, pad_2, side_ref, rest_ref)
                for k in range(4):
                    fresh[k, x, half : half + STEP, :] = moved[k]
        at = pl.ds(part * thick, thick)
        send(fresh.at[pl.ds(0, 3), at], velocity_ref.at[:, at])
        send(fresh.at[3, at], pressure_ref.at[at])
    for copy in copies:
        copy.wait()


def relax_all(pad, part, side, rest, heat, means):
    nx, ny, nz = heat.shape
    vmem = pl.BlockSpec(memory_space=pltpu.VMEM)
    hbm = pl.BlockSpec(memory_space=pltpu.HBM)
    return pl.pallas_call(
        relax_kernel,
        out_shape=(
            jax.ShapeDtypeStruct((3, nx, ny, nz), jnp.float32),
            jax.ShapeDtypeStruct((nx, ny, nz), jnp.float32),
            jax.ShapeDtypeStruct(heat.shape, jnp.float32),
            jax.ShapeDtypeStruct(means.shape, jnp.float32),
        ),
        in_specs=[vmem] * 6,
        out_specs=(hbm,) * 4,
        scratch_shapes=[
            pltpu.VMEM(pad.shape, jnp.float32),
            pltpu.VMEM(pad.shape, jnp.float32),
            pltpu.VMEM((4, nx, ny, nz), jnp.float32),
            pltpu.SemaphoreType.DMA((18,)),
        ],
        compiler_params=pltpu.CompilerParams(vmem_limit_bytes=16 * 1024 * 1024),
    )(pad, part, side, rest, heat, means)


def per_device(
    tile_flow_speed,
    tile_stress_mean,
    tile_heat_state,
    tile_drag_coefficient,
    marker_attributes,
    marker_holding_tile,
    marker_voxel_number,
    prior_slot_of_tile,
):
    tracers = marker_attributes.shape[1]
    results = migrate(
        prior_slot_of_tile,
        tile_flow_speed.transpose(1, 0, 2),
        tile_stress_mean,
        tile_heat_state,
        tile_drag_coefficient,
        marker_attributes,
        marker_holding_tile.reshape(1, tracers),
        marker_voxel_number.reshape(1, tracers),
    )
    return relax_all(*results)


def solution(mesh):
    in_specs = (
        P(("wide", "narrow"), None, None),
        P(("wide", "narrow"), None),
        P(("wide", "narrow"), None),
        P(("wide", "narrow"), None),
        P(None, ("wide", "narrow")),
        P(("wide", "narrow")),
        P(("wide", "narrow")),
        P(("wide", "narrow")),
    )
    out_specs = (
        P(None, "wide", "narrow", None),
        P("wide", "narrow", None),
        P("wide", "narrow", None),
        P(None, "wide", "narrow", None),
    )
    return jax.shard_map(
        per_device, mesh=mesh, in_specs=in_specs, out_specs=out_specs, check_vma=False
    )
```
